32 devices in a mesh: row: 4 (over x, core), seq: 8 (over z, y).
Axes of the slice: x: 2, y: 2, z: 4, core: 2. Of those that a mesh axis runs over, the one named last changes fastest.
Arguments:
- tokens: bfloat16 [8, 512, 1024], P('row', 'seq'), may hold values from -6 to 6
- memory: bfloat16 [8, 1024, 1024], P('row', 'seq'), may hold values from -6 to 6
- source_len: int32 [8], P('row'), may hold values from 1 to 1024, as said below
- bucket_order: int32 [16], replicated, may hold values from 0 to 15, each once
- prefix_self: float32 [2, 30, 1024], replicated, may hold values from -6 to 6
- prefix_cross: float32 [2, 30, 1024], replicated, may hold values from -6 to 6
- self_query: float32 [1024, 1024], P('row'), may hold values from -0.375 to 0.375
- self_kv: float32 [2, 1024, 1024], P(None, 'row'), may hold values from -0.1875 to 0.1875
- self_out: float32 [1024, 1024], P('row'), may hold values from -0.75 to 0.75
- cross_query: float32 [1024, 1024], P('row'), may hold values from -0.375 to 0.375
- cross_kv: float32 [2, 1024, 1024], P(None, 'row'), may hold values from -0.1875 to 0.1875
- cross_out: float32 [1024, 1024], P('row'), may hold values from -0.75 to 0.75
- fc_in: float32 [1024, 4096], P('row'), may hold values from -0.1875 to 0.1875
- fc_out: float32 [4096, 1024], P('row'), may hold values from -0.09375 to 0.09375
- ln_gain: float32 [3, 1024], replicated, may hold values from 0.5 to 1.5
- ln_bias: float32 [3, 1024], replicated, may hold values from -1.25 to 1.25
- ad_down: float32 [1024, 512], replicated, may hold values from -0.1875 to 0.1875
- ad_down_bias: float32 [512], replicated, may hold values from -3 to 3
- ad_up: float32 [512, 1024], replicated, may hold values from -0.125 to 0.125
- ad_up_bias: float32 [1024], replicated, may hold values from -1.5 to 1.5
- cotangent: bfloat16 [8, 512, 1024], P('row', 'seq'), may hold values from -6 to 6
Outputs:
- mixed: bfloat16 [8, 512, 1024], P('row', 'seq')
- d_tokens: bfloat16 [8, 512, 1024], P('row', 'seq')
- d_memory: bfloat16 [8, 1024, 1024], P('row', 'seq')
- grad_prefix_self: float32 [2, 30, 1024], replicated
- grad_prefix_cross: float32 [2, 30, 1024], replicated
- grad_ad_down: float32 [1024, 512], replicated
- grad_ad_down_bias: float32 [512], replicated
- grad_ad_up: float32 [512, 1024], replicated
- grad_ad_up_bias: float32 [1024], replicated
The draws below stay inside these ranges and needn't reach their ends.
Inputs may be any that keep to these rules, and one draw needn't show every extreme that they name: `source_len`: in every group of 2 sequences on one index of row one sequence has all 1024 slots live, the others fewer than 409. A permutation; index s of seq stores buckets bucket_order[2 s] and bucket_order[2 s + 1] of every sequence, each of 32 tokens.
All inputs are finite; a program needn't handle non-finite values.
Results may differ from the reference program's by a relative error of at most 0.025.
The reference program's roundings to bfloat16 on the way count: a program that leaves them out, or rounds other values in their place, can miss the bound.
Values may be sent and summed in bfloat16 or wider, within the bound.
No kernel may reach another device: no remote copies, remote signals or barrier semaphores. Data moves between devices by JAX's collectives and lax.ppermute only.
A program may use at most 384 MiB of HBM per device.

```python
import math
import jax
import jax.numpy as jnp
from jax import lax

D = 1024
H = 16
FF = 4096
HD = 64
A = 512
P_SIZE = 30
SRC = 1024
ROWS_DEV = 2
TOK_DEV = 64
SEQLEN = 512
ROWS = 8
NB = 16


def draw_source_len(key, part):
    key = jax.random.fold_in(key, 7)
    short_key, pick_key = jax.random.split(key)
    short_len = jax.random.randint(short_key, (ROWS,), 1, 2 * SRC // 5)
    group_pick = jax.random.randint(pick_key, (ROWS // ROWS_DEV,), 0, ROWS_DEV)
    row_number = jnp.arange(ROWS, dtype=jnp.int32)
    full_row = row_number % ROWS_DEV == jnp.repeat(group_pick, ROWS_DEV)
    return jnp.where(full_row, SRC, short_len).astype(jnp.int32)


def steps_of(key, shape, cuts, low, top_value):
    level, own = 1.0, jax.random.fold_in(key, 6)
    for axis_at, shards_of in cuts:
        steps = jnp.exp(jax.random.uniform(jax.random.fold_in(own, axis_at), (shards_of,), jnp.float32, low / len(cuts), top_value / len(cuts)))
        level = level * jnp.repeat(steps, shape[axis_at] // shards_of).reshape([-1 if axis == axis_at else 1 for axis in range(len(shape))])
    return level


def bell_draw(own_key, extent, width, most, shards=(), held_as=jnp.bfloat16):
    level = steps_of(own_key, extent, shards, -0.22, 0.18) if shards else 1.0
    values = jax.random.normal(own_key, extent, jnp.float32) * width * level
    return jnp.minimum(jnp.maximum(values, -most), most).astype(held_as)


def setup_inputs(seed: int = 0) -> dict:
    seeds = jax.random.split(jax.random.key(seed), 22)
    tokens = bell_draw(seeds[0], (ROWS, SEQLEN, D), 1.0, 6.0, ((0, 4), (1, 8)))
    memory = bell_draw(seeds[1], (ROWS, SRC, D), 1.0, 6.0, ((0, 4), (1, 8)))
    source_len = draw_source_len(jax.random.fold_in(seeds[21], 71), 0)
    bucket_order = jax.random.permutation(seeds[3], NB).astype(jnp.int32)
    prefix_self = bell_draw(seeds[4], (2, P_SIZE, D), 1.0, 6.0, (), jnp.float32)
    prefix_cross = bell_draw(seeds[5], (2, P_SIZE, D), 1.0, 6.0, (), jnp.float32)
    self_query = bell_draw(seeds[6], (D, D), (D // 4) ** -0.5, 0.375, ((0, 4),), jnp.float32)
    self_kv = bell_draw(seeds[7], (2, D, D), D ** -0.5, 0.1875, ((1, 4),), jnp.float32)
    self_out = bell_draw(seeds[8], (D, D), HD ** -0.5, 0.75, ((0, 4),), jnp.float32)
    cross_query = bell_draw(seeds[9], (D, D), (D // 4) ** -0.5, 0.375, ((0, 4),), jnp.float32)
    cross_kv = bell_draw(seeds[10], (2, D, D), D ** -0.5, 0.1875, ((1, 4),), jnp.float32)
    cross_out = bell_draw(seeds[11], (D, D), HD ** -0.5, 0.75, ((0, 4),), jnp.float32)
    fc_in = bell_draw(seeds[12], (D, FF), D ** -0.5, 0.1875, ((0, 4),), jnp.float32)
    fc_out = bell_draw(seeds[13], (FF, D), FF ** -0.5, 0.09375, ((0, 4),), jnp.float32)
    ln_gain = jnp.clip(1.0 + 0.1 * jax.random.normal(seeds[14], (3, D), jnp.float32), 0.5, 1.5)
    ln_bias = bell_draw(seeds[15], (3, D), 0.2, 1.25, (), jnp.float32)
    ad_down = bell_draw(seeds[16], (D, A), D ** -0.5, 0.1875, (), jnp.float32)
    ad_down_bias = bell_draw(seeds[17], (A,), 0.5, 3.0, (), jnp.float32)
    ad_up = bell_draw(seeds[18], (A, D), (4 * A) ** -0.5, 0.125, (), jnp.float32)
    ad_up_bias = bell_draw(seeds[19], (D,), 0.25, 1.5, (), jnp.float32)
    cotangent = bell_draw(seeds[20], (ROWS, SEQLEN, D), 1.0, 6.0, ((0, 4), (1, 8)))
    return {"tokens": tokens, "memory": memory, "source_len": source_len, "bucket_order": bucket_order, "prefix_self": prefix_self, "prefix_cross": prefix_cross, "self_query": self_query, "self_kv": self_kv, "self_out": self_out, "cross_query": cross_query, "cross_kv": cross_kv, "cross_out": cross_out, "fc_in": fc_in, "fc_out": fc_out, "ln_gain": ln_gain, "ln_bias": ln_bias, "ad_down": ad_down, "ad_down_bias": ad_down_bias, "ad_up": ad_up, "ad_up_bias": ad_up_bias, "cotangent": cotangent}


@jax.custom_vjp
def low(v):
    return lax.optimization_barrier(v.astype(jnp.bfloat16)).astype(jnp.float32)

@jax.custom_vjp
def low_back(v):
    return v

def low_keep(v):
    return (low(v), None)

def low_pass(kept, grad):
    return (grad,)

def back_keep(v):
    return (v, None)

def back_low(kept, grad):
    return (low(grad),)
low.defvjp(low_keep, low_pass)
low_back.defvjp(back_keep, back_low)
EPSILON = 1e-05
MASKED = -1e+30

def matmul(left, right):
    return jnp.dot(left, right, precision=lax.Precision.HIGHEST)

def rounded_both(value):
    return low_back(low(value))

def gelu_exact(value):
    return jax.nn.gelu(value, approximate=False)

def layer_norm(value, gain, shift):
    centre = value - lax.optimization_barrier(jnp.mean(value, axis=-1, keepdims=True))
    return centre * lax.rsqrt(lax.optimization_barrier(jnp.mean(centre * centre, axis=-1, keepdims=True)) + EPSILON) * gain + shift

def block_attend(key_heads, value_heads, query_block, mask_block):
    query_heads = query_block.reshape(query_block.shape[0], H, HD)
    scores = low_back(jnp.einsum('qhd,khd->hqk', query_heads, key_heads, precision=lax.Precision.HIGHEST))
    scores = jnp.where(mask_block[None], scores, MASKED)
    probs = low(jax.nn.softmax(scores, axis=-1))
    result = jnp.einsum('hqk,khd->qhd', probs, value_heads, precision=lax.Precision.HIGHEST)
    return result.reshape(query_block.shape[0], H * HD)

def attention(queries, keys, values, mask):
    length = queries.shape[0]
    block = math.gcd(length, 512)
    key_heads = keys.reshape(keys.shape[0], H, HD)
    value_heads = values.reshape(values.shape[0], H, HD)
    checked = jax.checkpoint(block_attend)
    blocks = lax.map(lambda pair: checked(key_heads, value_heads, pair[0], pair[1]), (queries.reshape(length // block, block, -1), mask.reshape(length // block, block, -1)))
    return blocks.reshape(length, -1)

def decoder_row(tokens, memory, length, positions, weights, ln_gain, ln_bias, prefix_self, prefix_cross, ad_down, ad_down_bias, ad_up, ad_up_bias):
    q_weight, kv_weight, o_weight, cq_weight, ckv_weight, co_weight, in_weight, out_weight = weights
    scale = HD ** (-0.5)
    seq_len = tokens.shape[0]
    prefix_count = prefix_self.shape[1]
    queries = rounded_both(scale * matmul(tokens, q_weight))
    keys = rounded_both(matmul(tokens, kv_weight[0]))
    values = rounded_both(matmul(tokens, kv_weight[1]))
    pre_self = low(prefix_self)
    self_mask = jnp.concatenate([jnp.ones((seq_len, prefix_count), jnp.bool_), positions[None, :] <= positions[:, None]], axis=1)
    attended = rounded_both(attention(queries, jnp.concatenate([pre_self[0], keys], 0), jnp.concatenate([pre_self[1], values], 0), self_mask))
    hidden_one = layer_norm(tokens + low_back(matmul(attended, o_weight)), ln_gain[0], ln_bias[0])
    cross_queries = rounded_both(scale * matmul(low(hidden_one), cq_weight))
    mem_keys = rounded_both(matmul(memory, ckv_weight[0]))
    mem_values = rounded_both(matmul(memory, ckv_weight[1]))
    pre_cross = low(prefix_cross)
    live = jnp.arange(memory.shape[0], dtype=jnp.int32) < length
    cross_mask = jnp.broadcast_to(jnp.concatenate([jnp.ones((prefix_count,), jnp.bool_), live])[None, :], (seq_len, prefix_count + memory.shape[0]))
    cross_att = rounded_both(attention(cross_queries, jnp.concatenate([pre_cross[0], mem_keys], 0), jnp.concatenate([pre_cross[1], mem_values], 0), cross_mask))
    hidden_two = layer_norm(hidden_one + low_back(matmul(cross_att, co_weight)), ln_gain[1], ln_bias[1])
    hidden_low = low(hidden_two)
    inner = low(gelu_exact(low_back(matmul(hidden_low, in_weight))))
    ffn_out = low_back(matmul(inner, out_weight))
    down_proj = low_back(matmul(hidden_low, low(ad_down)) + ad_down_bias)
    adapted = low_back(matmul(low(gelu_exact(down_proj)), low(ad_up)) + ad_up_bias)
    return layer_norm(hidden_two + ffn_out + 4.0 * adapted, ln_gain[2], ln_bias[2])

def reference(tokens, memory, source_len, bucket_order, prefix_self, prefix_cross, self_query, self_kv, self_out, cross_query, cross_kv, cross_out, fc_in, fc_out, ln_gain, ln_bias, ad_down, ad_down_bias, ad_up, ad_up_bias, cotangent):
    weights = (low(self_query), low(self_kv), low(self_out), low(cross_query), low(cross_kv), low(cross_out), low(fc_in), low(fc_out))
    half_len = TOK_DEV // 2
    positions = (bucket_order[:, None] * half_len + jnp.arange(half_len, dtype=jnp.int32)[None, :]).reshape(-1)
    trained = (prefix_self, prefix_cross, ad_down, ad_down_bias, ad_up, ad_up_bias)

    def one_row(totals, row_data):
        tok_row, mem_row, length, cot_row = row_data

        def forward(tok_value, mem_value, trained_args):
            return decoder_row(tok_value, mem_value, length, positions, weights, ln_gain, ln_bias, *trained_args)
        result, backward = jax.vjp(forward, tok_row.astype(jnp.float32), mem_row.astype(jnp.float32), trained)
        grad_tok, grad_mem, grad_trained = backward(cot_row.astype(jnp.float32))
        totals = jax.tree.map(lambda first, second: first + second, totals, grad_trained)
        return (totals, (result.astype(jnp.bfloat16), grad_tok.astype(jnp.bfloat16), grad_mem.astype(jnp.bfloat16)))
    zero_totals = jax.tree.map(jnp.zeros_like, trained)
    totals, outputs = lax.scan(one_row, zero_totals, (tokens, memory, source_len, cotangent))
    return (outputs[0], outputs[1], outputs[2], totals[0], totals[1], totals[2], totals[3], totals[4], totals[5])
```

```python
import jax
import jax.numpy as jnp
from jax import lax
from jax.sharding import PartitionSpec as P

H = 16
HD = 64


EPSILON = 1e-05
MASKED = -1e30


def normalize(value, gain, shift):
    centre = value - jnp.mean(value, axis=-1, keepdims=True)
    inv_dev = lax.rsqrt(jnp.mean(centre * centre, axis=-1, keepdims=True) + EPSILON)
    unit_val = centre * inv_dev
    return (unit_val * gain + shift, unit_val, inv_dev)


def normalize_back(grad, unit_val, inv_dev, gain):
    scaled = grad * gain
    return inv_dev * (
        scaled
        - jnp.mean(scaled, axis=-1, keepdims=True)
        - unit_val * jnp.mean(scaled * unit_val, axis=-1, keepdims=True)
    )


def gelu_exact(value):
    return jax.nn.gelu(value, approximate=False)


def gelu_back(value, grad):
    return jax.vjp(gelu_exact, value)[1](grad)[0]


def head_split(matrix):
    return matrix.reshape(matrix.shape[0], -1, HD)


def masked_scores(queries, keys, mask):
    scores = jnp.einsum(
        "qhd,khd->hqk", head_split(queries), head_split(keys), preferred_element_type=jnp.float32
    )
    return jnp.where(mask[None], scores, MASKED)


def attend(queries, keys, values, mask):
    scores = masked_scores(queries, keys, mask)
    top_score = jnp.max(scores, axis=-1, keepdims=True)
    log_total = top_score + jnp.log(jnp.sum(jnp.exp(scores - top_score), axis=-1, keepdims=True))
    probs = jnp.exp(scores - log_total).astype(jnp.bfloat16)
    result = jnp.einsum(
        "hqk,khd->qhd", probs, head_split(values), preferred_element_type=jnp.float32
    )
    return (result.reshape(queries.shape[0], -1), log_total)


def attend_back(queries, keys, values, mask, log_total, grad_out):
    probs = jnp.exp(masked_scores(queries, keys, mask) - log_total)
    grad_heads = head_split(grad_out)
    grad_probs = jnp.einsum(
        "qhd,khd->hqk", grad_heads, head_split(values), preferred_element_type=jnp.float32
    )
    row_delta = jnp.sum(probs * grad_probs, axis=-1, keepdims=True)
    grad_scores = (probs * (grad_probs - row_delta)).astype(jnp.bfloat16)
    grad_query = jnp.einsum(
        "hqk,khd->qhd", grad_scores, head_split(keys), preferred_element_type=jnp.float32
    )
    grad_keys = jnp.einsum(
        "hqk,qhd->khd", grad_scores, head_split(queries), preferred_element_type=jnp.float32
    )
    grad_values = jnp.einsum(
        "hqk,qhd->khd", probs.astype(jnp.bfloat16), grad_heads, preferred_element_type=jnp.float32
    )
    return (
        grad_query.reshape(queries.shape[0], -1),
        grad_keys.reshape(keys.shape[0], -1),
        grad_values.reshape(values.shape[0], -1),
    )


def project(left, right):
    return jnp.dot(left, right, preferred_element_type=jnp.float32)


def local_rows(
    tokens,
    memory,
    source_len,
    bucket_order,
    prefix_self,
    prefix_cross,
    self_query,
    self_kv,
    self_out,
    cross_query,
    cross_kv,
    cross_out,
    fc_in,
    fc_out,
    ln_gain,
    ln_bias,
    ad_down,
    ad_down_bias,
    ad_up,
    ad_up_bias,
    cotangent,
):
    low_type = jnp.bfloat16
    row_count, tok_count, width = tokens.shape
    slot_count = memory.shape[1]
    prefix_count = prefix_self.shape[1]
    half_len = tok_count // 2
    scale = HD ** (-0.5)
    weight_set = (
        lax.all_gather(self_query.astype(low_type), "row", axis=0, tiled=True),
        lax.all_gather(self_kv.astype(low_type), "row", axis=1, tiled=True),
        lax.all_gather(self_out.astype(low_type), "row", axis=0, tiled=True),
        lax.all_gather(cross_query.astype(low_type), "row", axis=0, tiled=True),
        lax.all_gather(cross_kv.astype(low_type), "row", axis=1, tiled=True),
        lax.all_gather(cross_out.astype(low_type), "row", axis=0, tiled=True),
        lax.all_gather(fc_in.astype(low_type), "row", axis=0, tiled=True),
        lax.all_gather(fc_out.astype(low_type), "row", axis=0, tiled=True),
    )
    q_weight, kv_weight, o_weight, cq_weight, ckv_weight, co_weight, in_weight, out_weight = (
        weight_set
    )
    place = lax.axis_index("seq")
    offsets = jnp.arange(half_len, dtype=jnp.int32)
    all_pos = (bucket_order[:, None] * half_len + offsets[None, :]).reshape(-1)
    own_pos = lax.dynamic_slice_in_dim(all_pos, place * tok_count, tok_count)
    self_mask = jnp.concatenate(
        [jnp.ones((tok_count, prefix_count), jnp.bool_), all_pos[None, :] <= own_pos[:, None]],
        axis=1,
    )
    flat_tokens = tokens.reshape(-1, width)
    queries = (project(flat_tokens, q_weight) * scale).astype(low_type)
    own_keys = (
        project(flat_tokens, kv_weight[0]).astype(low_type).reshape(row_count, tok_count, width)
    )
    own_values = (
        project(flat_tokens, kv_weight[1]).astype(low_type).reshape(row_count, tok_count, width)
    )
    flat_memory = memory.reshape(-1, width)
    mem_keys = (
        project(flat_memory, ckv_weight[0]).astype(low_type).reshape(row_count, slot_count, width)
    )
    mem_values = (
        project(flat_memory, ckv_weight[1]).astype(low_type).reshape(row_count, slot_count, width)
    )
    all_keys, all_values, all_mkeys, all_mvalues = (
        lax.all_gather(own_keys, "seq", axis=1, tiled=True),
        lax.all_gather(own_values, "seq", axis=1, tiled=True),
        lax.all_gather(mem_keys, "seq", axis=1, tiled=True),
        lax.all_gather(mem_values, "seq", axis=1, tiled=True),
    )
    src_total = all_mkeys.shape[1]
    pre_self = prefix_self.astype(low_type)
    pre_cross = prefix_cross.astype(low_type)
    self_key_sets = [
        jnp.concatenate([pre_self[0], all_keys[row_index]], 0) for row_index in range(row_count)
    ]
    self_value_sets = [
        jnp.concatenate([pre_self[1], all_values[row_index]], 0) for row_index in range(row_count)
    ]
    cross_key_sets = [
        jnp.concatenate([pre_cross[0], all_mkeys[row_index]], 0) for row_index in range(row_count)
    ]
    cross_value_sets = [
        jnp.concatenate([pre_cross[1], all_mvalues[row_index]], 0) for row_index in range(row_count)
    ]
    slot_number = jnp.arange(src_total, dtype=jnp.int32)
    cross_masks = [
        jnp.concatenate(
            [jnp.ones((prefix_count,), jnp.bool_), slot_number < source_len[row_index]]
        )[None, :]
        for row_index in range(row_count)
    ]

    def rows_of(matrix, row_index):
        return matrix[row_index * tok_count : (row_index + 1) * tok_count]

    self_parts = [
        attend(
            rows_of(queries, row_index),
            self_key_sets[row_index],
            self_value_sets[row_index],
            self_mask,
        )
        for row_index in range(row_count)
    ]
    attended = jnp.concatenate([part[0] for part in self_parts], 0).astype(low_type)
    resid_one = flat_tokens.astype(jnp.float32) + project(attended, o_weight)
    hidden_one, unit_one, inv_one = normalize(resid_one, ln_gain[0], ln_bias[0])
    cross_queries = (project(hidden_one.astype(low_type), cq_weight) * scale).astype(low_type)
    cross_parts = [
        attend(
            rows_of(cross_queries, row_index),
            cross_key_sets[row_index],
            cross_value_sets[row_index],
            cross_masks[row_index],
        )
        for row_index in range(row_count)
    ]
    cross_att = jnp.concatenate([part[0] for part in cross_parts], 0).astype(low_type)
    resid_two = hidden_one + project(cross_att, co_weight)
    hidden_two, unit_two, inv_two = normalize(resid_two, ln_gain[1], ln_bias[1])
    hidden_low = hidden_two.astype(low_type)
    up_proj = project(hidden_low, in_weight)
    activated = gelu_exact(up_proj).astype(low_type)
    ffn_out = project(activated, out_weight)
    down_weight = ad_down.astype(low_type)
    up_weight = ad_up.astype(low_type)
    down_proj = project(hidden_low, down_weight) + ad_down_bias
    down_act = gelu_exact(down_proj).astype(low_type)
    adapted = project(down_act, up_weight) + ad_up_bias
    resid_three = hidden_two + ffn_out + 4.0 * adapted
    output, unit_three, inv_three = normalize(resid_three, ln_gain[2], ln_bias[2])
    mixed = output.astype(low_type).reshape(row_count, tok_count, width)
    weight_set = (
        lax.all_gather(self_query.astype(low_type), "row", axis=0, tiled=True),
        lax.all_gather(self_kv.astype(low_type), "row", axis=1, tiled=True),
        lax.all_gather(self_out.astype(low_type), "row", axis=0, tiled=True),
        lax.all_gather(cross_query.astype(low_type), "row", axis=0, tiled=True),
        lax.all_gather(cross_kv.astype(low_type), "row", axis=1, tiled=True),
        lax.all_gather(cross_out.astype(low_type), "row", axis=0, tiled=True),
        lax.all_gather(fc_in.astype(low_type), "row", axis=0, tiled=True),
        lax.all_gather(fc_out.astype(low_type), "row", axis=0, tiled=True),
    )
    q_weight, kv_weight, o_weight, cq_weight, ckv_weight, co_weight, in_weight, out_weight = (
        weight_set
    )
    grad_out = cotangent.astype(jnp.float32).reshape(-1, width)
    grad_three = normalize_back(grad_out, unit_three, inv_three, ln_gain[2])
    grad_ffn = grad_three.astype(low_type)
    grad_adapt = (4.0 * grad_three).astype(low_type)
    grad_up_w = jnp.einsum("na,nd->ad", down_act, grad_adapt, preferred_element_type=jnp.float32)
    grad_up_b = jnp.sum(grad_adapt.astype(jnp.float32), axis=0)
    grad_down = gelu_back(down_proj, project(grad_adapt, up_weight.T)).astype(low_type)
    grad_down_w = jnp.einsum("nd,na->da", hidden_low, grad_down, preferred_element_type=jnp.float32)
    grad_down_b = jnp.sum(grad_down.astype(jnp.float32), axis=0)
    grad_inner = gelu_back(up_proj, project(grad_ffn, out_weight.T)).astype(low_type)
    grad_hidden_two = (
        grad_three + project(grad_inner, in_weight.T) + project(grad_down, down_weight.T)
    )
    grad_two = normalize_back(grad_hidden_two, unit_two, inv_two, ln_gain[1])
    grad_cross_att = project(grad_two.astype(low_type), co_weight.T).astype(low_type)
    cross_grads = [
        attend_back(
            rows_of(cross_queries, row_index),
            cross_key_sets[row_index],
            cross_value_sets[row_index],
            cross_masks[row_index],
            cross_parts[row_index][1],
            rows_of(grad_cross_att, row_index),
        )
        for row_index in range(row_count)
    ]
    grad_cq = jnp.concatenate([part[0] for part in cross_grads], 0).astype(low_type)
    grad_hidden_one = grad_two + project(grad_cq, cq_weight.T) * scale
    grad_one = normalize_back(grad_hidden_one, unit_one, inv_one, ln_gain[0])
    grad_attended = project(grad_one.astype(low_type), o_weight.T).astype(low_type)
    self_grads = [
        attend_back(
            rows_of(queries, row_index),
            self_key_sets[row_index],
            self_value_sets[row_index],
            self_mask,
            self_parts[row_index][1],
            rows_of(grad_attended, row_index),
        )
        for row_index in range(row_count)
    ]
    pre_self_grad = jnp.stack(
        [
            sum((part[1][:prefix_count] for part in self_grads)),
            sum((part[2][:prefix_count] for part in self_grads)),
        ]
    )
    pre_cross_grad = jnp.stack(
        [
            sum((part[1][:prefix_count] for part in cross_grads)),
            sum((part[2][:prefix_count] for part in cross_grads)),
        ]
    )
    summed = [
        (
            lax.psum_scatter(
                self_grads[row_index][1][prefix_count:].astype(jnp.bfloat16),
                "seq",
                scatter_dimension=0,
                tiled=True,
            ).astype(jnp.float32),
            lax.psum_scatter(
                self_grads[row_index][2][prefix_count:].astype(jnp.bfloat16),
                "seq",
                scatter_dimension=0,
                tiled=True,
            ).astype(jnp.float32),
            lax.psum_scatter(
                cross_grads[row_index][1][prefix_count:].astype(jnp.bfloat16),
                "seq",
                scatter_dimension=0,
                tiled=True,
            ).astype(jnp.float32),
            lax.psum_scatter(
                cross_grads[row_index][2][prefix_count:].astype(jnp.bfloat16),
                "seq",
                scatter_dimension=0,
                tiled=True,
            ).astype(jnp.float32),
        )
        for row_index in range(row_count)
    ]
    key_grad = jnp.stack([part[0] for part in summed])
    value_grad = jnp.stack([part[1] for part in summed])
    mkey_grad = jnp.stack([part[2] for part in summed])
    mvalue_grad = jnp.stack([part[3] for part in summed])
    grad_query = jnp.concatenate([part[0] for part in self_grads], 0).astype(low_type)
    d_tokens = (
        grad_one
        + project(grad_query, q_weight.T) * scale
        + project(key_grad.astype(low_type).reshape(-1, width), kv_weight[0].T)
        + project(value_grad.astype(low_type).reshape(-1, width), kv_weight[1].T)
    )
    d_memory = project(mkey_grad.astype(low_type).reshape(-1, width), ckv_weight[0].T) + project(
        mvalue_grad.astype(low_type).reshape(-1, width), ckv_weight[1].T
    )
    totals = lax.psum(
        (pre_self_grad, pre_cross_grad, grad_down_w, grad_down_b, grad_up_w, grad_up_b),
        ("row", "seq"),
    )
    return (
        mixed,
        d_tokens.astype(low_type).reshape(row_count, tok_count, width),
        d_memory.astype(low_type).reshape(row_count, slot_count, width),
        totals[0],
        totals[1],
        totals[2],
        totals[3],
        totals[4],
        totals[5],
    )


AXES = ("row", "seq")


def pairs_of(target):
    pairs = []
    for source in range(32):
        row, seq = divmod(source, 8)
        x, c, z, y = target(*divmod(row, 2), *divmod(seq, 2))
        pairs.append((source, (2 * x + c) * 8 + 2 * z + y))
    return pairs


SWAP_X = pairs_of(lambda x, c, z, y: (1 - x, c, z, y))
SWAP_C = pairs_of(lambda x, c, z, y: (x, 1 - c, z, y))
SWAP_Y = pairs_of(lambda x, c, z, y: (x, c, z, 1 - y))
TURN = [pairs_of(lambda x, c, z, y, r=r: (x, z // 2, 2 * c + (z + r) % 2, y)) for r in range(2)]


def send(value, pairs):
    return lax.ppermute(value, AXES, pairs)


def turn(first, second, odd):
    out = [send(jnp.where(odd, second, first), TURN[0]), send(jnp.where(odd, first, second), TURN[1])]
    return jnp.where(odd, out[1], out[0]), jnp.where(odd, out[0], out[1])


def local_pairs(
    tokens,
    memory,
    source_len,
    bucket_order,
    prefix_self,
    prefix_cross,
    self_query,
    self_kv,
    self_out,
    cross_query,
    cross_kv,
    cross_out,
    fc_in,
    fc_out,
    ln_gain,
    ln_bias,
    ad_down,
    ad_down_bias,
    ad_up,
    ad_up_bias,
    cotangent,
):
    low = jnp.bfloat16
    f32 = jnp.float32
    row, seq = lax.axis_index("row"), lax.axis_index("seq")
    x, c, z, y = row // 2, row % 2, seq // 2, seq % 2
    odd = z % 2 == 1
    scale = HD ** (-0.5)
    prefix_count = prefix_self.shape[1]

    tok_own = jnp.concatenate(turn(tokens[0], tokens[1], odd), 0)
    mem_own = jnp.concatenate(turn(memory[0], memory[1], odd), 0)
    cot_own = jnp.concatenate(turn(cotangent[0], cotangent[1], odd), 0)
    live = send(jnp.where(odd, source_len[1], source_len[0]).reshape(1, 1), TURN[0])[0, 0]
    tok_y = send(tok_own, SWAP_Y)
    tok_c = send(jnp.concatenate([tok_own, tok_y], 0), SWAP_C)
    tok_all = jnp.concatenate([tok_own, tok_y, tok_c], 0)

    def relative(values):
        values = jnp.where(c == 0, values, values[::-1])
        return jnp.where(y == 0, values, values[:, ::-1])

    def by_owner(values, size):
        values = values.reshape(2, 2, 2, size).transpose(0, 2, 1, 3)
        return relative(values).reshape(-1)

    places = bucket_order[:, None] * 32 + jnp.arange(32, dtype=jnp.int32)[None]
    pos = by_owner(places.reshape(-1), 64)
    slot = by_owner(jnp.arange(1024, dtype=jnp.int32), 128)

    packed = jnp.stack([self_query, self_kv[0], self_kv[1]])
    packed = lax.dynamic_slice_in_dim(packed.reshape(3, 256, 2, 512), y, 1, 2).reshape(3, 256, 2, 256)
    packed = packed.astype(low).transpose(2, 0, 1, 3)
    far = send(packed, SWAP_X)
    keep, give = jnp.where(c == 0, packed[0], packed[1]), jnp.where(c == 0, packed[1], packed[0])
    far_keep, far_give = jnp.where(c == 0, far[0], far[1]), jnp.where(c == 0, far[1], far[0])
    heads_parts = [keep, send(give, SWAP_C), far_keep, send(far_give, SWAP_C)]
    head_w = jnp.zeros((4, 3, 256, 256), low)
    for k, part in enumerate(heads_parts):
        head_w = lax.dynamic_update_index_in_dim(head_w, part, row ^ k, 0)
    head_w = head_w.transpose(1, 0, 2, 3).reshape(3, 1024, 256)

    def whole(weights):
        count, rows, cols = weights.shape
        own = weights.astype(low)
        half = rows // 2
        out = lax.dynamic_slice_in_dim(own, y * half, half, 1)
        x_own = send(out, SWAP_X)
        x_oth = send(x_own, SWAP_Y)
        mine = jnp.where(y == 0, jnp.concatenate([x_own, x_oth], 1), jnp.concatenate([x_oth, x_own], 1))
        full = jnp.zeros((count, 4, rows, cols), low)
        full = lax.dynamic_update_index_in_dim(full, own, row, 1)
        full = lax.dynamic_update_index_in_dim(full, send(own, SWAP_C), row ^ 1, 1)
        full = lax.dynamic_update_index_in_dim(full, mine, row ^ 2, 1)
        full = lax.dynamic_update_index_in_dim(full, send(mine, SWAP_C), row ^ 3, 1)
        return full.reshape(count, 4 * rows, cols)

    ckv_weight = whole(cross_kv)
    mid = whole(jnp.stack([self_out, cross_query, cross_out]))
    o_weight, cq_weight, co_weight = mid[0], mid[1], mid[2]
    in_weight = whole(fc_in[None])[0]
    out_weight = whole(fc_out[None])[0]

    mk = project(mem_own, ckv_weight[0]).astype(low)
    mv = project(mem_own, ckv_weight[1]).astype(low)
    mkv = jnp.stack([mk, mv])
    mkv_y = send(mkv, SWAP_Y)
    mkv2 = jnp.concatenate([mkv, mkv_y], 1)
    mkv_c = send(mkv2, SWAP_C)
    pre_cross = prefix_cross.astype(low)
    cross_k = jnp.concatenate([pre_cross[0], mkv2[0], mkv_c[0]], 0)
    cross_v = jnp.concatenate([pre_cross[1], mkv2[1], mkv_c[1]], 0)
    cross_mask = jnp.concatenate([jnp.ones((prefix_count,), jnp.bool_), slot < live])[None, :]

    group = 2 * y + c
    q = (project(tok_all, head_w[0]) * scale).astype(low)
    k = project(tok_all, head_w[1]).astype(low)
    v = project(tok_all, head_w[2]).astype(low)
    pre = lax.dynamic_slice_in_dim(prefix_self, group * 256, 256, 2).astype(low)
    self_k = jnp.concatenate([pre[0], k], 0)
    self_v = jnp.concatenate([pre[1], v], 0)
    self_mask = jnp.concatenate(
        [jnp.ones((512, prefix_count), jnp.bool_), pos[None, :] <= pos[:, None]], axis=1
    )
    att, self_lse = attend(q, self_k, self_v, self_mask)
    att = att.astype(low)

    def natural(parts):
        full = jnp.zeros((4, 128, 256), low)
        for k, part in enumerate(parts):
            where = (2 * (y ^ (k & 1))) + (c ^ (k >> 1))
            full = lax.dynamic_update_index_in_dim(full, part, where, 0)
        return full.transpose(1, 0, 2).reshape(128, 1024)

    att = att.reshape(4, 128, 256)
    got = send(jnp.stack([att[1], att[3]]), SWAP_Y)
    got_c = send(jnp.stack([att[2], got[1]]), SWAP_C)
    attended = natural([att[0], got[0], got_c[0], got_c[1]])

    resid_one = tok_own.astype(f32) + project(attended, o_weight)
    hidden_one, unit_one, inv_one = normalize(resid_one, ln_gain[0], ln_bias[0])
    cq = (project(hidden_one.astype(low), cq_weight) * scale).astype(low)
    catt, cross_lse = attend(cq, cross_k, cross_v, cross_mask)
    resid_two = hidden_one + project(catt.astype(low), co_weight)
    hidden_two, unit_two, inv_two = normalize(resid_two, ln_gain[1], ln_bias[1])
    hidden_low = hidden_two.astype(low)
    up_proj = project(hidden_low, in_weight)
    activated = gelu_exact(up_proj).astype(low)
    ffn_out = project(activated, out_weight)
    down_weight = ad_down.astype(low)
    up_weight = ad_up.astype(low)
    down_proj = project(hidden_low, down_weight) + ad_down_bias
    down_act = gelu_exact(down_proj).astype(low)
    adapted = project(down_act, up_weight) + ad_up_bias
    resid_three = hidden_two + ffn_out + 4.0 * adapted
    output, unit_three, inv_three = normalize(resid_three, ln_gain[2], ln_bias[2])
    mixed = output.astype(low).reshape(2, 64, 1024)
    mixed = jnp.stack(turn(mixed[0], mixed[1], odd))

    grad_three = normalize_back(cot_own.astype(f32), unit_three, inv_three, ln_gain[2])
    grad_ffn = grad_three.astype(low)
    grad_adapt = (4.0 * grad_three).astype(low)
    grad_up_w = jnp.einsum("na,nd->ad", down_act, grad_adapt, preferred_element_type=f32)
    grad_up_b = jnp.sum(grad_adapt.astype(f32), axis=0)
    grad_down = gelu_back(down_proj, project(grad_adapt, up_weight.T)).astype(low)
    grad_down_w = jnp.einsum("nd,na->da", hidden_low, grad_down, preferred_element_type=f32)
    grad_down_b = jnp.sum(grad_down.astype(f32), axis=0)
    grad_inner = gelu_back(up_proj, project(grad_ffn, out_weight.T)).astype(low)
    grad_hidden_two = (
        grad_three + project(grad_inner, in_weight.T) + project(grad_down, down_weight.T)
    )
    grad_two = normalize_back(grad_hidden_two, unit_two, inv_two, ln_gain[1])
    grad_catt = project(grad_two.astype(low), co_weight.T).astype(low)
    grad_cq, grad_ck, grad_cv = attend_back(cq, cross_k, cross_v, cross_mask, cross_lse, grad_catt)
    grad_hidden_one = grad_two + project(grad_cq.astype(low), cq_weight.T) * scale
    grad_one = normalize_back(grad_hidden_one, unit_one, inv_one, ln_gain[0])
    grad_att = project(grad_one.astype(low), o_weight.T).astype(low)

    parts = grad_att.reshape(128, 4, 256)
    at = lambda k: lax.dynamic_index_in_dim(
        parts, (2 * (y ^ (k & 1))) + (c ^ (k >> 1)), 1, keepdims=False
    )
    got_c = send(jnp.stack([at(2), at(3)]), SWAP_C)
    got = send(jnp.stack([at(1), got_c[1]]), SWAP_Y)
    grad_o = jnp.concatenate([at(0), got[0], got_c[0], got[1]], 0)
    dq, dk, dv = attend_back(q, self_k, self_v, self_mask, self_lse, grad_o)

    def fold(values):
        half = send(values[2:].astype(low), SWAP_C).astype(f32) + values[:2]
        return half[0] + send(half[1].astype(low), SWAP_Y).astype(f32)

    dmkv = jnp.concatenate([grad_ck[prefix_count:], grad_cv[prefix_count:]], 1).reshape(4, 256, 2048)
    dmkv = fold(dmkv).astype(low)
    d_memory = project(dmkv[:, :1024], ckv_weight[0].T) + project(dmkv[:, 1024:], ckv_weight[1].T)
    d_memory = d_memory.astype(low).reshape(2, 128, 1024)
    d_memory = jnp.stack(turn(d_memory[0], d_memory[1], odd))

    part = (
        project(dq.astype(low), head_w[0].T) * scale
        + project(dk[prefix_count:].astype(low), head_w[1].T)
        + project(dv[prefix_count:].astype(low), head_w[2].T)
    )
    d_tokens = (grad_one + fold(part.reshape(4, 128, 1024))).astype(low).reshape(2, 64, 1024)
    d_tokens = jnp.stack(turn(d_tokens[0], d_tokens[1], odd))

    pre_self_grad = jnp.stack([dk[:prefix_count], dv[:prefix_count]])
    pre_self_grad = lax.dynamic_update_slice_in_dim(
        jnp.zeros(prefix_self.shape, f32), pre_self_grad, group * 256, 2
    )
    pre_cross_grad = jnp.stack([grad_ck[:prefix_count], grad_cv[:prefix_count]])
    totals = lax.psum(
        (pre_self_grad, pre_cross_grad, grad_down_w, grad_down_b, grad_up_w, grad_up_b),
        ("row", "seq"),
    )
    return (mixed, d_tokens, d_memory, *totals)


def solution(mesh):
    in_specs = (
        P("row", "seq", None),
        P("row", "seq", None),
        P("row"),
        P(),
        P(),
        P(),
        P("row", None),
        P(None, "row", None),
        P("row", None),
        P("row", None),
        P(None, "row", None),
        P("row", None),
        P("row", None),
        P("row", None),
        P(),
        P(),
        P(),
        P(),
        P(),
        P(),
        P("row", "seq", None),
    )
    out_specs = (
        P("row", "seq", None),
        P("row", "seq", None),
        P("row", "seq", None),
        P(),
        P(),
        P(),
        P(),
        P(),
        P(),
    )
    local = local_pairs if (mesh.shape["row"], mesh.shape["seq"]) == (4, 8) else local_rows
    return jax.shard_map(local, mesh=mesh, in_specs=in_specs, out_specs=out_specs, check_vma=False)
```

```python
import functools

import jax
import jax.numpy as jnp
from jax import lax
from jax.experimental import pallas as pl
from jax.experimental.pallas import tpu as pltpu
from jax.sharding import PartitionSpec as P

H = 16
HD = 64


EPSILON = 1e-05
MASKED = -1e30


def normalize(value, gain, shift):
    centre = value - jnp.mean(value, axis=-1, keepdims=True)
    inv_dev = lax.rsqrt(jnp.mean(centre * centre, axis=-1, keepdims=True) + EPSILON)
    unit_val = centre * inv_dev
    return (unit_val * gain + shift, unit_val, inv_dev)


def normalize_back(grad, unit_val, inv_dev, gain):
    scaled = grad * gain
    return inv_dev * (
        scaled
        - jnp.mean(scaled, axis=-1, keepdims=True)
        - unit_val * jnp.mean(scaled * unit_val, axis=-1, keepdims=True)
    )


def gelu_exact(value):
    return jax.nn.gelu(value, approximate=False)


def gelu_back(value, grad):
    return jax.vjp(gelu_exact, value)[1](grad)[0]


def head_split(matrix):
    return matrix.reshape(matrix.shape[0], -1, HD)


def masked_scores(queries, keys, mask):
    scores = jnp.einsum(
        "qhd,khd->hqk", head_split(queries), head_split(keys), preferred_element_type=jnp.float32
    )
    return jnp.where(mask[None], scores, MASKED)


def attend(queries, keys, values, mask):
    scores = masked_scores(queries, keys, mask)
    top_score = jnp.max(scores, axis=-1, keepdims=True)
    log_total = top_score + jnp.log(jnp.sum(jnp.exp(scores - top_score), axis=-1, keepdims=True))
    probs = jnp.exp(scores - log_total).astype(jnp.bfloat16)
    result = jnp.einsum(
        "hqk,khd->qhd", probs, head_split(values), preferred_element_type=jnp.float32
    )
    return (result.reshape(queries.shape[0], -1), log_total)


def attend_back(queries, keys, values, mask, log_total, grad_out):
    probs = jnp.exp(masked_scores(queries, keys, mask) - log_total)
    grad_heads = head_split(grad_out)
    grad_probs = jnp.einsum(
        "qhd,khd->hqk", grad_heads, head_split(values), preferred_element_type=jnp.float32
    )
    row_delta = jnp.sum(probs * grad_probs, axis=-1, keepdims=True)
    grad_scores = (probs * (grad_probs - row_delta)).astype(jnp.bfloat16)
    grad_query = jnp.einsum(
        "hqk,khd->qhd", grad_scores, head_split(keys), preferred_element_type=jnp.float32
    )
    grad_keys = jnp.einsum(
        "hqk,qhd->khd", grad_scores, head_split(queries), preferred_element_type=jnp.float32
    )
    grad_values = jnp.einsum(
        "hqk,qhd->khd", probs.astype(jnp.bfloat16), grad_heads, preferred_element_type=jnp.float32
    )
    return (
        grad_query.reshape(queries.shape[0], -1),
        grad_keys.reshape(keys.shape[0], -1),
        grad_values.reshape(values.shape[0], -1),
    )


def project(left, right):
    return jnp.dot(left, right, preferred_element_type=jnp.float32)


def local_rows(
    tokens,
    memory,
    source_len,
    bucket_order,
    prefix_self,
    prefix_cross,
    self_query,
    self_kv,
    self_out,
    cross_query,
    cross_kv,
    cross_out,
    fc_in,
    fc_out,
    ln_gain,
    ln_bias,
    ad_down,
    ad_down_bias,
    ad_up,
    ad_up_bias,
    cotangent,
):
    low_type = jnp.bfloat16
    row_count, tok_count, width = tokens.shape
    slot_count = memory.shape[1]
    prefix_count = prefix_self.shape[1]
    half_len = tok_count // 2
    scale = HD ** (-0.5)
    weight_set = (
        lax.all_gather(self_query.astype(low_type), "row", axis=0, tiled=True),
        lax.all_gather(self_kv.astype(low_type), "row", axis=1, tiled=True),
        lax.all_gather(self_out.astype(low_type), "row", axis=0, tiled=True),
        lax.all_gather(cross_query.astype(low_type), "row", axis=0, tiled=True),
        lax.all_gather(cross_kv.astype(low_type), "row", axis=1, tiled=True),
        lax.all_gather(cross_out.astype(low_type), "row", axis=0, tiled=True),
        lax.all_gather(fc_in.astype(low_type), "row", axis=0, tiled=True),
        lax.all_gather(fc_out.astype(low_type), "row", axis=0, tiled=True),
    )
    q_weight, kv_weight, o_weight, cq_weight, ckv_weight, co_weight, in_weight, out_weight = (
        weight_set
    )
    place = lax.axis_index("seq")
    offsets = jnp.arange(half_len, dtype=jnp.int32)
    all_pos = (bucket_order[:, None] * half_len + offsets[None, :]).reshape(-1)
    own_pos = lax.dynamic_slice_in_dim(all_pos, place * tok_count, tok_count)
    self_mask = jnp.concatenate(
        [jnp.ones((tok_count, prefix_count), jnp.bool_), all_pos[None, :] <= own_pos[:, None]],
        axis=1,
    )
    flat_tokens = tokens.reshape(-1, width)
    queries = (project(flat_tokens, q_weight) * scale).astype(low_type)
    own_keys = (
        project(flat_tokens, kv_weight[0]).astype(low_type).reshape(row_count, tok_count, width)
    )
    own_values = (
        project(flat_tokens, kv_weight[1]).astype(low_type).reshape(row_count, tok_count, width)
    )
    flat_memory = memory.reshape(-1, width)
    mem_keys = (
        project(flat_memory, ckv_weight[0]).astype(low_type).reshape(row_count, slot_count, width)
    )
    mem_values = (
        project(flat_memory, ckv_weight[1]).astype(low_type).reshape(row_count, slot_count, width)
    )
    all_keys, all_values, all_mkeys, all_mvalues = (
        lax.all_gather(own_keys, "seq", axis=1, tiled=True),
        lax.all_gather(own_values, "seq", axis=1, tiled=True),
        lax.all_gather(mem_keys, "seq", axis=1, tiled=True),
        lax.all_gather(mem_values, "seq", axis=1, tiled=True),
    )
    src_total = all_mkeys.shape[1]
    pre_self = prefix_self.astype(low_type)
    pre_cross = prefix_cross.astype(low_type)
    self_key_sets = [
        jnp.concatenate([pre_self[0], all_keys[row_index]], 0) for row_index in range(row_count)
    ]
    self_value_sets = [
        jnp.concatenate([pre_self[1], all_values[row_index]], 0) for row_index in range(row_count)
    ]
    cross_key_sets = [
        jnp.concatenate([pre_cross[0], all_mkeys[row_index]], 0) for row_index in range(row_count)
    ]
    cross_value_sets = [
        jnp.concatenate([pre_cross[1], all_mvalues[row_index]], 0) for row_index in range(row_count)
    ]
    slot_number = jnp.arange(src_total, dtype=jnp.int32)
    cross_masks = [
        jnp.concatenate(
            [jnp.ones((prefix_count,), jnp.bool_), slot_number < source_len[row_index]]
        )[None, :]
        for row_index in range(row_count)
    ]

    def rows_of(matrix, row_index):
        return matrix[row_index * tok_count : (row_index + 1) * tok_count]

    self_parts = [
        attend(
            rows_of(queries, row_index),
            self_key_sets[row_index],
            self_value_sets[row_index],
            self_mask,
        )
        for row_index in range(row_count)
    ]
    attended = jnp.concatenate([part[0] for part in self_parts], 0).astype(low_type)
    resid_one = flat_tokens.astype(jnp.float32) + project(attended, o_weight)
    hidden_one, unit_one, inv_one = normalize(resid_one, ln_gain[0], ln_bias[0])
    cross_queries = (project(hidden_one.astype(low_type), cq_weight) * scale).astype(low_type)
    cross_parts = [
        attend(
            rows_of(cross_queries, row_index),
            cross_key_sets[row_index],
            cross_value_sets[row_index],
            cross_masks[row_index],
        )
        for row_index in range(row_count)
    ]
    cross_att = jnp.concatenate([part[0] for part in cross_parts], 0).astype(low_type)
    resid_two = hidden_one + project(cross_att, co_weight)
    hidden_two, unit_two, inv_two = normalize(resid_two, ln_gain[1], ln_bias[1])
    hidden_low = hidden_two.astype(low_type)
    up_proj = project(hidden_low, in_weight)
    activated = gelu_exact(up_proj).astype(low_type)
    ffn_out = project(activated, out_weight)
    down_weight = ad_down.astype(low_type)
    up_weight = ad_up.astype(low_type)
    down_proj = project(hidden_low, down_weight) + ad_down_bias
    down_act = gelu_exact(down_proj).astype(low_type)
    adapted = project(down_act, up_weight) + ad_up_bias
    resid_three = hidden_two + ffn_out + 4.0 * adapted
    output, unit_three, inv_three = normalize(resid_three, ln_gain[2], ln_bias[2])
    mixed = output.astype(low_type).reshape(row_count, tok_count, width)
    weight_set = (
        lax.all_gather(self_query.astype(low_type), "row", axis=0, tiled=True),
        lax.all_gather(self_kv.astype(low_type), "row", axis=1, tiled=True),
        lax.all_gather(self_out.astype(low_type), "row", axis=0, tiled=True),
        lax.all_gather(cross_query.astype(low_type), "row", axis=0, tiled=True),
        lax.all_gather(cross_kv.astype(low_type), "row", axis=1, tiled=True),
        lax.all_gather(cross_out.astype(low_type), "row", axis=0, tiled=True),
        lax.all_gather(fc_in.astype(low_type), "row", axis=0, tiled=True),
        lax.all_gather(fc_out.astype(low_type), "row", axis=0, tiled=True),
    )
    q_weight, kv_weight, o_weight, cq_weight, ckv_weight, co_weight, in_weight, out_weight = (
        weight_set
    )
    grad_out = cotangent.astype(jnp.float32).reshape(-1, width)
    grad_three = normalize_back(grad_out, unit_three, inv_three, ln_gain[2])
    grad_ffn = grad_three.astype(low_type)
    grad_adapt = (4.0 * grad_three).astype(low_type)
    grad_up_w = jnp.einsum("na,nd->ad", down_act, grad_adapt, preferred_element_type=jnp.float32)
    grad_up_b = jnp.sum(grad_adapt.astype(jnp.float32), axis=0)
    grad_down = gelu_back(down_proj, project(grad_adapt, up_weight.T)).astype(low_type)
    grad_down_w = jnp.einsum("nd,na->da", hidden_low, grad_down, preferred_element_type=jnp.float32)
    grad_down_b = jnp.sum(grad_down.astype(jnp.float32), axis=0)
    grad_inner = gelu_back(up_proj, project(grad_ffn, out_weight.T)).astype(low_type)
    grad_hidden_two = (
        grad_three + project(grad_inner, in_weight.T) + project(grad_down, down_weight.T)
    )
    grad_two = normalize_back(grad_hidden_two, unit_two, inv_two, ln_gain[1])
    grad_cross_att = project(grad_two.astype(low_type), co_weight.T).astype(low_type)
    cross_grads = [
        attend_back(
            rows_of(cross_queries, row_index),
            cross_key_sets[row_index],
            cross_value_sets[row_index],
            cross_masks[row_index],
            cross_parts[row_index][1],
            rows_of(grad_cross_att, row_index),
        )
        for row_index in range(row_count)
    ]
    grad_cq = jnp.concatenate([part[0] for part in cross_grads], 0).astype(low_type)
    grad_hidden_one = grad_two + project(grad_cq, cq_weight.T) * scale
    grad_one = normalize_back(grad_hidden_one, unit_one, inv_one, ln_gain[0])
    grad_attended = project(grad_one.astype(low_type), o_weight.T).astype(low_type)
    self_grads = [
        attend_back(
            rows_of(queries, row_index),
            self_key_sets[row_index],
            self_value_sets[row_index],
            self_mask,
            self_parts[row_index][1],
            rows_of(grad_attended, row_index),
        )
        for row_index in range(row_count)
    ]
    pre_self_grad = jnp.stack(
        [
            sum((part[1][:prefix_count] for part in self_grads)),
            sum((part[2][:prefix_count] for part in self_grads)),
        ]
    )
    pre_cross_grad = jnp.stack(
        [
            sum((part[1][:prefix_count] for part in cross_grads)),
            sum((part[2][:prefix_count] for part in cross_grads)),
        ]
    )
    summed = [
        (
            lax.psum_scatter(
                self_grads[row_index][1][prefix_count:].astype(jnp.bfloat16),
                "seq",
                scatter_dimension=0,
                tiled=True,
            ).astype(jnp.float32),
            lax.psum_scatter(
                self_grads[row_index][2][prefix_count:].astype(jnp.bfloat16),
                "seq",
                scatter_dimension=0,
                tiled=True,
            ).astype(jnp.float32),
            lax.psum_scatter(
                cross_grads[row_index][1][prefix_count:].astype(jnp.bfloat16),
                "seq",
                scatter_dimension=0,
                tiled=True,
            ).astype(jnp.float32),
            lax.psum_scatter(
                cross_grads[row_index][2][prefix_count:].astype(jnp.bfloat16),
                "seq",
                scatter_dimension=0,
                tiled=True,
            ).astype(jnp.float32),
        )
        for row_index in range(row_count)
    ]
    key_grad = jnp.stack([part[0] for part in summed])
    value_grad = jnp.stack([part[1] for part in summed])
    mkey_grad = jnp.stack([part[2] for part in summed])
    mvalue_grad = jnp.stack([part[3] for part in summed])
    grad_query = jnp.concatenate([part[0] for part in self_grads], 0).astype(low_type)
    d_tokens = (
        grad_one
        + project(grad_query, q_weight.T) * scale
        + project(key_grad.astype(low_type).reshape(-1, width), kv_weight[0].T)
        + project(value_grad.astype(low_type).reshape(-1, width), kv_weight[1].T)
    )
    d_memory = project(mkey_grad.astype(low_type).reshape(-1, width), ckv_weight[0].T) + project(
        mvalue_grad.astype(low_type).reshape(-1, width), ckv_weight[1].T
    )
    totals = lax.psum(
        (pre_self_grad, pre_cross_grad, grad_down_w, grad_down_b, grad_up_w, grad_up_b),
        ("row", "seq"),
    )
    return (
        mixed,
        d_tokens.astype(low_type).reshape(row_count, tok_count, width),
        d_memory.astype(low_type).reshape(row_count, slot_count, width),
        totals[0],
        totals[1],
        totals[2],
        totals[3],
        totals[4],
        totals[5],
    )


LOW = jnp.bfloat16
F32 = jnp.float32
SCALE = 0.125
VMEM = pl.BlockSpec(memory_space=pltpu.VMEM)
SMEM = pl.BlockSpec(memory_space=pltpu.SMEM)
ANY = pl.BlockSpec(memory_space=pl.ANY)


def shape_of(shape, dtype=LOW):
    return jax.ShapeDtypeStruct(shape, dtype)


def nn(left, right):
    return jnp.dot(left, right, preferred_element_type=F32)


def nt(left, right):
    return lax.dot_general(left, right, (((1,), (1,)), ((), ())), preferred_element_type=F32)


def tn(left, right):
    return lax.dot_general(left, right, (((0,), (0,)), ((), ())), preferred_element_type=F32)


def cols(start, size):
    return pl.ds(pl.multiple_of(start, 128), size)


def ln(value, gain, shift):
    centre = value - jnp.mean(value, axis=-1, keepdims=True)
    inv = lax.rsqrt(jnp.mean(centre * centre, axis=-1, keepdims=True) + EPSILON)
    unit = centre * inv
    return unit * gain + shift, unit, inv


def ln_back(grad, unit, inv, gain):
    scaled = grad * gain
    return inv * (
        scaled
        - jnp.mean(scaled, axis=-1, keepdims=True)
        - unit * jnp.mean(scaled * unit, axis=-1, keepdims=True)
    )


def gelu_both(value):
    cdf = 0.5 * (1.0 + lax.erf(value * 0.7071067811865476))
    return value * cdf, cdf + value * (jnp.exp(-0.5 * value * value) * 0.3989422804014327)


def stacked(block):
    first = lax.broadcasted_iota(jnp.int32, block.shape, 1) < 64
    zero = jnp.zeros_like(block)
    return jnp.concatenate([jnp.where(first, block, zero), jnp.where(first, zero, block)], 0)


def unstacked(both, n):
    return jnp.concatenate([both[:64, :n], both[64:, n:]], 0).T


def pre_mask(shape, count):
    return lax.broadcasted_iota(jnp.int32, shape, 0) < count


def soft_pair(qs, k_pre, k_blocks, vt_pre, vt_blocks, biases, count):
    s_pre = nt(k_pre, qs)
    s_pre = jnp.where(pre_mask(s_pre.shape, count), s_pre, MASKED)
    s_blocks = [nt(k, qs) + b for k, b in zip(k_blocks, biases)]
    top = jnp.max(s_pre, axis=0, keepdims=True)
    for s in s_blocks:
        top = jnp.maximum(top, jnp.max(s, axis=0, keepdims=True))
    e_pre = jnp.exp(s_pre - top)
    total = jnp.sum(e_pre, axis=0, keepdims=True)
    out = nn(vt_pre, e_pre.astype(LOW))
    for s, vt in zip(s_blocks, vt_blocks):
        e = jnp.exp(s - top)
        total += jnp.sum(e, axis=0, keepdims=True)
        out += nn(vt, e.astype(LOW))
    return out * (1.0 / total), top + jnp.log(total)


def soft_pair_back(qs, dos, lse, k_pre, v_pre, kt_pre, ks, vs, kts, biases, count):
    s_pre = nt(k_pre, qs)
    p_pre = jnp.where(pre_mask(s_pre.shape, count), jnp.exp(s_pre - lse), 0.0)
    d_pre = nt(v_pre, dos)
    delta = jnp.sum(p_pre * d_pre, axis=0, keepdims=True)
    ps, ds = [], []
    for k, v, b in zip(ks, vs, biases):
        p = jnp.exp(nt(k, qs) + b - lse)
        d = nt(v, dos)
        delta += jnp.sum(p * d, axis=0, keepdims=True)
        ps.append(p)
        ds.append(d)
    g_pre = (p_pre * (d_pre - delta)).astype(LOW)
    dq = nn(kt_pre, g_pre)
    dk, dv = [nn(g_pre, qs)], [nn(p_pre.astype(LOW), dos)]
    for p, d, kt in zip(ps, ds, kts):
        g = (p * (d - delta)).astype(LOW)
        dq += nn(kt, g)
        dk.append(nn(g, qs))
        dv.append(nn(p.astype(LOW), dos))
    return dq, dk, dv


def self_bias(kpos_ref, qpos_ref, t):
    seen = kpos_ref[...] <= qpos_ref[:, t * 128 : (t + 1) * 128]
    bias = jnp.where(seen, 0.0, MASKED)
    return jnp.concatenate([bias, bias], 1)


def self_fwd_kernel(
    count, ids, tok_a, tok_b, w0, w1, w2, w3, pre, pre_t, kpos, qpos, q_ref, k_ref, v_ref, o_ref, lse_ref, vt
):
    for t, tok in enumerate((tok_a, tok_b)):
        rows = slice(t * 256, (t + 1) * 256)
        for j, out in enumerate((q_ref, k_ref, v_ref)):
            acc = None
            for n, w in enumerate((w0, w1, w2, w3)):
                term = nn(tok[:, cols(ids[n] * 256, 256)], w[j])
                acc = term if acc is None else acc + term
            out[rows, :] = (acc * SCALE if j == 0 else acc).astype(LOW)
    vt[...] = v_ref[...].T
    for t in range(4):
        bias = self_bias(kpos, qpos, t)
        for p in range(2):
            lanes = slice(p * 128, (p + 1) * 128)
            qs = stacked(q_ref[t * 128 : (t + 1) * 128, lanes])
            out, lse = soft_pair(
                qs, pre[0, :, lanes], [k_ref[:, lanes]], pre_t[1, lanes, :], [vt[lanes, :]], [bias], count
            )
            o_ref[t, :, lanes] = unstacked(out, 128).astype(LOW)
            lse_ref[p, t] = lse


def self_fwd(ids, tok_a, tok_b, ws, pre, pre_t, kpos, qpos, count):
    return pl.pallas_call(
        functools.partial(self_fwd_kernel, count),
        in_specs=[SMEM] + [VMEM] * 10,
        out_specs=[VMEM] * 5,
        out_shape=[
            shape_of((512, 256)),
            shape_of((512, 256)),
            shape_of((512, 256)),
            shape_of((4, 128, 256)),
            shape_of((2, 4, 1, 256), F32),
        ],
        scratch_shapes=[pltpu.VMEM((256, 512), LOW)],
        compiler_params=pltpu.CompilerParams(vmem_limit_bytes=40 * 2**20),
        name="self_fwd",
    )(ids, tok_a, tok_b, *ws, pre, pre_t, kpos, qpos)


def self_bwd_kernel(
    count, ids, q, k, v, do_ref, lse_ref, w0, w1, w2, w3, pre, pre_t, kpos, qpos, part_ref, gpre_ref, kt, dq, dk, dv
):
    kt[...] = k[...].T
    for t in range(4):
        bias = self_bias(kpos, qpos, t)
        for p in range(2):
            lanes = slice(p * 128, (p + 1) * 128)
            qs = stacked(q[t * 128 : (t + 1) * 128, lanes])
            dos = stacked(do_ref[t, :, lanes])
            g, gk, gv = soft_pair_back(
                qs,
                dos,
                lse_ref[p, t],
                pre[0, :, lanes],
                pre[1, :, lanes],
                pre_t[0, lanes, :],
                [k[:, lanes]],
                [v[:, lanes]],
                [kt[lanes, :]],
                [bias],
                count,
            )
            dq[t * 128 : (t + 1) * 128, lanes] = unstacked(g, 128).astype(LOW)
            if t == 0:
                gpre_ref[0, :, lanes] = gk[0]
                gpre_ref[1, :, lanes] = gv[0]
                dk[:, lanes] = gk[1]
                dv[:, lanes] = gv[1]
            else:
                gpre_ref[0, :, lanes] += gk[0]
                gpre_ref[1, :, lanes] += gv[0]
                dk[:, lanes] += gk[1]
                dv[:, lanes] += gv[1]
    dkl, dvl = dk[...].astype(LOW), dv[...].astype(LOW)
    for n, w in enumerate((w0, w1, w2, w3)):
        part_ref[:, cols(ids[n] * 256, 256)] = (
            nt(dq[...], w[0]) * SCALE + nt(dkl, w[1]) + nt(dvl, w[2])
        ).astype(LOW)


def self_bwd(ids, q, k, v, do, lse, ws, pre, pre_t, kpos, qpos, count):
    return pl.pallas_call(
        functools.partial(self_bwd_kernel, count),
        in_specs=[SMEM] + [VMEM] * 13,
        out_specs=[VMEM] * 2,
        out_shape=[shape_of((512, 1024)), shape_of((2, 32, 256), F32)],
        scratch_shapes=[
            pltpu.VMEM((256, 512), LOW),
            pltpu.VMEM((512, 256), LOW),
            pltpu.VMEM((512, 256), F32),
            pltpu.VMEM((512, 256), F32),
        ],
        compiler_params=pltpu.CompilerParams(vmem_limit_bytes=40 * 2**20),
        name="self_bwd",
    )(ids, q, k, v, do, lse, *ws, pre, pre_t, kpos, qpos)


def part_sizes(parts):
    return [p.shape[1] for p in parts]


def mm(x_ref, parts, ids, j):
    acc = None
    for n, part in enumerate(parts):
        size = part.shape[1]
        term = nn(x_ref[:, cols(ids[4 + n] * 128, size)], part[j])
        acc = term if acc is None else acc + term
    return acc


def mem_kernel(ids, mem, *refs):
    parts, out = refs[:6], refs[6]
    for j in range(2):
        out[j] = mm(mem, parts, ids, j).astype(LOW)


def mem_fwd(ids, mem, parts):
    return pl.pallas_call(
        mem_kernel,
        in_specs=[SMEM] + [VMEM] * 7,
        out_specs=VMEM,
        out_shape=shape_of((2, 256, 1024)),
        compiler_params=pltpu.CompilerParams(vmem_limit_bytes=40 * 2**20),
        name="mem_fwd",
    )(ids, mem, *parts)


def mem_back_kernel(ids, near, far_c, far_y, *refs):
    parts, out = refs[:6], refs[6]
    total = [
        (near[j, :256].astype(F32) + far_c[j, :256].astype(F32) + far_y[j].astype(F32)).astype(LOW)
        for j in range(2)
    ]
    for n, part in enumerate(parts):
        out[:, cols(ids[4 + n] * 128, part.shape[1])] = (nt(total[0], part[0]) + nt(total[1], part[1])).astype(LOW)


def mem_back(ids, near, far_c, far_y, parts):
    return pl.pallas_call(
        mem_back_kernel,
        in_specs=[SMEM] + [VMEM] * 9,
        out_specs=VMEM,
        out_shape=shape_of((256, 1024)),
        compiler_params=pltpu.CompilerParams(vmem_limit_bytes=40 * 2**20),
        name="mem_back",
    )(ids, near, far_c, far_y, *parts)


def fill_bias(bias, ids):
    live, c, y = ids[10], ids[11], ids[12]
    for n in range(8):
        core = c if n < 4 else 1 - c
        line = y if n % 4 < 2 else 1 - y
        first = (2 * (2 * core + n % 2) + line) * 128
        slot = lax.broadcasted_iota(jnp.int32, (128, 256), 0) + first
        bias[n * 128 : (n + 1) * 128, :] = jnp.where(slot < live, 0.0, MASKED)


def mid_fwd_kernel(
    count, ids, o0, o1, o2, o3, tok, gain, shift, pre, pre_t, mkv_a, mkv_b, *refs
):
    parts, outs, (bias, flat) = refs[:6], refs[6:14], refs[14:]
    cq_ref, lse_ref, unit1, inv1, h2_ref, unit2, inv2, h2l = outs
    for n, o in enumerate((o0, o1, o2, o3)):
        flat[:, cols(ids[13 + n] * 256, 256)] = o[...]
    fill_bias(bias, ids)
    h1, unit, inv = ln(tok[...].astype(F32) + mm(flat, parts, ids, 0), gain[0:1], shift[0:1])
    unit1[...] = unit
    inv1[...] = inv
    flat[...] = h1.astype(LOW)
    cq_ref[...] = (mm(flat, parts, ids, 1) * SCALE).astype(LOW)
    for p in range(8):
        lanes = slice(p * 128, (p + 1) * 128)
        qs = stacked(cq_ref[:, lanes])
        out, lse = soft_pair(
            qs,
            pre[0, :, lanes],
            [mkv_a[0, :, lanes], mkv_b[0, :, lanes]],
            pre_t[1, lanes, :],
            [mkv_a[1, :, lanes].T, mkv_b[1, :, lanes].T],
            [bias[:512], bias[512:]],
            count,
        )
        flat[:, lanes] = unstacked(out, 128).astype(LOW)
        lse_ref[p] = lse
    h2, unit, inv = ln(h1 + mm(flat, parts, ids, 2), gain[1:2], shift[1:2])
    h2_ref[...] = h2
    unit2[...] = unit
    inv2[...] = inv
    h2l[...] = h2.astype(LOW)


def mid_fwd(ids, os, tok, gain, shift, pre, pre_t, mkv_a, mkv_b, parts, count):
    wide = shape_of((128, 1024), F32)
    thin = shape_of((128, 1), F32)
    return pl.pallas_call(
        functools.partial(mid_fwd_kernel, count),
        in_specs=[SMEM] + [VMEM] * 17,
        out_specs=[VMEM] * 8,
        out_shape=[shape_of((128, 1024)), shape_of((8, 1, 256), F32), wide, thin, wide, wide, thin, shape_of((128, 1024))],
        scratch_shapes=[pltpu.VMEM((1024, 256), F32), pltpu.VMEM((128, 1024), LOW)],
        compiler_params=pltpu.CompilerParams(vmem_limit_bytes=48 * 2**20),
        name="mid_fwd",
    )(ids, *os, tok, gain, shift, pre, pre_t, mkv_a, mkv_b, *parts)


def mlp_kernel(ids, h2, h2l, unit2, inv2, cot, gain, shift, down_b, up_b, down_any, up_any, *refs):
    parts, outs, scratch = refs[:6], refs[6:12], refs[12:]
    mixed, dr2, gau, gadt, gaub, gadb = outs
    bufs, (down, up, act, slope, acc, sems) = scratch[:6], scratch[6:]
    copies = []
    for n in range(6):
        copies.append([pltpu.make_async_copy(parts[n].at[pl.ds(4 * h, 4)], bufs[n].at[pl.ds(4 * h, 4)], sems.at[2 * n + h]) for h in range(2)])
    ad = [pltpu.make_async_copy(down_any, down, sems.at[12]), pltpu.make_async_copy(up_any, up, sems.at[13])]
    for n in range(6):
        copies[n][0].start()
    ad[0].start()
    ad[1].start()
    for n in range(6):
        copies[n][1].start()
    for n in range(6):
        copies[n][0].wait()
    for s in range(4):
        u = mm(h2l, bufs, ids, s)
        lanes = slice(s * 1024, (s + 1) * 1024)
        value, gradient = gelu_both(u)
        act[:, lanes] = value.astype(LOW)
        slope[:, lanes] = gradient
    ad[0].wait()
    ad[1].wait()
    down_w, up_w = down[...].astype(LOW), up[...].astype(LOW)
    a, a_slope = gelu_both(nn(h2l[...], down_w) + down_b[...])
    a = a.astype(LOW)
    adapted = nn(a, up_w) + up_b[...]
    total = h2[...] + 4.0 * adapted
    for n in range(6):
        copies[n][1].wait()

    def rows(n, s):
        return (ids[4 + n] // 2) * 1024 + s * 256 + (ids[4 + n] % 2) * 128

    for s in range(4):
        for n, buf in enumerate(bufs):
            total += nn(act[:, cols(rows(n, s), buf.shape[1])], buf[4 + s])
    out, unit3, inv3 = ln(total, gain[2:3], shift[2:3])
    mixed[...] = out.astype(LOW)
    dr3 = ln_back(cot[...].astype(F32), unit3, inv3, gain[2:3])
    dffn = dr3.astype(LOW)
    dad = (4.0 * dr3).astype(LOW)
    gau[...] = tn(a, dad)
    gaub[...] = jnp.sum(dad.astype(F32), axis=0, keepdims=True)
    ddn = (a_slope * nt(dad, up_w)).astype(LOW)
    gadt[...] = tn(ddn, h2l[...])
    gadb[...] = jnp.sum(ddn.astype(F32), axis=0, keepdims=True)
    for s in range(4):
        for n, buf in enumerate(bufs):
            where = cols(rows(n, s), buf.shape[1])
            act[:, where] = (slope[:, where] * nt(dffn, buf[4 + s])).astype(LOW)
    for n, buf in enumerate(bufs):
        term = nt(act[:, :1024], buf[0])
        for s in range(1, 4):
            term += nt(act[:, s * 1024 : (s + 1) * 1024], buf[s])
        acc[:, cols(ids[4 + n] * 128, buf.shape[1])] = term
    dh2 = dr3 + acc[...] + nt(ddn, down_w)
    dr2[...] = ln_back(dh2, unit2[...], inv2[...], gain[1:2])


def mlp(ids, h2, h2l, unit2, inv2, cot, gain, shift, down_b, up_b, down, up, parts):
    return pl.pallas_call(
        mlp_kernel,
        in_specs=[SMEM] + [VMEM] * 9 + [ANY] * 8,
        out_specs=[VMEM] * 6,
        out_shape=[
            shape_of((128, 1024)),
            shape_of((128, 1024), F32),
            shape_of((512, 1024), F32),
            shape_of((512, 1024), F32),
            shape_of((1, 1024), F32),
            shape_of((1, 512), F32),
        ],
        scratch_shapes=[pltpu.VMEM(p.shape, LOW) for p in parts]
        + [
            pltpu.VMEM((1024, 512), F32),
            pltpu.VMEM((512, 1024), F32),
            pltpu.VMEM((128, 4096), LOW),
            pltpu.VMEM((128, 4096), F32),
            pltpu.VMEM((128, 1024), F32),
            pltpu.SemaphoreType.DMA((14,)),
        ],
        compiler_params=pltpu.CompilerParams(vmem_limit_bytes=56 * 2**20),
        name="mlp",
    )(ids, h2, h2l, unit2, inv2, cot, gain, shift, down_b, up_b, down, up, *parts)


def mid_bwd_kernel(count, ids, dr2, cq, lse, unit1, inv1, gain, pre, pre_t, mkv_a, mkv_b, *refs):
    parts, outs, (bias, flat, wide) = refs[:6], refs[6:11], refs[11:]
    near, far, gpre, dr1, do_ref = outs
    fill_bias(bias, ids)

    def back(value, j):
        for n, part in enumerate(parts):
            wide[:, cols(ids[4 + n] * 128, part.shape[1])] = nt(value, part[j])

    back(dr2[...].astype(LOW), 2)
    flat[...] = wide[...].astype(LOW)
    for p in range(8):
        lanes = slice(p * 128, (p + 1) * 128)
        qs = stacked(cq[:, lanes])
        dos = stacked(flat[:, lanes])
        g, gk, gv = soft_pair_back(
            qs,
            dos,
            lse[p],
            pre[0, :, lanes],
            pre[1, :, lanes],
            pre_t[0, lanes, :],
            [mkv_a[0, :, lanes], mkv_b[0, :, lanes]],
            [mkv_a[1, :, lanes], mkv_b[1, :, lanes]],
            [mkv_a[0, :, lanes].T, mkv_b[0, :, lanes].T],
            [bias[:512], bias[512:]],
            count,
        )
        for j, got in enumerate((gk, gv)):
            gpre[j, :, lanes] = got[0]
            near[j, :, lanes] = got[1].astype(LOW)
            far[j, :, lanes] = got[2].astype(LOW)
        flat[:, lanes] = unstacked(g, 128).astype(LOW)
    back(flat[...], 1)
    dh1 = dr2[...] + SCALE * wide[...]
    grad = ln_back(dh1, unit1[...], inv1[...], gain[0:1])
    dr1[...] = grad
    back(grad.astype(LOW), 0)
    for n in range(4):
        do_ref[n] = wide[:, cols(ids[13 + n] * 256, 256)].astype(LOW)


def mid_bwd(ids, dr2, cq, lse, unit1, inv1, gain, pre, pre_t, mkv_a, mkv_b, parts, count):
    return pl.pallas_call(
        functools.partial(mid_bwd_kernel, count),
        in_specs=[SMEM] + [VMEM] * 16,
        out_specs=[VMEM] * 5,
        out_shape=[
            shape_of((2, 512, 1024)),
            shape_of((2, 512, 1024)),
            shape_of((2, 32, 1024), F32),
            shape_of((128, 1024), F32),
            shape_of((4, 128, 256)),
        ],
        scratch_shapes=[
            pltpu.VMEM((1024, 256), F32),
            pltpu.VMEM((128, 1024), LOW),
            pltpu.VMEM((128, 1024), F32),
        ],
        compiler_params=pltpu.CompilerParams(vmem_limit_bytes=52 * 2**20),
        name="mid_bwd",
    )(ids, dr2, cq, lse, unit1, inv1, gain, pre, pre_t, mkv_a, mkv_b, *parts)


def pack_kernel(sources, ids, *refs):
    n_args = max(a for a, *_ in sources) + 1
    args, (own, half), (wide, low_buf, in_sem, own_sem, half_sem) = refs[:n_args], refs[n_args : n_args + 2], refs[n_args + 2 :]
    y = ids[12]
    count = len(sources)

    def fetch(m):
        a, lead, row, col = sources[m]
        src = args[a] if lead is None else args[a].at[lead]
        return pltpu.make_async_copy(src.at[pl.ds(row, 256), pl.ds(col, 1024)], wide.at[m % 3], in_sem.at[m % 3])

    def store(m):
        return (
            pltpu.make_async_copy(low_buf.at[m % 3], own.at[m], own_sem.at[m % 3]),
            pltpu.make_async_copy(low_buf.at[m % 3, pl.ds(pl.multiple_of(y * 128, 128), 128)], half.at[m], half_sem.at[m % 3]),
        )

    for m in range(min(2, count)):
        fetch(m).start()
    for m in range(count):
        if m + 2 < count:
            fetch(m + 2).start()
        fetch(m).wait()
        if m >= 3:
            for s in store(m - 3):
                s.wait()
        low_buf[m % 3] = wide[m % 3].astype(LOW)
        for s in store(m):
            s.start()
    for m in range(max(0, count - 3), count):
        for s in store(m):
            s.wait()


def pack(ids, sources, *args):
    count = len(sources)
    return pl.pallas_call(
        functools.partial(pack_kernel, sources),
        in_specs=[SMEM] + [ANY] * len(args),
        out_specs=[ANY] * 2,
        out_shape=[shape_of((count, 256, 1024)), shape_of((count, 128, 1024))],
        scratch_shapes=[
            pltpu.VMEM((3, 256, 1024), F32),
            pltpu.VMEM((3, 256, 1024), LOW),
            pltpu.SemaphoreType.DMA((3,)),
            pltpu.SemaphoreType.DMA((3,)),
            pltpu.SemaphoreType.DMA((3,)),
        ],
        compiler_params=pltpu.CompilerParams(vmem_limit_bytes=16 * 2**20),
        name="pack",
    )(ids, *args)


AXES = ("row", "seq")


def pairs_of(target):
    pairs = []
    for source in range(32):
        row, seq = divmod(source, 8)
        x, c, z, y = target(*divmod(row, 2), *divmod(seq, 2))
        pairs.append((source, (2 * x + c) * 8 + 2 * z + y))
    return pairs


SWAP_X = pairs_of(lambda x, c, z, y: (1 - x, c, z, y))
SWAP_C = pairs_of(lambda x, c, z, y: (x, 1 - c, z, y))
SWAP_Y = pairs_of(lambda x, c, z, y: (x, c, z, 1 - y))
TURN = [pairs_of(lambda x, c, z, y, r=r: (x, z // 2, 2 * c + (z + r) % 2, y)) for r in range(2)]


def send(value, pairs):
    return lax.ppermute(value, AXES, pairs)


def turn(first, second, odd):
    out = [send(jnp.where(odd, second, first), TURN[0]), send(jnp.where(odd, first, second), TURN[1])]
    return jnp.where(odd, out[1], out[0]), jnp.where(odd, out[0], out[1])


def local_pairs(
    tokens,
    memory,
    source_len,
    bucket_order,
    prefix_self,
    prefix_cross,
    self_query,
    self_kv,
    self_out,
    cross_query,
    cross_kv,
    cross_out,
    fc_in,
    fc_out,
    ln_gain,
    ln_bias,
    ad_down,
    ad_down_bias,
    ad_up,
    ad_up_bias,
    cotangent,
):
    low = jnp.bfloat16
    f32 = jnp.float32
    row, seq = lax.axis_index("row"), lax.axis_index("seq")
    x, c, z, y = row // 2, row % 2, seq // 2, seq % 2
    odd = z % 2 == 1
    count = prefix_self.shape[1]

    live = send(jnp.where(odd, source_len[1], source_len[0]).reshape(1, 1), TURN[0])[0, 0]
    group = 2 * y + c
    far_row = 2 * (row ^ 2)
    both_row = 2 * (row ^ 3)
    ids = jnp.stack(
        [row, row ^ 1, row ^ 2, row ^ 3]
        + [2 * row, 2 * (row ^ 1), far_row + y, far_row + 1 - y, both_row + y, both_row + 1 - y]
        + [jnp.int32(0), c, y]
        + [group, group ^ 2, group ^ 1, group ^ 3]
    ).astype(jnp.int32)
    ids_live = ids.at[10].set(live)

    tok_own = jnp.concatenate(turn(tokens[0], tokens[1], odd), 0)
    mem_own = jnp.concatenate(turn(memory[0], memory[1], odd), 0)
    cot_own = jnp.concatenate(turn(cotangent[0], cotangent[1], odd), 0)
    tok_a = jnp.concatenate([tok_own, send(tok_own, SWAP_Y)], 0)
    tok_b = send(tok_a, SWAP_C)

    places = (bucket_order[:, None] * 32 + jnp.arange(32, dtype=jnp.int32)[None]).reshape(2, 2, 2, 64)
    places = places.transpose(0, 2, 1, 3)
    places = jnp.where(c == 0, places, places[::-1])
    places = jnp.where(y == 0, places, places[:, ::-1])
    kpos, qpos = places.reshape(512, 1), places.reshape(1, 512)

    packed = jnp.stack([self_query, self_kv[0], self_kv[1]])
    packed = lax.dynamic_slice_in_dim(packed.reshape(3, 256, 2, 512), y, 1, 2).reshape(3, 256, 2, 256)
    packed = packed.astype(low).transpose(2, 0, 1, 3)
    far = send(packed, SWAP_X)
    keep, give = jnp.where(c == 0, packed[0], packed[1]), jnp.where(c == 0, packed[1], packed[0])
    far_keep, far_give = jnp.where(c == 0, far[0], far[1]), jnp.where(c == 0, far[1], far[0])
    head_parts = [keep, send(give, SWAP_C), far_keep, send(far_give, SWAP_C)]

    def whole(sources, *arrays):
        own, half = pack(ids, sources, *arrays)
        near = send(half, SWAP_X)
        return (own, send(own, SWAP_C)), near

    def rest(own, near):
        other = send(near, SWAP_Y)
        return (*own, near, other, send(near, SWAP_C), send(other, SWAP_C))

    ckv_parts = rest(*whole([(0, 0, 0, 0), (0, 1, 0, 0)], cross_kv))
    mid_parts = rest(
        *whole([(n, None, 0, 0) for n in range(3)], self_out, cross_query, cross_out)
    )
    ffn_parts = rest(
        *whole(
            [(0, None, 0, s * 1024) for s in range(4)] + [(1, None, s * 256, 0) for s in range(4)],
            fc_in,
            fc_out,
        )
    )

    def padded(prefix):
        wide = jnp.pad(prefix.astype(low), ((0, 0), (0, 32 - count), (0, 0)))
        return wide, wide.transpose(0, 2, 1)

    pre_c, pre_ct = padded(prefix_cross)
    pre_s, pre_st = padded(lax.dynamic_slice_in_dim(prefix_self, group * 256, 256, 2))

    mkv = mem_fwd(ids, mem_own, ckv_parts)
    mkv_a = jnp.concatenate([mkv, send(mkv, SWAP_Y)], 1)
    mkv_b = send(mkv_a, SWAP_C)

    q, k, v, att, self_lse = self_fwd(ids, tok_a, tok_b, head_parts, pre_s, pre_st, kpos, qpos, count)
    got = send(jnp.stack([att[1], att[3]]), SWAP_Y)
    got_c = send(jnp.stack([att[2], got[1]]), SWAP_C)

    cq, cross_lse, unit1, inv1, h2, unit2, inv2, h2l = mid_fwd(
        ids_live,
        (att[0], got[0], got_c[0], got_c[1]),
        tok_own,
        ln_gain,
        ln_bias,
        pre_c,
        pre_ct,
        mkv_a,
        mkv_b,
        mid_parts,
        count,
    )
    mixed, dr2, gau, gadt, gaub, gadb = mlp(
        ids,
        h2,
        h2l,
        unit2,
        inv2,
        cot_own,
        ln_gain,
        ln_bias,
        ad_down_bias[None],
        ad_up_bias[None],
        ad_down,
        ad_up,
        ffn_parts,
    )
    mixed = mixed.reshape(2, 64, 1024)
    mixed = jnp.stack(turn(mixed[0], mixed[1], odd))

    near, far_c, gpre_cross, dr1, grad_att = mid_bwd(
        ids_live, dr2, cq, cross_lse, unit1, inv1, ln_gain, pre_c, pre_ct, mkv_a, mkv_b, mid_parts, count
    )

    got_c = send(grad_att[2:], SWAP_C)
    got = send(jnp.stack([grad_att[1], got_c[1]]), SWAP_Y)
    grad_o = jnp.stack([grad_att[0], got[0], got_c[0], got[1]])
    part, gpre_self = self_bwd(
        ids, q, k, v, grad_o, self_lse, head_parts, pre_s, pre_st, kpos, qpos, count
    )

    got_c = send(far_c, SWAP_C)
    got = send((near[:, 256:].astype(f32) + got_c[:, 256:].astype(f32)).astype(low), SWAP_Y)
    d_memory = mem_back(ids, near, got_c, got, ckv_parts).reshape(2, 128, 1024)
    d_memory = jnp.stack(turn(d_memory[0], d_memory[1], odd))

    half = part[:256].astype(f32) + send(part[256:], SWAP_C).astype(f32)
    d_tokens = dr1 + half[:128] + send(half[128:].astype(low), SWAP_Y).astype(f32)
    d_tokens = d_tokens.astype(low).reshape(2, 64, 1024)
    d_tokens = jnp.stack(turn(d_tokens[0], d_tokens[1], odd))

    pre_self_grad = lax.dynamic_update_slice_in_dim(
        jnp.zeros(prefix_self.shape, f32), gpre_self[:, :count], group * 256, 2
    )
    totals = lax.psum(
        (pre_self_grad, gpre_cross[:, :count], gadt, gadb[0], gau, gaub[0]), ("row", "seq")
    )
    return (mixed, d_tokens, d_memory, totals[0], totals[1], totals[2].T, *totals[3:])


def solution(mesh):
    in_specs = (
        P("row", "seq", None),
        P("row", "seq", None),
        P("row"),
        P(),
        P(),
        P(),
        P("row", None),
        P(None, "row", None),
        P("row", None),
        P("row", None),
        P(None, "row", None),
        P("row", None),
        P("row", None),
        P("row", None),
        P(),
        P(),
        P(),
        P(),
        P(),
        P(),
        P("row", "seq", None),
    )
    out_specs = (
        P("row", "seq", None),
        P("row", "seq", None),
        P("row", "seq", None),
        P(),
        P(),
        P(),
        P(),
        P(),
        P(),
    )
    local = local_pairs if (mesh.shape["row"], mesh.shape["seq"]) == (4, 8) else local_rows
    return jax.shard_map(local, mesh=mesh, in_specs=in_specs, out_specs=out_specs, check_vma=False)
```

```python
import functools

import jax
import jax.numpy as jnp
from jax import lax
from jax.experimental import pallas as pl
from jax.experimental.pallas import tpu as pltpu
from jax.sharding import PartitionSpec as P

H = 16
HD = 64


EPSILON = 1e-05
MASKED = -1e30


def normalize(value, gain, shift):
    centre = value - jnp.mean(value, axis=-1, keepdims=True)
    inv_dev = lax.rsqrt(jnp.mean(centre * centre, axis=-1, keepdims=True) + EPSILON)
    unit_val = centre * inv_dev
    return (unit_val * gain + shift, unit_val, inv_dev)


def normalize_back(grad, unit_val, inv_dev, gain):
    scaled = grad * gain
    return inv_dev * (
        scaled
        - jnp.mean(scaled, axis=-1, keepdims=True)
        - unit_val * jnp.mean(scaled * unit_val, axis=-1, keepdims=True)
    )


def gelu_exact(value):
    return jax.nn.gelu(value, approximate=False)


def gelu_back(value, grad):
    return jax.vjp(gelu_exact, value)[1](grad)[0]


def head_split(matrix):
    return matrix.reshape(matrix.shape[0], -1, HD)


def masked_scores(queries, keys, mask):
    scores = jnp.einsum(
        "qhd,khd->hqk", head_split(queries), head_split(keys), preferred_element_type=jnp.float32
    )
    return jnp.where(mask[None], scores, MASKED)


def attend(queries, keys, values, mask):
    scores = masked_scores(queries, keys, mask)
    top_score = jnp.max(scores, axis=-1, keepdims=True)
    log_total = top_score + jnp.log(jnp.sum(jnp.exp(scores - top_score), axis=-1, keepdims=True))
    probs = jnp.exp(scores - log_total).astype(jnp.bfloat16)
    result = jnp.einsum(
        "hqk,khd->qhd", probs, head_split(values), preferred_element_type=jnp.float32
    )
    return (result.reshape(queries.shape[0], -1), log_total)


def attend_back(queries, keys, values, mask, log_total, grad_out):
    probs = jnp.exp(masked_scores(queries, keys, mask) - log_total)
    grad_heads = head_split(grad_out)
    grad_probs = jnp.einsum(
        "qhd,khd->hqk", grad_heads, head_split(values), preferred_element_type=jnp.float32
    )
    row_delta = jnp.sum(probs * grad_probs, axis=-1, keepdims=True)
    grad_scores = (probs * (grad_probs - row_delta)).astype(jnp.bfloat16)
    grad_query = jnp.einsum(
        "hqk,khd->qhd", grad_scores, head_split(keys), preferred_element_type=jnp.float32
    )
    grad_keys = jnp.einsum(
        "hqk,qhd->khd", grad_scores, head_split(queries), preferred_element_type=jnp.float32
    )
    grad_values = jnp.einsum(
        "hqk,qhd->khd", probs.astype(jnp.bfloat16), grad_heads, preferred_element_type=jnp.float32
    )
    return (
        grad_query.reshape(queries.shape[0], -1),
        grad_keys.reshape(keys.shape[0], -1),
        grad_values.reshape(values.shape[0], -1),
    )


def project(left, right):
    return jnp.dot(left, right, preferred_element_type=jnp.float32)


def local_rows(
    tokens,
    memory,
    source_len,
    bucket_order,
    prefix_self,
    prefix_cross,
    self_query,
    self_kv,
    self_out,
    cross_query,
    cross_kv,
    cross_out,
    fc_in,
    fc_out,
    ln_gain,
    ln_bias,
    ad_down,
    ad_down_bias,
    ad_up,
    ad_up_bias,
    cotangent,
):
    low_type = jnp.bfloat16
    row_count, tok_count, width = tokens.shape
    slot_count = memory.shape[1]
    prefix_count = prefix_self.shape[1]
    half_len = tok_count // 2
    scale = HD ** (-0.5)
    weight_set = (
        lax.all_gather(self_query.astype(low_type), "row", axis=0, tiled=True),
        lax.all_gather(self_kv.astype(low_type), "row", axis=1, tiled=True),
        lax.all_gather(self_out.astype(low_type), "row", axis=0, tiled=True),
        lax.all_gather(cross_query.astype(low_type), "row", axis=0, tiled=True),
        lax.all_gather(cross_kv.astype(low_type), "row", axis=1, tiled=True),
        lax.all_gather(cross_out.astype(low_type), "row", axis=0, tiled=True),
        lax.all_gather(fc_in.astype(low_type), "row", axis=0, tiled=True),
        lax.all_gather(fc_out.astype(low_type), "row", axis=0, tiled=True),
    )
    q_weight, kv_weight, o_weight, cq_weight, ckv_weight, co_weight, in_weight, out_weight = (
        weight_set
    )
    place = lax.axis_index("seq")
    offsets = jnp.arange(half_len, dtype=jnp.int32)
    all_pos = (bucket_order[:, None] * half_len + offsets[None, :]).reshape(-1)
    own_pos = lax.dynamic_slice_in_dim(all_pos, place * tok_count, tok_count)
    self_mask = jnp.concatenate(
        [jnp.ones((tok_count, prefix_count), jnp.bool_), all_pos[None, :] <= own_pos[:, None]],
        axis=1,
    )
    flat_tokens = tokens.reshape(-1, width)
    queries = (project(flat_tokens, q_weight) * scale).astype(low_type)
    own_keys = (
        project(flat_tokens, kv_weight[0]).astype(low_type).reshape(row_count, tok_count, width)
    )
    own_values = (
        project(flat_tokens, kv_weight[1]).astype(low_type).reshape(row_count, tok_count, width)
    )
    flat_memory = memory.reshape(-1, width)
    mem_keys = (
        project(flat_memory, ckv_weight[0]).astype(low_type).reshape(row_count, slot_count, width)
    )
    mem_values = (
        project(flat_memory, ckv_weight[1]).astype(low_type).reshape(row_count, slot_count, width)
    )
    all_keys, all_values, all_mkeys, all_mvalues = (
        lax.all_gather(own_keys, "seq", axis=1, tiled=True),
        lax.all_gather(own_values, "seq", axis=1, tiled=True),
        lax.all_gather(mem_keys, "seq", axis=1, tiled=True),
        lax.all_gather(mem_values, "seq", axis=1, tiled=True),
    )
    src_total = all_mkeys.shape[1]
    pre_self = prefix_self.astype(low_type)
    pre_cross = prefix_cross.astype(low_type)
    self_key_sets = [
        jnp.concatenate([pre_self[0], all_keys[row_index]], 0) for row_index in range(row_count)
    ]
    self_value_sets = [
        jnp.concatenate([pre_self[1], all_values[row_index]], 0) for row_index in range(row_count)
    ]
    cross_key_sets = [
        jnp.concatenate([pre_cross[0], all_mkeys[row_index]], 0) for row_index in range(row_count)
    ]
    cross_value_sets = [
        jnp.concatenate([pre_cross[1], all_mvalues[row_index]], 0) for row_index in range(row_count)
    ]
    slot_number = jnp.arange(src_total, dtype=jnp.int32)
    cross_masks = [
        jnp.concatenate(
            [jnp.ones((prefix_count,), jnp.bool_), slot_number < source_len[row_index]]
        )[None, :]
        for row_index in range(row_count)
    ]

    def rows_of(matrix, row_index):
        return matrix[row_index * tok_count : (row_index + 1) * tok_count]

    self_parts = [
        attend(
            rows_of(queries, row_index),
            self_key_sets[row_index],
            self_value_sets[row_index],
            self_mask,
        )
        for row_index in range(row_count)
    ]
    attended = jnp.concatenate([part[0] for part in self_parts], 0).astype(low_type)
    resid_one = flat_tokens.astype(jnp.float32) + project(attended, o_weight)
    hidden_one, unit_one, inv_one = normalize(resid_one, ln_gain[0], ln_bias[0])
    cross_queries = (project(hidden_one.astype(low_type), cq_weight) * scale).astype(low_type)
    cross_parts = [
        attend(
            rows_of(cross_queries, row_index),
            cross_key_sets[row_index],
            cross_value_sets[row_index],
            cross_masks[row_index],
        )
        for row_index in range(row_count)
    ]
    cross_att = jnp.concatenate([part[0] for part in cross_parts], 0).astype(low_type)
    resid_two = hidden_one + project(cross_att, co_weight)
    hidden_two, unit_two, inv_two = normalize(resid_two, ln_gain[1], ln_bias[1])
    hidden_low = hidden_two.astype(low_type)
    up_proj = project(hidden_low, in_weight)
    activated = gelu_exact(up_proj).astype(low_type)
    ffn_out = project(activated, out_weight)
    down_weight = ad_down.astype(low_type)
    up_weight = ad_up.astype(low_type)
    down_proj = project(hidden_low, down_weight) + ad_down_bias
    down_act = gelu_exact(down_proj).astype(low_type)
    adapted = project(down_act, up_weight) + ad_up_bias
    resid_three = hidden_two + ffn_out + 4.0 * adapted
    output, unit_three, inv_three = normalize(resid_three, ln_gain[2], ln_bias[2])
    mixed = output.astype(low_type).reshape(row_count, tok_count, width)
    weight_set = (
        lax.all_gather(self_query.astype(low_type), "row", axis=0, tiled=True),
        lax.all_gather(self_kv.astype(low_type), "row", axis=1, tiled=True),
        lax.all_gather(self_out.astype(low_type), "row", axis=0, tiled=True),
        lax.all_gather(cross_query.astype(low_type), "row", axis=0, tiled=True),
        lax.all_gather(cross_kv.astype(low_type), "row", axis=1, tiled=True),
        lax.all_gather(cross_out.astype(low_type), "row", axis=0, tiled=True),
        lax.all_gather(fc_in.astype(low_type), "row", axis=0, tiled=True),
        lax.all_gather(fc_out.astype(low_type), "row", axis=0, tiled=True),
    )
    q_weight, kv_weight, o_weight, cq_weight, ckv_weight, co_weight, in_weight, out_weight = (
        weight_set
    )
    grad_out = cotangent.astype(jnp.float32).reshape(-1, width)
    grad_three = normalize_back(grad_out, unit_three, inv_three, ln_gain[2])
    grad_ffn = grad_three.astype(low_type)
    grad_adapt = (4.0 * grad_three).astype(low_type)
    grad_up_w = jnp.einsum("na,nd->ad", down_act, grad_adapt, preferred_element_type=jnp.float32)
    grad_up_b = jnp.sum(grad_adapt.astype(jnp.float32), axis=0)
    grad_down = gelu_back(down_proj, project(grad_adapt, up_weight.T)).astype(low_type)
    grad_down_w = jnp.einsum("nd,na->da", hidden_low, grad_down, preferred_element_type=jnp.float32)
    grad_down_b = jnp.sum(grad_down.astype(jnp.float32), axis=0)
    grad_inner = gelu_back(up_proj, project(grad_ffn, out_weight.T)).astype(low_type)
    grad_hidden_two = (
        grad_three + project(grad_inner, in_weight.T) + project(grad_down, down_weight.T)
    )
    grad_two = normalize_back(grad_hidden_two, unit_two, inv_two, ln_gain[1])
    grad_cross_att = project(grad_two.astype(low_type), co_weight.T).astype(low_type)
    cross_grads = [
        attend_back(
            rows_of(cross_queries, row_index),
            cross_key_sets[row_index],
            cross_value_sets[row_index],
            cross_masks[row_index],
            cross_parts[row_index][1],
            rows_of(grad_cross_att, row_index),
        )
        for row_index in range(row_count)
    ]
    grad_cq = jnp.concatenate([part[0] for part in cross_grads], 0).astype(low_type)
    grad_hidden_one = grad_two + project(grad_cq, cq_weight.T) * scale
    grad_one = normalize_back(grad_hidden_one, unit_one, inv_one, ln_gain[0])
    grad_attended = project(grad_one.astype(low_type), o_weight.T).astype(low_type)
    self_grads = [
        attend_back(
            rows_of(queries, row_index),
            self_key_sets[row_index],
            self_value_sets[row_index],
            self_mask,
            self_parts[row_index][1],
            rows_of(grad_attended, row_index),
        )
        for row_index in range(row_count)
    ]
    pre_self_grad = jnp.stack(
        [
            sum((part[1][:prefix_count] for part in self_grads)),
            sum((part[2][:prefix_count] for part in self_grads)),
        ]
    )
    pre_cross_grad = jnp.stack(
        [
            sum((part[1][:prefix_count] for part in cross_grads)),
            sum((part[2][:prefix_count] for part in cross_grads)),
        ]
    )
    summed = [
        (
            lax.psum_scatter(
                self_grads[row_index][1][prefix_count:].astype(jnp.bfloat16),
                "seq",
                scatter_dimension=0,
                tiled=True,
            ).astype(jnp.float32),
            lax.psum_scatter(
                self_grads[row_index][2][prefix_count:].astype(jnp.bfloat16),
                "seq",
                scatter_dimension=0,
                tiled=True,
            ).astype(jnp.float32),
            lax.psum_scatter(
                cross_grads[row_index][1][prefix_count:].astype(jnp.bfloat16),
                "seq",
                scatter_dimension=0,
                tiled=True,
            ).astype(jnp.float32),
            lax.psum_scatter(
                cross_grads[row_index][2][prefix_count:].astype(jnp.bfloat16),
                "seq",
                scatter_dimension=0,
                tiled=True,
            ).astype(jnp.float32),
        )
        for row_index in range(row_count)
    ]
    key_grad = jnp.stack([part[0] for part in summed])
    value_grad = jnp.stack([part[1] for part in summed])
    mkey_grad = jnp.stack([part[2] for part in summed])
    mvalue_grad = jnp.stack([part[3] for part in summed])
    grad_query = jnp.concatenate([part[0] for part in self_grads], 0).astype(low_type)
    d_tokens = (
        grad_one
        + project(grad_query, q_weight.T) * scale
        + project(key_grad.astype(low_type).reshape(-1, width), kv_weight[0].T)
        + project(value_grad.astype(low_type).reshape(-1, width), kv_weight[1].T)
    )
    d_memory = project(mkey_grad.astype(low_type).reshape(-1, width), ckv_weight[0].T) + project(
        mvalue_grad.astype(low_type).reshape(-1, width), ckv_weight[1].T
    )
    totals = lax.psum(
        (pre_self_grad, pre_cross_grad, grad_down_w, grad_down_b, grad_up_w, grad_up_b),
        ("row", "seq"),
    )
    return (
        mixed,
        d_tokens.astype(low_type).reshape(row_count, tok_count, width),
        d_memory.astype(low_type).reshape(row_count, slot_count, width),
        totals[0],
        totals[1],
        totals[2],
        totals[3],
        totals[4],
        totals[5],
    )


LOW = jnp.bfloat16
F32 = jnp.float32
SCALE = 0.125
VMEM = pl.BlockSpec(memory_space=pltpu.VMEM)
SMEM = pl.BlockSpec(memory_space=pltpu.SMEM)
HBM = pl.BlockSpec(memory_space=pltpu.HBM)


def shape_of(shape, dtype=LOW):
    return jax.ShapeDtypeStruct(shape, dtype)


def nn(left, right):
    return jnp.dot(left, right, preferred_element_type=F32)


def nt(left, right):
    return lax.dot_general(left, right, (((1,), (1,)), ((), ())), preferred_element_type=F32)


def tn(left, right):
    return lax.dot_general(left, right, (((0,), (0,)), ((), ())), preferred_element_type=F32)


def cols(start, size):
    return pl.ds(pl.multiple_of(start, 128), size)


def ln(value, gain, shift):
    centre = value - jnp.mean(value, axis=-1, keepdims=True)
    inv = lax.rsqrt(jnp.mean(centre * centre, axis=-1, keepdims=True) + EPSILON)
    unit = centre * inv
    return unit * gain + shift, unit, inv


def ln_back(grad, unit, inv, gain):
    scaled = grad * gain
    return inv * (
        scaled
        - jnp.mean(scaled, axis=-1, keepdims=True)
        - unit * jnp.mean(scaled * unit, axis=-1, keepdims=True)
    )


def gelu_both(value):
    cdf = 0.5 * (1.0 + lax.erf(value * 0.7071067811865476))
    return value * cdf, cdf + value * (jnp.exp(-0.5 * value * value) * 0.3989422804014327)


def stacked(block):
    first = lax.broadcasted_iota(jnp.int32, block.shape, 1) < 64
    zero = jnp.zeros_like(block)
    return jnp.concatenate([jnp.where(first, block, zero), jnp.where(first, zero, block)], 0)


def unstacked(both, n):
    return jnp.concatenate([both[:64, :n], both[64:, n:]], 0).T


def pre_mask(shape, count):
    return lax.broadcasted_iota(jnp.int32, shape, 0) < count


def soft_pair(qs, k_pre, k_blocks, v_pre, vt_blocks, biases, count):
    s_pre = nt(k_pre, qs)
    s_pre = jnp.where(pre_mask(s_pre.shape, count), s_pre, MASKED)
    s_blocks = [nt(k, qs) + b for k, b in zip(k_blocks, biases)]
    top = jnp.max(s_pre, axis=0, keepdims=True)
    for s in s_blocks:
        top = jnp.maximum(top, jnp.max(s, axis=0, keepdims=True))
    e_pre = jnp.exp(s_pre - top)
    total = jnp.sum(e_pre, axis=0, keepdims=True)
    out = tn(v_pre, e_pre.astype(LOW))
    for s, vt in zip(s_blocks, vt_blocks):
        e = jnp.exp(s - top)
        total += jnp.sum(e, axis=0, keepdims=True)
        out += nn(vt, e.astype(LOW))
    return out * (1.0 / total), top + jnp.log(total)


def soft_pair_back(qs, dos, lse, k_pre, v_pre, ks, vs, kts, biases, count):
    s_pre = nt(k_pre, qs)
    p_pre = jnp.where(pre_mask(s_pre.shape, count), jnp.exp(s_pre - lse), 0.0)
    d_pre = nt(v_pre, dos)
    delta = jnp.sum(p_pre * d_pre, axis=0, keepdims=True)
    ps, ds = [], []
    for k, v, b in zip(ks, vs, biases):
        p = jnp.exp(nt(k, qs) + b - lse)
        d = nt(v, dos)
        delta += jnp.sum(p * d, axis=0, keepdims=True)
        ps.append(p)
        ds.append(d)
    g_pre = (p_pre * (d_pre - delta)).astype(LOW)
    dq = tn(k_pre, g_pre)
    dk, dv = [nn(g_pre, qs)], [nn(p_pre.astype(LOW), dos)]
    for p, d, kt in zip(ps, ds, kts):
        g = (p * (d - delta)).astype(LOW)
        dq += nn(kt, g)
        dk.append(nn(g, qs))
        dv.append(nn(p.astype(LOW), dos))
    return dq, dk, dv


COSTS = {
    "pack_heads": 1.5,
    "pack": 5.0,
    "self_fwd": 5.0,
    "mem_fwd": 2.3,
    "mid_fwd": 10.0,
    "mlp": 20.0,
    "cross_bwd": 11.0,
    "query_bwd": 3.0,
    "self_bwd": 6.5,
    "mem_back": 2.5,
    "totals": 3.0,
}
LIMITS = {
    "pack_heads": 60,
    "inbound": 20,
    "tokens": 4,
    "pack": 60,
    "self_fwd": 14,
    "self_bwd": 18,
    "mem_fwd": 14,
    "mem_back": 14,
    "mid_fwd": 24,
    "mlp": 60,
    "cross_bwd": 60,
    "query_bwd": 12,
    "halve": 6,
    "join": 8,
    "totals": 20,
    "mix": 4,
}


def call(kernel, name, ins, outs, scratch=()):
    flops = int(COSTS.get(name, 0.8) * 0.3e9)
    return pl.pallas_call(
        kernel,
        cost_estimate=pl.CostEstimate(flops=flops, bytes_accessed=1000, transcendentals=0),
        in_specs=ins,
        out_specs=[o[0] for o in outs],
        out_shape=[o[1] for o in outs],
        scratch_shapes=list(scratch),
        compiler_params=pltpu.CompilerParams(vmem_limit_bytes=LIMITS[name] * 2**20),
        name=name,
    )


def out(shape, dtype=LOW, space=VMEM):
    return space, jax.ShapeDtypeStruct(shape, dtype)


def inbound_kernel(ids, tokens, memory, first, second, sems):
    copies = []
    for n, dst in enumerate((first, second)):
        row = ids[12] if n == 0 else 1 - ids[12]
        for m, (src, start, size) in enumerate(((tokens, 0, 64), (memory, 64, 128))):
            copies.append(pltpu.make_async_copy(src.at[row], dst.at[pl.ds(start, size)], sems.at[n, m]))
    for copy in copies:
        copy.start()
    for copy in copies:
        copy.wait()


def inbound(ids, tokens, memory):
    return call(
        inbound_kernel,
        "inbound",
        [SMEM, HBM, HBM],
        [out((192, 1024)), out((192, 1024))],
        [pltpu.SemaphoreType.DMA((2, 2))],
    )(ids, tokens, memory)


def tokens_kernel(first, second, dst, sems):
    copies = [
        pltpu.make_async_copy(src.at[pl.ds(0, 64)], dst.at[pl.ds(64 * n, 64)], sems.at[n])
        for n, src in enumerate((first, second))
    ]
    for copy in copies:
        copy.start()
    for copy in copies:
        copy.wait()


def pack_first_kernel(ids, query, kv, ckv, dst, wide, sems):
    copies = [pltpu.make_async_copy(ckv.at[n], wide.at[pl.ds(256 * n, 256)], sems.at[n]) for n in range(2)]
    for n in range(2):
        group = cols(ids[13 + 2 * n] * 256, 256)
        for j, src in enumerate((query, kv.at[0])):
            copies.append(
                pltpu.make_async_copy(
                    src.at[:, group],
                    wide.at[pl.ds(512, 256), pl.ds(512 * n + 256 * j, 256)],
                    sems.at[2 + 4 * n + j],
                )
            )
        for j in range(2):
            copies.append(
                pltpu.make_async_copy(
                    kv.at[1, pl.ds(128 * j, 128), group],
                    wide.at[pl.ds(768, 128), pl.ds(512 * j + 256 * n, 256)],
                    sems.at[4 + 4 * n + j],
                )
            )
    for copy in copies:
        copy.start()
    for copy in copies:
        copy.wait()
    dst[...] = wide[...].astype(LOW)


def pack_first(ids, query, kv, ckv):
    return call(
        pack_first_kernel,
        "pack_heads",
        [SMEM, HBM, HBM, HBM],
        [out((896, 1024))],
        [pltpu.VMEM((896, 1024), F32), pltpu.SemaphoreType.DMA((10,))],
    )(ids, query, kv, ckv)[0]


def head_weights(parts):
    for n, part in enumerate(parts):
        g = n % 2
        yield (
            part[512:768, 512 * g : 512 * g + 256],
            part[512:768, 512 * g + 256 : 512 * g + 512],
            part[768:, 256 * g : 256 * g + 256],
            part[768:, 512 + 256 * g : 768 + 256 * g],
        )


def pack_kernel(sources, n_args, ids, *refs):
    args, refs = refs[:n_args], refs[n_args:]
    outs, (wide, narrow, in_sem, own_sem, part_sem) = refs[:-5], refs[-5:]
    count = len(sources)

    def fetch(m):
        arg, lead, row, col, kept_in = sources[m][:5]
        src = args[arg] if lead is None else args[arg].at[lead]
        start, size = row, 256
        if kept_in is None:
            start, size = pl.multiple_of(row + ids[sources[m][-1]] * 128, 128), 128
        return pltpu.make_async_copy(
            src.at[pl.ds(start, size), pl.ds(col, 1024)], wide.at[m, pl.ds(0, size)], in_sem.at[m]
        )

    def store(m):
        kept_in, kept_at, number, index, bit = sources[m][4:]
        kept = narrow.at[m]
        half = kept
        if kept_in is None:
            half = kept.at[pl.ds(0, 128)]
        elif bit is not None:
            half = kept.at[pl.ds(pl.multiple_of(ids[bit] * 128, 128), 128)]
        part = pltpu.make_async_copy(half, outs[number].at[index], part_sem.at[m])
        if kept_in is None:
            return (part,)
        return pltpu.make_async_copy(kept, outs[kept_in].at[kept_at], own_sem.at[m]), part

    for m in range(count):
        fetch(m).start()
    for m in range(count):
        fetch(m).wait()
        narrow[m] = wide[m].astype(LOW)
        for copy in store(m):
            copy.start()
    for m in range(count):
        for copy in store(m):
            copy.wait()


def pack(ids, sources, shapes, *args):
    return call(
        functools.partial(pack_kernel, sources, len(args)),
        "pack",
        [SMEM] + [HBM] * len(args),
        [out(shape, LOW, HBM) for shape in shapes],
        [
            pltpu.VMEM((len(sources), 256, 1024), F32),
            pltpu.VMEM((len(sources), 256, 1024), LOW),
            pltpu.SemaphoreType.DMA((len(sources),)),
            pltpu.SemaphoreType.DMA((len(sources),)),
            pltpu.SemaphoreType.DMA((len(sources),)),
        ],
    )(ids, *args)


PLACES = {
    "own": (lambda ids: ids[4], 256),
    "core": (lambda ids: ids[5], 256),
    "near": (lambda ids: ids[6], 128),
    "other": (lambda ids: ids[7], 128),
    "core_near": (lambda ids: ids[8], 128),
    "core_other": (lambda ids: ids[9], 128),
    "near_y": (lambda ids: ids[21], 128),
    "other_y": (lambda ids: ids[22], 128),
    "core_near_y": (lambda ids: ids[23], 128),
    "core_other_y": (lambda ids: ids[24], 128),
    "far": (lambda ids: 2 * ids[2], 256),
    "core_far": (lambda ids: 2 * ids[3], 256),
}
DIRECT = ("own", "core", "far", "core_far")
SHARED = ("own", "core", "near", "other", "core_near", "core_other")


def shared(index, first):
    return [(n, index + first if n < 2 else index, place) for n, place in enumerate(SHARED)]


def direct(index):
    return [(n, index, place) for n, place in enumerate(DIRECT)]


def place_of(ids, place):
    first, size = PLACES[place]
    return cols(first(ids) * 128, size)


def mm(x_ref, refs, matrix, ids):
    acc = None
    for n, index, place in matrix:
        term = nn(x_ref[:, place_of(ids, place)], refs[n][index])
        acc = term if acc is None else acc + term
    return acc


def mm_back(value, refs, matrix, ids, out_ref):
    for n, index, place in matrix:
        out_ref[:, place_of(ids, place)] = nt(value, refs[n][index])


class Fetch:
    def __init__(self, sources, targets, sems, matrices, first=0):
        self.copies, number = [], 0
        for matrix in matrices:
            mine = []
            for n, index, _ in matrix:
                to = index - first if n < 2 else index
                mine.append(pltpu.make_async_copy(sources[n].at[index], targets[n].at[to], sems.at[number]))
                number += 1
            self.copies.append(mine)

    def start(self, m):
        for copy in self.copies[m]:
            copy.start()

    def wait(self, m):
        for copy in self.copies[m]:
            copy.wait()


def fill_prefix(pre, wide, narrow, count, where=None):
    wide[...] = jnp.zeros_like(wide)
    wide[:, :count, :] = pre[...] if where is None else pre[:, :, where]
    narrow[...] = wide[...].astype(LOW)


def fill_places(order, ids, kpos, qpos):
    c, y, odd = ids[10], ids[11], ids[12]
    lane = lax.broadcasted_iota(jnp.int32, (1, 512), 1)
    column = jnp.zeros((1, 512), jnp.int32)
    for n in range(16):
        core = c if n < 8 else 1 - c
        line = y if n % 8 < 4 else 1 - y
        turned = odd if n % 4 < 2 else 1 - odd
        bucket = 2 * (2 * (2 * core + turned) + line) + n % 2
        first = order[bucket] * 32
        kpos[n * 32 : (n + 1) * 32, :] = lax.broadcasted_iota(jnp.int32, (32, 1), 0) + first
        column = jnp.where(lane // 32 == n, first + lane % 32, column)
    qpos[...] = column


def self_bias(kpos, qpos, t):
    seen = kpos[...] <= qpos[:, t * 128 : (t + 1) * 128]
    bias = jnp.where(seen, 0.0, MASKED)
    return jnp.concatenate([bias, bias], 1)


def self_fwd_kernel(
    count, ids, order, t0, t1, t2, t3, w0, w1, w2, w3, pre, q_ref, k_ref, v_ref,
    o0, o1, o2, o3, lse_ref, vt, kpos, qpos, wide, pre_l
):
    fill_places(order, ids, kpos, qpos)
    fill_prefix(pre, wide, pre_l, count, cols(ids[13] * 256, 256))
    for t, tok in enumerate((t0, t1, t2, t3)):
        rows = slice(t * 128, (t + 1) * 128)
        acc = [0.0, 0.0, 0.0]
        for n, (wq, wk, wv, wv2) in enumerate(head_weights((w0, w1, w2, w3))):
            some = tok[:, cols(ids[n] * 256, 256)]
            acc[0] += nn(some, wq)
            acc[1] += nn(some, wk)
            acc[2] += nn(some[:, :128], wv) + nn(some[:, 128:], wv2)
        q_ref[rows, :] = (acc[0] * SCALE).astype(LOW)
        k_ref[rows, :] = acc[1].astype(LOW)
        v_ref[rows, :] = acc[2].astype(LOW)
    vt[...] = v_ref[...].T
    for t in (3, 1, 2, 0):
        bias = self_bias(kpos, qpos, t)
        for p in range(2):
            lanes = slice(p * 128, (p + 1) * 128)
            qs = stacked(q_ref[t * 128 : (t + 1) * 128, lanes])
            got, lse = soft_pair(
                qs, pre_l[0, :, lanes], [k_ref[:, lanes]], pre_l[1, :, lanes], [vt[lanes, :]], [bias], count
            )
            (o0, o1, o2, o3)[t][:, lanes] = unstacked(got, 128).astype(LOW)
            lse_ref[p, t] = lse


def self_fwd(ids, order, toks, ws, pre, count):
    return call(
        functools.partial(self_fwd_kernel, count),
        "self_fwd",
        [SMEM, SMEM] + [VMEM] * 9,
        [
            out((512, 256)),
            out((512, 256)),
            out((512, 256)),
            out((128, 256)),
            out((128, 256)),
            out((128, 256)),
            out((128, 256)),
            out((2, 4, 1, 256), F32),
        ],
        [
            pltpu.VMEM((256, 512), LOW),
            pltpu.VMEM((512, 1), jnp.int32),
            pltpu.VMEM((1, 512), jnp.int32),
            pltpu.VMEM((2, 32, 256), F32),
            pltpu.VMEM((2, 32, 256), LOW),
        ],
    )(ids, order, *toks, *ws, pre)


def self_bwd_kernel(
    count, ids, order, q, k, v, d0, d1, d2, d3, g0, lse_ref, w0, w1, w2, w3, pre,
    near_ref, far_ref, sums_ref, kt, dq, dk, dv, gpre_ref, kpos, qpos, wide, pre_l
):
    fill_places(order, ids, kpos, qpos)
    fill_prefix(pre, wide, pre_l, count, cols(ids[13] * 256, 256))
    kt[...] = k[...].T
    grads = (d0, d1, d2, d3)
    for t in range(4):
        bias = self_bias(kpos, qpos, t)
        for p in range(2):
            lanes = slice(p * 128, (p + 1) * 128)
            qs = stacked(q[t * 128 : (t + 1) * 128, lanes])
            dos = stacked(grads[t][:128, lanes])
            g, gk, gv = soft_pair_back(
                qs,
                dos,
                lse_ref[p, t],
                pre_l[0, :, lanes],
                pre_l[1, :, lanes],
                [k[:, lanes]],
                [v[:, lanes]],
                [kt[lanes, :]],
                [bias],
                count,
            )
            dq[t * 128 : (t + 1) * 128, lanes] = unstacked(g, 128).astype(LOW)
            if t == 0:
                gpre_ref[:32, lanes] = gk[0]
                gpre_ref[32:, lanes] = gv[0]
                dk[:, lanes] = gk[1]
                dv[:, lanes] = gv[1]
            else:
                gpre_ref[:32, lanes] += gk[0]
                gpre_ref[32:, lanes] += gv[0]
                dk[:, lanes] += gk[1]
                dv[:, lanes] += gv[1]
    cross = g0[...] + d1[128:].astype(F32) + d2[128:].astype(F32) + d3[128:].astype(F32)
    for n, rows in enumerate((gpre_ref[:32], gpre_ref[32:], cross[:32], cross[32:])):
        sums_ref[:, 256 * n : 256 * (n + 1)] = rows.astype(LOW)
    dkl, dvl = dk[...].astype(LOW), dv[...].astype(LOW)
    for n, (wq, wk, wv, wv2) in enumerate(head_weights((w0, w1, w2, w3))):
        part = jnp.concatenate([nt(dvl, wv), nt(dvl, wv2)], 1)
        part = (part + nt(dq[...], wq) * SCALE + nt(dkl, wk)).astype(LOW)
        near_ref[:, cols(ids[n] * 256, 256)] = part[:256]
        far_ref[:, cols(ids[n] * 256, 256)] = part[256:]


def self_bwd(ids, order, q, k, v, grads, g0, lse, ws, pre, count):
    return call(
        functools.partial(self_bwd_kernel, count),
        "self_bwd",
        [SMEM, SMEM] + [VMEM] * 14,
        [out((256, 1024)), out((256, 1024)), out((32, 1024))],
        [
            pltpu.VMEM((256, 512), LOW),
            pltpu.VMEM((512, 256), LOW),
            pltpu.VMEM((512, 256), F32),
            pltpu.VMEM((512, 256), F32),
            pltpu.VMEM((64, 256), F32),
            pltpu.VMEM((512, 1), jnp.int32),
            pltpu.VMEM((1, 512), jnp.int32),
            pltpu.VMEM((2, 32, 256), F32),
            pltpu.VMEM((2, 32, 256), LOW),
        ],
    )(ids, order, q, k, v, *grads, g0, lse, *ws, pre)


def memory_fetch(parts, bufs, sems):
    copies = [
        [
            pltpu.make_async_copy(p.at[pl.ds(256 * j, 256)], b.at[j], sems.at[4 * j + n])
            for n, (p, b) in enumerate(zip(parts, bufs))
        ]
        for j in range(2)
    ]
    for copy in copies[0] + copies[1]:
        copy.start()
    return copies


def mem_kernel(ids, m0, m1, *refs):
    parts, res, bufs, sems = refs[:4], refs[4], refs[5:9], refs[9]
    copies = memory_fetch(parts, bufs, sems)
    for j in range(2):
        for copy in copies[j]:
            copy.wait()
        for n, mem in enumerate((m0.at[pl.ds(64, 128)], m1.at[pl.ds(64, 128)])):
            res[j, n * 128 : (n + 1) * 128, :] = mm(mem, bufs, direct(j), ids).astype(LOW)


def mem_fwd(ids, m0, m1, parts):
    return call(
        mem_kernel,
        "mem_fwd",
        [SMEM] + [VMEM] * 2 + [HBM] * 4,
        [out((2, 256, 1024))],
        [pltpu.VMEM((2, 256, 1024), LOW) for p in parts] + [pltpu.SemaphoreType.DMA((8,))],
    )(ids, m0, m1, *parts)[0]


def mem_back_kernel(ids, near, far_c, far_k, far_v, *refs):
    parts, (r0, r1), bufs, (wide, sems) = refs[:4], refs[4:6], refs[6:10], refs[10:]
    copies = memory_fetch(parts, bufs, sems)
    total = [
        (near[j].astype(F32) + far_c[j].astype(F32) + far_y[...].astype(F32)).astype(LOW)
        for j, far_y in enumerate((far_k, far_v))
    ]
    for copy in copies[0] + copies[1]:
        copy.wait()
    for n, place in enumerate(DIRECT):
        wide[:, place_of(ids, place)] = nt(total[0], bufs[n][0]) + nt(total[1], bufs[n][1])
    r0[...] = wide[:128].astype(LOW)
    r1[...] = wide[128:].astype(LOW)


def mem_back(ids, near, far_c, far_k, far_v, parts):
    return call(
        mem_back_kernel,
        "mem_back",
        [SMEM] + [VMEM] * 4 + [HBM] * 4,
        [out((128, 1024)), out((128, 1024))],
        [pltpu.VMEM((2, 256, 1024), LOW) for p in parts]
        + [pltpu.VMEM((256, 1024), F32), pltpu.SemaphoreType.DMA((8,))],
    )(ids, near, far_c, far_k, far_v, *parts)


def fill_bias(bias, ids, live):
    c, y, odd = ids[10], ids[11], ids[12]
    for n in range(8):
        core = c if n < 4 else 1 - c
        line = y if n % 4 < 2 else 1 - y
        turned = odd if n % 2 == 0 else 1 - odd
        first = (2 * (2 * core + turned) + line) * 128
        slot = lax.broadcasted_iota(jnp.int32, (128, 256), 0) + first
        bias[n * 128 : (n + 1) * 128, :] = jnp.where(slot < live[0, 0], 0.0, MASKED)


def mid_fwd_kernel(count, ids, live, o0, o1, o2, o3, tok, gain, shift, pre, *refs):
    kvs, parts, refs = refs[:4], refs[4:10], refs[10:]
    cq_ref, lse_ref, unit1, inv1, h2_ref, unit2, inv2, h2l = refs[:8]
    kv, bufs, (bias, flat, wide, pre_l, sems, kv_sems) = refs[8:12], refs[12:18], refs[18:]
    fetch = Fetch(parts, bufs, sems, [shared(j, 0) for j in range(3)])
    loads = [
        pltpu.make_async_copy(kvs[n].at[j], kv[n].at[j], kv_sems.at[n, j]) for j in range(2) for n in range(4)
    ]
    fetch.start(0)
    fetch.start(1)
    for copy in loads:
        copy.start()
    fetch.start(2)
    for n, o in enumerate((o0, o1, o2, o3)):
        flat[:, cols(ids[13 + n] * 256, 256)] = o[...]
    fill_bias(bias, ids, live)
    fill_prefix(pre, wide, pre_l, count)
    fetch.wait(0)
    h1, unit, inv = ln(
        tok[...].astype(F32) + mm(flat, bufs, shared(0, 0), ids), gain[0:1], shift[0:1]
    )
    unit1[...] = unit
    inv1[...] = inv
    flat[...] = h1.astype(LOW)
    fetch.wait(1)
    cq_ref[...] = (mm(flat, bufs, shared(1, 0), ids) * SCALE).astype(LOW)
    for copy in loads:
        copy.wait()
    for p in range(8):
        lanes = slice(p * 128, (p + 1) * 128)
        got, lse = soft_pair(
            stacked(cq_ref[:, lanes]),
            pre_l[0, :, lanes],
            [kv[n][0, :, lanes] for n in range(4)],
            pre_l[1, :, lanes],
            [kv[n][1, :, lanes].T for n in range(4)],
            [bias[n * 256 : (n + 1) * 256] for n in range(4)],
            count,
        )
        flat[:, lanes] = unstacked(got, 128).astype(LOW)
        lse_ref[p] = lse
    fetch.wait(2)
    h2, unit, inv = ln(h1 + mm(flat, bufs, shared(2, 0), ids), gain[1:2], shift[1:2])
    h2_ref[...] = h2
    unit2[...] = unit
    inv2[...] = inv
    h2l[...] = h2.astype(LOW)


def mid_fwd(ids, live, os, tok, gain, shift, pre, kvs, parts, count):
    wide, thin = out((128, 1024), F32), out((128, 1), F32)
    return call(
        functools.partial(mid_fwd_kernel, count),
        "mid_fwd",
        [SMEM, SMEM] + [VMEM] * 8 + [HBM] * 10,
        [out((128, 1024)), out((8, 1, 256), F32), wide, thin, wide, wide, thin, out((128, 1024))],
        [pltpu.VMEM((2, 256, 1024), LOW)] * 4
        + [pltpu.VMEM((3, *p.shape[1:]), LOW) for p in parts]
        + [
            pltpu.VMEM((1024, 256), F32),
            pltpu.VMEM((128, 1024), LOW),
            pltpu.VMEM((2, 32, 1024), F32),
            pltpu.VMEM((2, 32, 1024), LOW),
            pltpu.SemaphoreType.DMA((18,)),
            pltpu.SemaphoreType.DMA((4, 2)),
        ],
    )(ids, live, *os, tok, gain, shift, pre, *kvs, *parts)


def mlp_kernel(matrices, ids, h2, h2l, unit2, inv2, c0, c1, gain, shift, down_b, up_b, down_any, up_any, *refs):
    count = 1 + max(n for matrix in matrices for n, _, _ in matrix)
    parts, refs = refs[:count], refs[count:]
    m0, m1, dr2, keep, give, gaub, gadb = refs[:7]
    bufs, (down, up, act, slope, acc, sems, ad_sems) = refs[7 : 7 + count], refs[7 + count :]
    fetch = Fetch(parts, bufs, sems, matrices)
    ad = [
        pltpu.make_async_copy(down_any, down, ad_sems.at[0]),
        pltpu.make_async_copy(up_any, up, ad_sems.at[1]),
    ]
    for s in range(4):
        fetch.start(s)
    for copy in ad:
        copy.start()
    for s in range(4, 8):
        fetch.start(s)
    for s in range(4):
        fetch.wait(s)
        value, gradient = gelu_both(mm(h2l, bufs, matrices[s], ids))
        lanes = slice(s * 1024, (s + 1) * 1024)
        act[:, lanes] = value.astype(LOW)
        slope[:, lanes] = gradient
    for copy in ad:
        copy.wait()
    down_w, up_w = down[...].astype(LOW), up[...].astype(LOW)
    a, a_slope = gelu_both(nn(h2l[...], down_w) + down_b[...])
    a = a.astype(LOW)
    total = h2[...] + 4.0 * (nn(a, up_w) + up_b[...])

    def rows(s, place):
        first, size = PLACES[place]
        first = first(ids)
        return cols((first // 2) * 1024 + s * 256 + (first % 2) * 128, size)

    for s in range(4):
        fetch.wait(4 + s)
        for n, index, place in matrices[4 + s]:
            total += nn(act[:, rows(s, place)], bufs[n][index])
    res, unit3, inv3 = ln(total, gain[2:3], shift[2:3])
    m0[...] = res[:64].astype(LOW)
    m1[...] = res[64:].astype(LOW)
    cot = jnp.concatenate([c0[...], c1[...]], 0).astype(F32)
    dr3 = ln_back(cot, unit3, inv3, gain[2:3])
    dffn = dr3.astype(LOW)
    dad = (4.0 * dr3).astype(LOW)
    gau = tn(a, dad)
    gaub[...] = jnp.sum(dad.astype(F32), axis=0, keepdims=True)
    ddn = (a_slope * nt(dad, up_w)).astype(LOW)
    gadb[:, :512] = jnp.sum(ddn.astype(F32), axis=0, keepdims=True)
    gadb[:, 512:] = jnp.zeros((1, 512), F32)
    gadt = tn(ddn, h2l[...])
    first_core = ids[10] == 0
    keep[...] = jnp.where(first_core, gau, gadt)
    give[...] = jnp.where(first_core, gadt, gau).astype(LOW)
    for s in range(4):
        for n, index, place in matrices[4 + s]:
            where = rows(s, place)
            act[:, where] = (slope[:, where] * nt(dffn, bufs[n][index])).astype(LOW)
    acc[...] = dr3 + nt(ddn, down_w)
    for s in range(4):
        for n, index, place in matrices[s]:
            acc[:, place_of(ids, place)] += nt(act[:, s * 1024 : (s + 1) * 1024], bufs[n][index])
    dr2[...] = ln_back(acc[...], unit2[...], inv2[...], gain[1:2])


def mlp(ids, h2, h2l, unit2, inv2, cots, gain, shift, down_b, up_b, down, up, parts, matrices):
    return call(
        functools.partial(mlp_kernel, matrices),
        "mlp",
        [SMEM] + [VMEM] * 10 + [HBM] * (2 + len(parts)),
        [
            out((64, 1024)),
            out((64, 1024)),
            out((128, 1024), F32),
            out((512, 1024), F32),
            out((512, 1024)),
            out((1, 1024), F32),
            out((1, 1024), F32),
        ],
        [pltpu.VMEM((8, *p.shape[1:]) if n < 2 else p.shape, LOW) for n, p in enumerate(parts)]
        + [
            pltpu.VMEM((1024, 512), F32),
            pltpu.VMEM((512, 1024), F32),
            pltpu.VMEM((128, 4096), LOW),
            pltpu.VMEM((128, 4096), F32),
            pltpu.VMEM((128, 1024), F32),
            pltpu.SemaphoreType.DMA((sum(len(m) for m in matrices),)),
            pltpu.SemaphoreType.DMA((2,)),
        ],
    )(ids, h2, h2l, unit2, inv2, *cots, gain, shift, down_b, up_b, down, up, *parts)


def cross_bwd_kernel(count, ids, live, dr2, cq, lse, gaub, gadb, pre, *refs):
    kvs, parts, refs = refs[:4], refs[4:10], refs[10:]
    grads, (dcq, *sums) = refs[:4], refs[4:9]
    kv, bufs, (bias, flat, wide, wide_pre, pre_l, gpre, sems, kv_sems) = refs[9:13], refs[13:19], refs[19:]
    copies = [
        pltpu.make_async_copy(parts[n].at[2], bufs[n], sems.at[n]) for n in range(6)
    ]
    loads = [
        pltpu.make_async_copy(kvs[n].at[j], kv[n].at[j], kv_sems.at[n, j]) for j in range(2) for n in range(4)
    ]
    for copy in copies + loads:
        copy.start()
    fill_bias(bias, ids, live)
    fill_prefix(pre, wide_pre, pre_l, count)
    for copy in copies:
        copy.wait()
    value = dr2[...].astype(LOW)
    for n, place in enumerate(SHARED):
        wide[:, place_of(ids, place)] = nt(value, bufs[n][...])
    flat[...] = wide[...].astype(LOW)
    for copy in loads:
        copy.wait()
    for p in range(8):
        lanes = slice(p * 128, (p + 1) * 128)
        g, gk, gv = soft_pair_back(
            stacked(cq[:, lanes]),
            stacked(flat[:, lanes]),
            lse[p],
            pre_l[0, :, lanes],
            pre_l[1, :, lanes],
            [kv[n][0, :, lanes] for n in range(4)],
            [kv[n][1, :, lanes] for n in range(4)],
            [kv[n][0, :, lanes].T for n in range(4)],
            [bias[n * 256 : (n + 1) * 256] for n in range(4)],
            count,
        )
        for j, got in enumerate((gk, gv)):
            gpre[j, :, lanes] = got[0]
            for n in range(4):
                grads[n][j, :, lanes] = got[1 + n].astype(LOW)
        dcq[:, lanes] = unstacked(g, 128).astype(LOW)
    gpre[0, count : count + 1, :] = gaub[...]
    gpre[1, count : count + 1, :] = gadb[...]
    for j in range(2):
        rows = slice(32 * j, 32 * (j + 1))
        for n, dst in enumerate(sums):
            dst[rows, :] = gpre[j, :, cols(ids[13 + n] * 256, 256)].astype(dst.dtype)


def cross_bwd(ids, live, dr2, cq, lse, gaub, gadb, pre, kvs, parts, count):
    grad = out((2, 256, 1024))
    return call(
        functools.partial(cross_bwd_kernel, count),
        "cross_bwd",
        [SMEM, SMEM] + [VMEM] * 6 + [HBM] * 10,
        [grad, grad, grad, grad, out((128, 1024)), out((64, 256), F32)] + [out((64, 256))] * 3,
        [pltpu.VMEM((2, 256, 1024), LOW)] * 4
        + [pltpu.VMEM(p.shape[1:], LOW) for p in parts]
        + [
            pltpu.VMEM((1024, 256), F32),
            pltpu.VMEM((128, 1024), LOW),
            pltpu.VMEM((128, 1024), F32),
            pltpu.VMEM((2, 32, 1024), F32),
            pltpu.VMEM((2, 32, 1024), LOW),
            pltpu.VMEM((2, 32, 1024), F32),
            pltpu.SemaphoreType.DMA((6,)),
            pltpu.SemaphoreType.DMA((4, 2)),
        ],
    )(ids, live, dr2, cq, lse, gaub, gadb, pre, *kvs, *parts)


def query_bwd_kernel(ids, dr2, dcq, unit1, inv1, gain, g1, g2, g3, *refs):
    parts, (dr1, *grads), rest = refs[:6], refs[6:11], refs[11:]
    bufs, (wide, sems) = rest[:6], rest[6:]
    fetch = Fetch(parts, bufs, sems, [shared(1, 0), shared(0, 0)])
    fetch.start(0)
    fetch.start(1)
    fetch.wait(0)
    mm_back(dcq[...], bufs, shared(1, 0), ids, wide)
    grad = ln_back(dr2[...] + SCALE * wide[...], unit1[...], inv1[...], gain[0:1])
    dr1[...] = grad
    fetch.wait(1)
    mm_back(grad.astype(LOW), bufs, shared(0, 0), ids, wide)
    for dst, g in zip(grads[1:], (g1, g2, g3)):
        dst[128:, :] = g[...]
    for n, dst in enumerate(grads):
        dst[:128, :] = wide[:, cols(ids[13 + n] * 256, 256)].astype(LOW)


def query_bwd(ids, dr2, dcq, unit1, inv1, gain, sums, parts):
    return call(
        query_bwd_kernel,
        "query_bwd",
        [SMEM] + [VMEM] * 8 + [HBM] * 6,
        [out((128, 1024), F32), out((128, 256))] + [out((192, 256))] * 3,
        [pltpu.VMEM((2, *p.shape[1:]), LOW) for p in parts]
        + [pltpu.VMEM((128, 1024), F32), pltpu.SemaphoreType.DMA((12,))],
    )(ids, dr2, dcq, unit1, inv1, gain, *sums, *parts)


def quarters(ids, bits, size, start=0):
    first, second = ids[bits[0]], ids[bits[1]]
    pairs = ((first, second), (1 - first, second), (first, 1 - second), (1 - first, 1 - second))
    return [pl.ds(pl.multiple_of(start + (2 * a + b) * size, size), size) for a, b in pairs]


def halve_kernel(bits, count, ids, keep, *refs):
    gots, outs = refs[:count], refs[count:]
    for dst, rows in zip(outs, quarters(ids, bits, outs[0].shape[0])):
        total = keep[rows, :]
        for got in gots:
            total += got[rows, :].astype(F32)
        dst[...] = total.astype(dst.dtype)


def halve(ids, bits, keep, gots):
    size = keep.shape[0] // 4
    return call(
        functools.partial(halve_kernel, bits, len(gots)),
        "halve",
        [SMEM] + [VMEM] * (1 + len(gots)),
        [out((size, 1024), F32)] + [out((size, 1024))] * 3,
    )(ids, keep, *gots)


def mix_kernel(keep, part, g1, g2, g3, dst):
    dst[:32, :] = (
        keep[...] + g1[...].astype(F32) + g2[...].astype(F32) + g3[...].astype(F32)
    ).astype(LOW)
    dst[32:, :] = part[...]


def join_kernel(bits, ids, *refs):
    parts, dst = refs[:4], refs[4]
    for part, rows in zip(parts, quarters(ids, bits, 32)):
        dst[rows, :] = part[:32, :]
    own, other_y, other_z, both = (part[32:, :].astype(F32) for part in parts)
    dst[128:160, :] = (own + other_z).astype(LOW)
    dst[160:, :] = (other_y + both).astype(LOW)


def join_last_kernel(bits, ids, p0, p1, p2, p3, dst, wide):
    parts = (p0, p1, p2, p3)
    for part, rows in zip(parts, quarters(ids, bits, 128)):
        dst[rows, :] = part[:128, :]
    for part, rows in zip(parts, quarters(ids, bits, 64)):
        wide[rows, :] = part[128:, :].astype(F32)
    dst[512:, :] = (wide[:64] + wide[64:128] + wide[128:192] + wide[192:]).astype(LOW)


def totals_kernel(count, ids, mine, got, gau, gad, gps, gpc, gaub, gadb, wide):
    first_core = ids[10] == 0
    gau[...] = jnp.where(first_core, mine[:512], got[:512]).astype(F32)
    gad[...] = jnp.where(first_core, got[:512], mine[:512]).astype(F32).T
    for n in range(4):
        rows = (mine, got)[n // 2][512 + 32 * (n % 2) : 544 + 32 * (n % 2), :].astype(F32)
        for a in range(4):
            wide[32 * a : 32 * a + 32, cols(ids[13 + n] * 256, 256)] = rows[:, 256 * a : 256 * a + 256]
    for j in range(2):
        gps[j] = wide[32 * j : 32 * j + count, :]
        gpc[j] = wide[64 + 32 * j : 64 + 32 * j + count, :]
    gaub[...] = wide[64 + count : 65 + count, :]
    gadb[...] = wide[96 + count : 97 + count, :512]


AXES = ("x", "core", "pair", "z", "y")


def pairs_of(target):
    pairs = []
    for source in range(32):
        row, seq = divmod(source, 8)
        x, c, z, y = target(*divmod(row, 2), *divmod(seq, 2))
        pairs.append((source, (2 * x + c) * 8 + 2 * z + y))
    return pairs


SWAP_X = pairs_of(lambda x, c, z, y: (1 - x, c, z, y))
SWAP_C = pairs_of(lambda x, c, z, y: (x, 1 - c, z, y))
SWAP_Y = pairs_of(lambda x, c, z, y: (x, c, z, 1 - y))
SWAP_CY = pairs_of(lambda x, c, z, y: (x, 1 - c, z, 1 - y))
SWAP_Z = pairs_of(lambda x, c, z, y: (x, c, z ^ 1, y))
SWAP_PAIRS = pairs_of(lambda x, c, z, y: (x, c, z ^ 2, y))
SQUARE = (
    ((17, 18), (SWAP_X, SWAP_Z, pairs_of(lambda x, c, z, y: (1 - x, c, z ^ 1, y)))),
    ((20, 19), (SWAP_Y, SWAP_PAIRS, pairs_of(lambda x, c, z, y: (x, c, z ^ 2, 1 - y)))),
)
TURN = [pairs_of(lambda x, c, z, y, r=r: (x, z // 2, 2 * c + (z + r) % 2, y)) for r in range(2)]


def send(value, pairs):
    return lax.ppermute(value, AXES, pairs)


def local_pairs(
    tokens,
    memory,
    source_len,
    bucket_order,
    prefix_self,
    prefix_cross,
    self_query,
    self_kv,
    self_out,
    cross_query,
    cross_kv,
    cross_out,
    fc_in,
    fc_out,
    ln_gain,
    ln_bias,
    ad_down,
    ad_down_bias,
    ad_up,
    ad_up_bias,
    cotangent,
):
    f32 = F32
    x, c, odd, y = (lax.axis_index(name) for name in ("x", "core", "z", "y"))
    z = 2 * lax.axis_index("pair") + odd
    row = 2 * x + c
    count = prefix_self.shape[1]
    group = 2 * y + c
    far_row, both_row = 2 * (row ^ 2), 2 * (row ^ 3)
    ids = jnp.stack(
        [row, row ^ 1, row ^ 2, row ^ 3]
        + [2 * row, 2 * (row ^ 1), far_row + odd, far_row + 1 - odd, both_row + odd, both_row + 1 - odd]
        + [c, y, odd]
        + [group, group ^ 2, group ^ 1, group ^ 3]
        + [x, odd, z // 2, y]
        + [far_row + y, far_row + 1 - y, both_row + y, both_row + 1 - y]
    ).astype(jnp.int32)

    def after(value, *others):
        if isinstance(value, tuple):
            return lax.optimization_barrier((*value, *others))[: len(value)]
        return lax.optimization_barrier((value, *others))[0]

    def turn_out(first, second):
        first, second = send(first, TURN[0]), send(second, TURN[1])
        return jnp.stack([jnp.where(odd == 1, second, first), jnp.where(odd == 1, first, second)])

    blocks = inbound(ids, tokens, memory)
    first, second = (send(block, turn) for block, turn in zip(blocks, TURN))
    one = pack_first(after(ids, blocks[0]), self_query, self_kv, cross_kv)
    one_far, one_c = send(one, SWAP_X), send(one, SWAP_C)
    live = send(jnp.where(odd == 1, source_len[1], source_len[0]).reshape(1, 1), TURN[0])
    tok = call(
        tokens_kernel, "tokens", [VMEM, VMEM], [out((128, 1024))], [pltpu.SemaphoreType.DMA((2,))]
    )(after(first, one_c, live), second)[0]
    tok_y, tok_c = send(tok, SWAP_Y), send(tok, SWAP_C)
    toks = (tok, tok_y, tok_c, send(tok_y, SWAP_C))
    mid_own, ffn_own, mid_half, in_half, out_half, out_whole = pack(
        after(ids, tok),
        [(n, None, 0, 0, 0, n, 2, n, 12) for n in range(3)]
        + [(3, None, 0, 1024 * n, 1, n, 3, n, 12) for n in range(4)]
        + [(4, None, 256 * n, 0, 1, 4 + n, 4, n, 11) for n in range(2)]
        + [(4, None, 256 * n, 0, 1, 4 + n, 5, n - 2, None) for n in range(2, 4)],
        [
            (3, 256, 1024),
            (8, 256, 1024),
            (3, 128, 1024),
            (4, 128, 1024),
            (2, 128, 1024),
            (2, 256, 1024),
        ],
        self_out,
        cross_query,
        cross_out,
        fc_in,
        fc_out,
    )
    mid_near = send(mid_half, SWAP_X)
    mid_c = send(mid_own, SWAP_C)
    in_near = send(after(in_half, one_far), SWAP_X)

    one_parts = (one, one_c, one_far, send(after(one_far, toks[3], mid_half), SWAP_C))
    mkv = mem_fwd(ids, first, second, one_parts)
    mkv_y = send(mkv, SWAP_Y)
    mkv_c = send(mkv, SWAP_C)

    q, k, v, o0, o1, o2, o3, self_lse = self_fwd(
        ids, bucket_order, after(toks, mkv, mid_c), one_parts, prefix_self, count
    )
    os = (o0, send(o1, SWAP_Y), send(o2, SWAP_C), send(o3, SWAP_CY))
    out_near = send(after(out_half, *os), SWAP_X)
    ffn_c = send(after(ffn_own, q), SWAP_C)
    mid_near_o = after(mid_near, q)
    mid_other = send(mid_near_o, SWAP_Z)
    mid_parts = (mid_own, mid_c, mid_near, mid_other, send(after(mid_near, mkv_y), SWAP_C), send(mid_other, SWAP_C))
    in_other = send(after(in_near, mid_other), SWAP_Z)
    kvs = (mkv, mkv_y, mkv_c, send(mkv_y, SWAP_C))

    cq, cross_lse, unit1, inv1, h2, unit2, inv2, h2l = mid_fwd(
        ids, live, os, tok, ln_gain, ln_bias, prefix_cross, kvs, mid_parts, count
    )
    cot = [jnp.where(odd == 1, cotangent[1 - n], cotangent[n]) for n in range(2)]
    cots = [send(after(v, h2l), t) for v, t in zip(cot, TURN)]
    out_far = send(after(out_whole, h2l), SWAP_X)
    in_near_l, out_near_l = after((in_near, out_near), h2l)
    out_other = send(out_near_l, SWAP_Y)
    ffn_parts = [ffn_own, ffn_c, in_near, in_other]
    ffn_parts += [send(t, SWAP_C) for t in (in_near_l, in_other)]
    ffn_parts += [out_near, out_other]
    ffn_parts += [send(t, SWAP_C) for t in (out_near_l, out_other)]
    ffn_parts += [out_far, send(out_far, SWAP_C)]
    matrices = [[(0, m, "own"), (1, m, "core")] for m in range(8)]
    for m in range(4):
        matrices[m] += [(2 + k, m, place) for k, place in enumerate(SHARED[2:])]
    for m in range(2):
        matrices[4 + m] += [(6 + k, m, place + "_y") for k, place in enumerate(SHARED[2:])]
        matrices[6 + m] += [(10, m, "far"), (11, m, "core_far")]
    m0, m1, dr2, keep, give, gaub, gadb = mlp(
        ids,
        h2,
        h2l,
        unit2,
        inv2,
        cots,
        ln_gain,
        ln_bias,
        ad_down_bias[None],
        ad_up_bias[None],
        ad_down,
        ad_up,
        ffn_parts,
        matrices,
    )
    mixed = turn_out(m0, m1)

    parts = [send(give, SWAP_C)]
    n0, n1, f0, f1, dcq, g0, *gs = cross_bwd(
        ids, live, dr2, cq, cross_lse, gaub, gadb, prefix_cross, kvs, mid_parts, count
    )
    far_c, near_c = send(f1, SWAP_C), send(f0, SWAP_C)
    bits, pairs = SQUARE[0]
    keep, *gives = halve(ids, bits, after(keep, dcq), parts)
    parts = [send(g, p) for g, p in zip(gives, pairs)]
    dr1, d0, d1, d2, d3 = query_bwd(ids, dr2, after(dcq, *gives), unit1, inv1, ln_gain, gs, mid_parts)
    grads = (d0, send(d1, SWAP_Y), send(d2, SWAP_C), send(d3, SWAP_CY))
    mem_k, mem_v = [
        (n1[n].astype(f32) + after(far_c, d0)[n].astype(f32)).astype(LOW) for n in range(2)
    ]
    far_k = send(after(mem_k, *grads), SWAP_Y)
    bits, pairs = SQUARE[1]
    keep, *gives = halve(ids, bits, keep, parts)
    parts = [send(g, p) for g, p in zip(gives, pairs)]
    near, far_part, part = self_bwd(
        ids,
        bucket_order,
        after(q, mem_k, mem_v, mixed, near_c),
        k,
        v,
        grads,
        g0,
        self_lse,
        one_parts,
        prefix_self,
        count,
    )
    got_c = send(after(far_part, far_k), SWAP_C)
    far_v = send(mem_v, SWAP_Y)
    mine = call(mix_kernel, "mix", [VMEM] * 5, [out((64, 1024))])(keep, part, *parts)[0]
    parts = [send(mine, p) for p in pairs]

    give_y = (near[128:].astype(f32) + got_c[128:].astype(f32)).astype(LOW)
    d_own = dr1 + near[:128].astype(f32) + got_c[:128].astype(f32)
    d_own = (d_own + send(give_y, SWAP_Y).astype(f32)).astype(LOW)
    d_tokens = turn_out(d_own[:64], d_own[64:])

    d_memory = turn_out(*mem_back(ids, n0, near_c, far_k, far_v, one_parts))

    whole = call(
        functools.partial(join_kernel, bits), "join", [SMEM] + [VMEM] * 4, [out((192, 1024))]
    )(ids, mine, *parts)[0]
    bits, pairs = SQUARE[0]
    parts = [send(whole, p) for p in pairs]
    whole = call(
        functools.partial(join_last_kernel, bits),
        "join",
        [SMEM] + [VMEM] * 4,
        [out((576, 1024))],
        [pltpu.VMEM((256, 1024), F32)],
    )(ids, whole, *parts)[0]
    grad_up, grad_down, grad_ps, grad_pc, grad_ub, grad_db = call(
        functools.partial(totals_kernel, count),
        "totals",
        [SMEM, VMEM, VMEM],
        [
            out((512, 1024), F32),
            out((1024, 512), F32),
            out(prefix_self.shape, F32),
            out(prefix_cross.shape, F32),
            out((1, 1024), F32),
            out((1, 512), F32),
        ],
        [pltpu.VMEM((128, 1024), F32)],
    )(ids, whole, send(whole, SWAP_C))
    return (
        mixed,
        d_tokens,
        d_memory,
        grad_ps,
        grad_pc,
        grad_down,
        grad_db[0],
        grad_up,
        grad_ub[0],
    )


def solution(mesh):
    in_specs = (
        P("row", "seq", None),
        P("row", "seq", None),
        P("row"),
        P(),
        P(),
        P(),
        P("row", None),
        P(None, "row", None),
        P("row", None),
        P("row", None),
        P(None, "row", None),
        P("row", None),
        P("row", None),
        P("row", None),
        P(),
        P(),
        P(),
        P(),
        P(),
        P(),
        P("row", "seq", None),
    )
    out_specs = (
        P("row", "seq", None),
        P("row", "seq", None),
        P("row", "seq", None),
        P(),
        P(),
        P(),
        P(),
        P(),
        P(),
    )
    if (mesh.shape["row"], mesh.shape["seq"]) != (4, 8):
        return jax.shard_map(
            local_rows, mesh=mesh, in_specs=in_specs, out_specs=out_specs, check_vma=False
        )
    fine = jax.sharding.Mesh(mesh.devices.reshape(2, 2, 2, 2, 2), AXES)
    split = {"row": ("x", "core"), "seq": ("pair", "z", "y")}

    def renamed(specs):
        return tuple(P(*(split.get(name) for name in spec)) for spec in specs)

    return jax.shard_map(
        local_pairs, mesh=fine, in_specs=renamed(in_specs), out_specs=renamed(out_specs), check_vma=False
    )
```

```python
import functools

import jax
import jax.numpy as jnp
from jax import lax
from jax.experimental import pallas as pl
from jax.experimental.pallas import tpu as pltpu
from jax.sharding import PartitionSpec as P

H = 16
HD = 64


EPSILON = 1e-05
MASKED = -1e30


def normalize(value, gain, shift):
    centre = value - jnp.mean(value, axis=-1, keepdims=True)
    inv_dev = lax.rsqrt(jnp.mean(centre * centre, axis=-1, keepdims=True) + EPSILON)
    unit_val = centre * inv_dev
    return (unit_val * gain + shift, unit_val, inv_dev)


def normalize_back(grad, unit_val, inv_dev, gain):
    scaled = grad * gain
    return inv_dev * (
        scaled
        - jnp.mean(scaled, axis=-1, keepdims=True)
        - unit_val * jnp.mean(scaled * unit_val, axis=-1, keepdims=True)
    )


def gelu_exact(value):
    return jax.nn.gelu(value, approximate=False)


def gelu_back(value, grad):
    return jax.vjp(gelu_exact, value)[1](grad)[0]


def head_split(matrix):
    return matrix.reshape(matrix.shape[0], -1, HD)


def masked_scores(queries, keys, mask):
    scores = jnp.einsum(
        "qhd,khd->hqk", head_split(queries), head_split(keys), preferred_element_type=jnp.float32
    )
    return jnp.where(mask[None], scores, MASKED)


def attend(queries, keys, values, mask):
    scores = masked_scores(queries, keys, mask)
    top_score = jnp.max(scores, axis=-1, keepdims=True)
    log_total = top_score + jnp.log(jnp.sum(jnp.exp(scores - top_score), axis=-1, keepdims=True))
    probs = jnp.exp(scores - log_total).astype(jnp.bfloat16)
    result = jnp.einsum(
        "hqk,khd->qhd", probs, head_split(values), preferred_element_type=jnp.float32
    )
    return (result.reshape(queries.shape[0], -1), log_total)


def attend_back(queries, keys, values, mask, log_total, grad_out):
    probs = jnp.exp(masked_scores(queries, keys, mask) - log_total)
    grad_heads = head_split(grad_out)
    grad_probs = jnp.einsum(
        "qhd,khd->hqk", grad_heads, head_split(values), preferred_element_type=jnp.float32
    )
    row_delta = jnp.sum(probs * grad_probs, axis=-1, keepdims=True)
    grad_scores = (probs * (grad_probs - row_delta)).astype(jnp.bfloat16)
    grad_query = jnp.einsum(
        "hqk,khd->qhd", grad_scores, head_split(keys), preferred_element_type=jnp.float32
    )
    grad_keys = jnp.einsum(
        "hqk,qhd->khd", grad_scores, head_split(queries), preferred_element_type=jnp.float32
    )
    grad_values = jnp.einsum(
        "hqk,qhd->khd", probs.astype(jnp.bfloat16), grad_heads, preferred_element_type=jnp.float32
    )
    return (
        grad_query.reshape(queries.shape[0], -1),
        grad_keys.reshape(keys.shape[0], -1),
        grad_values.reshape(values.shape[0], -1),
    )


def project(left, right):
    return jnp.dot(left, right, preferred_element_type=jnp.float32)


def local_rows(
    tokens,
    memory,
    source_len,
    bucket_order,
    prefix_self,
    prefix_cross,
    self_query,
    self_kv,
    self_out,
    cross_query,
    cross_kv,
    cross_out,
    fc_in,
    fc_out,
    ln_gain,
    ln_bias,
    ad_down,
    ad_down_bias,
    ad_up,
    ad_up_bias,
    cotangent,
):
    low_type = jnp.bfloat16
    row_count, tok_count, width = tokens.shape
    slot_count = memory.shape[1]
    prefix_count = prefix_self.shape[1]
    half_len = tok_count // 2
    scale = HD ** (-0.5)
    weight_set = (
        lax.all_gather(self_query.astype(low_type), "row", axis=0, tiled=True),
        lax.all_gather(self_kv.astype(low_type), "row", axis=1, tiled=True),
        lax.all_gather(self_out.astype(low_type), "row", axis=0, tiled=True),
        lax.all_gather(cross_query.astype(low_type), "row", axis=0, tiled=True),
        lax.all_gather(cross_kv.astype(low_type), "row", axis=1, tiled=True),
        lax.all_gather(cross_out.astype(low_type), "row", axis=0, tiled=True),
        lax.all_gather(fc_in.astype(low_type), "row", axis=0, tiled=True),
        lax.all_gather(fc_out.astype(low_type), "row", axis=0, tiled=True),
    )
    q_weight, kv_weight, o_weight, cq_weight, ckv_weight, co_weight, in_weight, out_weight = (
        weight_set
    )
    place = lax.axis_index("seq")
    offsets = jnp.arange(half_len, dtype=jnp.int32)
    all_pos = (bucket_order[:, None] * half_len + offsets[None, :]).reshape(-1)
    own_pos = lax.dynamic_slice_in_dim(all_pos, place * tok_count, tok_count)
    self_mask = jnp.concatenate(
        [jnp.ones((tok_count, prefix_count), jnp.bool_), all_pos[None, :] <= own_pos[:, None]],
        axis=1,
    )
    flat_tokens = tokens.reshape(-1, width)
    queries = (project(flat_tokens, q_weight) * scale).astype(low_type)
    own_keys = (
        project(flat_tokens, kv_weight[0]).astype(low_type).reshape(row_count, tok_count, width)
    )
    own_values = (
        project(flat_tokens, kv_weight[1]).astype(low_type).reshape(row_count, tok_count, width)
    )
    flat_memory = memory.reshape(-1, width)
    mem_keys = (
        project(flat_memory, ckv_weight[0]).astype(low_type).reshape(row_count, slot_count, width)
    )
    mem_values = (
        project(flat_memory, ckv_weight[1]).astype(low_type).reshape(row_count, slot_count, width)
    )
    all_keys, all_values, all_mkeys, all_mvalues = (
        lax.all_gather(own_keys, "seq", axis=1, tiled=True),
        lax.all_gather(own_values, "seq", axis=1, tiled=True),
        lax.all_gather(mem_keys, "seq", axis=1, tiled=True),
        lax.all_gather(mem_values, "seq", axis=1, tiled=True),
    )
    src_total = all_mkeys.shape[1]
    pre_self = prefix_self.astype(low_type)
    pre_cross = prefix_cross.astype(low_type)
    self_key_sets = [
        jnp.concatenate([pre_self[0], all_keys[row_index]], 0) for row_index in range(row_count)
    ]
    self_value_sets = [
        jnp.concatenate([pre_self[1], all_values[row_index]], 0) for row_index in range(row_count)
    ]
    cross_key_sets = [
        jnp.concatenate([pre_cross[0], all_mkeys[row_index]], 0) for row_index in range(row_count)
    ]
    cross_value_sets = [
        jnp.concatenate([pre_cross[1], all_mvalues[row_index]], 0) for row_index in range(row_count)
    ]
    slot_number = jnp.arange(src_total, dtype=jnp.int32)
    cross_masks = [
        jnp.concatenate(
            [jnp.ones((prefix_count,), jnp.bool_), slot_number < source_len[row_index]]
        )[None, :]
        for row_index in range(row_count)
    ]

    def rows_of(matrix, row_index):
        return matrix[row_index * tok_count : (row_index + 1) * tok_count]

    self_parts = [
        attend(
            rows_of(queries, row_index),
            self_key_sets[row_index],
            self_value_sets[row_index],
            self_mask,
        )
        for row_index in range(row_count)
    ]
    attended = jnp.concatenate([part[0] for part in self_parts], 0).astype(low_type)
    resid_one = flat_tokens.astype(jnp.float32) + project(attended, o_weight)
    hidden_one, unit_one, inv_one = normalize(resid_one, ln_gain[0], ln_bias[0])
    cross_queries = (project(hidden_one.astype(low_type), cq_weight) * scale).astype(low_type)
    cross_parts = [
        attend(
            rows_of(cross_queries, row_index),
            cross_key_sets[row_index],
            cross_value_sets[row_index],
            cross_masks[row_index],
        )
        for row_index in range(row_count)
    ]
    cross_att = jnp.concatenate([part[0] for part in cross_parts], 0).astype(low_type)
    resid_two = hidden_one + project(cross_att, co_weight)
    hidden_two, unit_two, inv_two = normalize(resid_two, ln_gain[1], ln_bias[1])
    hidden_low = hidden_two.astype(low_type)
    up_proj = project(hidden_low, in_weight)
    activated = gelu_exact(up_proj).astype(low_type)
    ffn_out = project(activated, out_weight)
    down_weight = ad_down.astype(low_type)
    up_weight = ad_up.astype(low_type)
    down_proj = project(hidden_low, down_weight) + ad_down_bias
    down_act = gelu_exact(down_proj).astype(low_type)
    adapted = project(down_act, up_weight) + ad_up_bias
    resid_three = hidden_two + ffn_out + 4.0 * adapted
    output, unit_three, inv_three = normalize(resid_three, ln_gain[2], ln_bias[2])
    mixed = output.astype(low_type).reshape(row_count, tok_count, width)
    weight_set = (
        lax.all_gather(self_query.astype(low_type), "row", axis=0, tiled=True),
        lax.all_gather(self_kv.astype(low_type), "row", axis=1, tiled=True),
        lax.all_gather(self_out.astype(low_type), "row", axis=0, tiled=True),
        lax.all_gather(cross_query.astype(low_type), "row", axis=0, tiled=True),
        lax.all_gather(cross_kv.astype(low_type), "row", axis=1, tiled=True),
        lax.all_gather(cross_out.astype(low_type), "row", axis=0, tiled=True),
        lax.all_gather(fc_in.astype(low_type), "row", axis=0, tiled=True),
        lax.all_gather(fc_out.astype(low_type), "row", axis=0, tiled=True),
    )
    q_weight, kv_weight, o_weight, cq_weight, ckv_weight, co_weight, in_weight, out_weight = (
        weight_set
    )
    grad_out = cotangent.astype(jnp.float32).reshape(-1, width)
    grad_three = normalize_back(grad_out, unit_three, inv_three, ln_gain[2])
    grad_ffn = grad_three.astype(low_type)
    grad_adapt = (4.0 * grad_three).astype(low_type)
    grad_up_w = jnp.einsum("na,nd->ad", down_act, grad_adapt, preferred_element_type=jnp.float32)
    grad_up_b = jnp.sum(grad_adapt.astype(jnp.float32), axis=0)
    grad_down = gelu_back(down_proj, project(grad_adapt, up_weight.T)).astype(low_type)
    grad_down_w = jnp.einsum("nd,na->da", hidden_low, grad_down, preferred_element_type=jnp.float32)
    grad_down_b = jnp.sum(grad_down.astype(jnp.float32), axis=0)
    grad_inner = gelu_back(up_proj, project(grad_ffn, out_weight.T)).astype(low_type)
    grad_hidden_two = (
        grad_three + project(grad_inner, in_weight.T) + project(grad_down, down_weight.T)
    )
    grad_two = normalize_back(grad_hidden_two, unit_two, inv_two, ln_gain[1])
    grad_cross_att = project(grad_two.astype(low_type), co_weight.T).astype(low_type)
    cross_grads = [
        attend_back(
            rows_of(cross_queries, row_index),
            cross_key_sets[row_index],
            cross_value_sets[row_index],
            cross_masks[row_index],
            cross_parts[row_index][1],
            rows_of(grad_cross_att, row_index),
        )
        for row_index in range(row_count)
    ]
    grad_cq = jnp.concatenate([part[0] for part in cross_grads], 0).astype(low_type)
    grad_hidden_one = grad_two + project(grad_cq, cq_weight.T) * scale
    grad_one = normalize_back(grad_hidden_one, unit_one, inv_one, ln_gain[0])
    grad_attended = project(grad_one.astype(low_type), o_weight.T).astype(low_type)
    self_grads = [
        attend_back(
            rows_of(queries, row_index),
            self_key_sets[row_index],
            self_value_sets[row_index],
            self_mask,
            self_parts[row_index][1],
            rows_of(grad_attended, row_index),
        )
        for row_index in range(row_count)
    ]
    pre_self_grad = jnp.stack(
        [
            sum((part[1][:prefix_count] for part in self_grads)),
            sum((part[2][:prefix_count] for part in self_grads)),
        ]
    )
    pre_cross_grad = jnp.stack(
        [
            sum((part[1][:prefix_count] for part in cross_grads)),
            sum((part[2][:prefix_count] for part in cross_grads)),
        ]
    )
    summed = [
        (
            lax.psum_scatter(
                self_grads[row_index][1][prefix_count:].astype(jnp.bfloat16),
                "seq",
                scatter_dimension=0,
                tiled=True,
            ).astype(jnp.float32),
            lax.psum_scatter(
                self_grads[row_index][2][prefix_count:].astype(jnp.bfloat16),
                "seq",
                scatter_dimension=0,
                tiled=True,
            ).astype(jnp.float32),
            lax.psum_scatter(
                cross_grads[row_index][1][prefix_count:].astype(jnp.bfloat16),
                "seq",
                scatter_dimension=0,
                tiled=True,
            ).astype(jnp.float32),
            lax.psum_scatter(
                cross_grads[row_index][2][prefix_count:].astype(jnp.bfloat16),
                "seq",
                scatter_dimension=0,
                tiled=True,
            ).astype(jnp.float32),
        )
        for row_index in range(row_count)
    ]
    key_grad = jnp.stack([part[0] for part in summed])
    value_grad = jnp.stack([part[1] for part in summed])
    mkey_grad = jnp.stack([part[2] for part in summed])
    mvalue_grad = jnp.stack([part[3] for part in summed])
    grad_query = jnp.concatenate([part[0] for part in self_grads], 0).astype(low_type)
    d_tokens = (
        grad_one
        + project(grad_query, q_weight.T) * scale
        + project(key_grad.astype(low_type).reshape(-1, width), kv_weight[0].T)
        + project(value_grad.astype(low_type).reshape(-1, width), kv_weight[1].T)
    )
    d_memory = project(mkey_grad.astype(low_type).reshape(-1, width), ckv_weight[0].T) + project(
        mvalue_grad.astype(low_type).reshape(-1, width), ckv_weight[1].T
    )
    totals = lax.psum(
        (pre_self_grad, pre_cross_grad, grad_down_w, grad_down_b, grad_up_w, grad_up_b),
        ("row", "seq"),
    )
    return (
        mixed,
        d_tokens.astype(low_type).reshape(row_count, tok_count, width),
        d_memory.astype(low_type).reshape(row_count, slot_count, width),
        totals[0],
        totals[1],
        totals[2],
        totals[3],
        totals[4],
        totals[5],
    )


LOW = jnp.bfloat16
F32 = jnp.float32
SCALE = 0.125
VMEM = pl.BlockSpec(memory_space=pltpu.VMEM)
SMEM = pl.BlockSpec(memory_space=pltpu.SMEM)
HBM = pl.BlockSpec(memory_space=pltpu.HBM)


def shape_of(shape, dtype=LOW):
    return jax.ShapeDtypeStruct(shape, dtype)


def nn(left, right):
    return jnp.dot(left, right, preferred_element_type=F32)


def nt(left, right):
    return lax.dot_general(left, right, (((1,), (1,)), ((), ())), preferred_element_type=F32)


def tn(left, right):
    return lax.dot_general(left, right, (((0,), (0,)), ((), ())), preferred_element_type=F32)


def cols(start, size):
    return pl.ds(pl.multiple_of(start, 128), size)


def ln(value, gain, shift):
    centre = value - jnp.mean(value, axis=-1, keepdims=True)
    inv = lax.rsqrt(jnp.mean(centre * centre, axis=-1, keepdims=True) + EPSILON)
    unit = centre * inv
    return unit * gain + shift, unit, inv


def ln_back(grad, unit, inv, gain):
    scaled = grad * gain
    return inv * (
        scaled
        - jnp.mean(scaled, axis=-1, keepdims=True)
        - unit * jnp.mean(scaled * unit, axis=-1, keepdims=True)
    )


def gelu_both(value):
    cdf = 0.5 * (1.0 + lax.erf(value * 0.7071067811865476))
    return value * cdf, cdf + value * (jnp.exp(-0.5 * value * value) * 0.3989422804014327)


def stacked(block):
    first = lax.broadcasted_iota(jnp.int32, block.shape, 1) < 64
    zero = jnp.zeros_like(block)
    return jnp.concatenate([jnp.where(first, block, zero), jnp.where(first, zero, block)], 0)


def unstacked(both, n):
    return jnp.concatenate([both[:64, :n], both[64:, n:]], 0).T


def pre_mask(shape, count):
    return lax.broadcasted_iota(jnp.int32, shape, 0) < count


def soft_pair(qs, k_pre, k_blocks, v_pre, vt_blocks, biases, count):
    s_pre = nt(k_pre, qs)
    s_pre = jnp.where(pre_mask(s_pre.shape, count), s_pre, MASKED)
    s_blocks = [nt(k, qs) + b for k, b in zip(k_blocks, biases)]
    top = jnp.max(s_pre, axis=0, keepdims=True)
    for s in s_blocks:
        top = jnp.maximum(top, jnp.max(s, axis=0, keepdims=True))
    e_pre = jnp.exp(s_pre - top)
    total = jnp.sum(e_pre, axis=0, keepdims=True)
    out = tn(v_pre, e_pre.astype(LOW))
    for s, vt in zip(s_blocks, vt_blocks):
        e = jnp.exp(s - top)
        total += jnp.sum(e, axis=0, keepdims=True)
        out += nn(vt, e.astype(LOW))
    return out * (1.0 / total), top + jnp.log(total)


def soft_pair_back(qs, dos, lse, k_pre, v_pre, ks, vs, kts, biases, count):
    s_pre = nt(k_pre, qs)
    p_pre = jnp.where(pre_mask(s_pre.shape, count), jnp.exp(s_pre - lse), 0.0)
    d_pre = nt(v_pre, dos)
    delta = jnp.sum(p_pre * d_pre, axis=0, keepdims=True)
    ps, ds = [], []
    for k, v, b in zip(ks, vs, biases):
        p = jnp.exp(nt(k, qs) + b - lse)
        d = nt(v, dos)
        delta += jnp.sum(p * d, axis=0, keepdims=True)
        ps.append(p)
        ds.append(d)
    g_pre = (p_pre * (d_pre - delta)).astype(LOW)
    dq = tn(k_pre, g_pre)
    dk, dv = [nn(g_pre, qs)], [nn(p_pre.astype(LOW), dos)]
    for p, d, kt in zip(ps, ds, kts):
        g = (p * (d - delta)).astype(LOW)
        dq += nn(kt, g)
        dk.append(nn(g, qs))
        dv.append(nn(p.astype(LOW), dos))
    return dq, dk, dv


COSTS = {
    "pack_heads": 1.5,
    "pack": 5.0,
    "self_fwd": 5.0,
    "mem_fwd": 2.3,
    "mid_fwd": 10.0,
    "mlp": 20.0,
    "cross_bwd": 11.0,
    "query_bwd": 3.0,
    "self_bwd": 6.5,
    "mem_back": 2.5,
    "totals": 3.0,
}
LIMITS = {
    "pack_heads": 60,
    "inbound": 20,
    "tokens": 4,
    "pack": 60,
    "self_fwd": 14,
    "self_bwd": 18,
    "mem_fwd": 14,
    "mem_back": 14,
    "mid_fwd": 24,
    "mlp": 60,
    "cross_bwd": 60,
    "query_bwd": 12,
    "halve": 6,
    "join": 8,
    "totals": 20,
    "mix": 4,
}


def call(kernel, name, ins, outs, scratch=()):
    flops = int(COSTS.get(name, 0.8) * 0.3e9)
    return pl.pallas_call(
        kernel,
        cost_estimate=pl.CostEstimate(flops=flops, bytes_accessed=1000, transcendentals=0),
        in_specs=ins,
        out_specs=[o[0] for o in outs],
        out_shape=[o[1] for o in outs],
        scratch_shapes=list(scratch),
        compiler_params=pltpu.CompilerParams(vmem_limit_bytes=LIMITS[name] * 2**20),
        name=name,
    )


def out(shape, dtype=LOW, space=VMEM):
    return space, jax.ShapeDtypeStruct(shape, dtype)


def inbound_kernel(ids, tokens, memory, first, second, sems):
    copies = []
    for n, dst in enumerate((first, second)):
        row = ids[12] if n == 0 else 1 - ids[12]
        for m, (src, start, size) in enumerate(((tokens, 0, 64), (memory, 64, 128))):
            copies.append(pltpu.make_async_copy(src.at[row], dst.at[pl.ds(start, size)], sems.at[n, m]))
    for copy in copies:
        copy.start()
    for copy in copies:
        copy.wait()


def inbound(ids, tokens, memory):
    return call(
        inbound_kernel,
        "inbound",
        [SMEM, HBM, HBM],
        [out((192, 1024)), out((192, 1024))],
        [pltpu.SemaphoreType.DMA((2, 2))],
    )(ids, tokens, memory)


def tokens_kernel(first, second, dst, sems):
    copies = [
        pltpu.make_async_copy(src.at[pl.ds(0, 64)], dst.at[pl.ds(64 * n, 64)], sems.at[n])
        for n, src in enumerate((first, second))
    ]
    for copy in copies:
        copy.start()
    for copy in copies:
        copy.wait()


def pack_first_kernel(ids, query, kv, ckv, dst, wide, sems):
    copies = [pltpu.make_async_copy(ckv.at[n], wide.at[pl.ds(256 * n, 256)], sems.at[n]) for n in range(2)]
    for n in range(2):
        group = cols(ids[13 + 2 * n] * 256, 256)
        for j, src in enumerate((query, kv.at[0])):
            copies.append(
                pltpu.make_async_copy(
                    src.at[:, group],
                    wide.at[pl.ds(512, 256), pl.ds(512 * n + 256 * j, 256)],
                    sems.at[2 + 4 * n + j],
                )
            )
        for j in range(2):
            copies.append(
                pltpu.make_async_copy(
                    kv.at[1, pl.ds(128 * j, 128), group],
                    wide.at[pl.ds(768, 128), pl.ds(512 * j + 256 * n, 256)],
                    sems.at[4 + 4 * n + j],
                )
            )
    for copy in copies:
        copy.start()
    for copy in copies:
        copy.wait()
    dst[...] = wide[...].astype(LOW)


def pack_first(ids, query, kv, ckv):
    return call(
        pack_first_kernel,
        "pack_heads",
        [SMEM, HBM, HBM, HBM],
        [out((896, 1024))],
        [pltpu.VMEM((896, 1024), F32), pltpu.SemaphoreType.DMA((10,))],
    )(ids, query, kv, ckv)[0]


def head_weights(parts):
    for n, part in enumerate(parts):
        g = n % 2
        yield (
            part[512:768, 512 * g : 512 * g + 256],
            part[512:768, 512 * g + 256 : 512 * g + 512],
            part[768:, 256 * g : 256 * g + 256],
            part[768:, 512 + 256 * g : 768 + 256 * g],
        )


def pack_kernel(sources, n_args, ids, *refs):
    args, refs = refs[:n_args], refs[n_args:]
    outs, (wide, narrow, in_sem, own_sem, part_sem) = refs[:-5], refs[-5:]
    count = len(sources)

    def fetch(m):
        arg, lead, row, col, kept_in = sources[m][:5]
        src = args[arg] if lead is None else args[arg].at[lead]
        start, size = row, 256
        if kept_in is None:
            start, size = pl.multiple_of(row + ids[sources[m][-1]] * 128, 128), 128
        return pltpu.make_async_copy(
            src.at[pl.ds(start, size), pl.ds(col, 1024)], wide.at[m, pl.ds(0, size)], in_sem.at[m]
        )

    def store(m):
        kept_in, kept_at, number, index, bit = sources[m][4:]
        kept = narrow.at[m]
        half = kept
        if kept_in is None:
            half = kept.at[pl.ds(0, 128)]
        elif bit is not None:
            half = kept.at[pl.ds(pl.multiple_of(ids[bit] * 128, 128), 128)]
        part = pltpu.make_async_copy(half, outs[number].at[index], part_sem.at[m])
        if kept_in is None:
            return (part,)
        return pltpu.make_async_copy(kept, outs[kept_in].at[kept_at], own_sem.at[m]), part

    for m in range(count):
        fetch(m).start()
    for m in range(count):
        fetch(m).wait()
        narrow[m] = wide[m].astype(LOW)
        for copy in store(m):
            copy.start()
    for m in range(count):
        for copy in store(m):
            copy.wait()


def pack(ids, sources, shapes, *args):
    return call(
        functools.partial(pack_kernel, sources, len(args)),
        "pack",
        [SMEM] + [HBM] * len(args),
        [out(shape, LOW, HBM) for shape in shapes],
        [
            pltpu.VMEM((len(sources), 256, 1024), F32),
            pltpu.VMEM((len(sources), 256, 1024), LOW),
            pltpu.SemaphoreType.DMA((len(sources),)),
            pltpu.SemaphoreType.DMA((len(sources),)),
            pltpu.SemaphoreType.DMA((len(sources),)),
        ],
    )(ids, *args)


PLACES = {
    "own": (lambda ids: ids[4], 256),
    "core": (lambda ids: ids[5], 256),
    "near": (lambda ids: ids[6], 128),
    "other": (lambda ids: ids[7], 128),
    "core_near": (lambda ids: ids[8], 128),
    "core_other": (lambda ids: ids[9], 128),
    "near_y": (lambda ids: ids[21], 128),
    "other_y": (lambda ids: ids[22], 128),
    "core_near_y": (lambda ids: ids[23], 128),
    "core_other_y": (lambda ids: ids[24], 128),
    "far": (lambda ids: 2 * ids[2], 256),
    "core_far": (lambda ids: 2 * ids[3], 256),
}
DIRECT = ("own", "core", "far", "core_far")
SHARED = ("own", "core", "near", "other", "core_near", "core_other")


def shared(index, first):
    return [(n, index + first if n < 2 else index, place) for n, place in enumerate(SHARED)]


def direct(index):
    return [(n, index, place) for n, place in enumerate(DIRECT)]


def place_of(ids, place):
    first, size = PLACES[place]
    return cols(first(ids) * 128, size)


def mm(x_ref, refs, matrix, ids):
    acc = None
    for n, index, place in matrix:
        term = nn(x_ref[:, place_of(ids, place)], refs[n][index])
        acc = term if acc is None else acc + term
    return acc


def mm_back(value, refs, matrix, ids, out_ref):
    for n, index, place in matrix:
        out_ref[:, place_of(ids, place)] = nt(value, refs[n][index])


class Fetch:
    def __init__(self, sources, targets, sems, matrices, first=0):
        self.copies, number = [], 0
        for matrix in matrices:
            mine = []
            for n, index, _ in matrix:
                to = index - first if n < 2 else index
                mine.append(pltpu.make_async_copy(sources[n].at[index], targets[n].at[to], sems.at[number]))
                number += 1
            self.copies.append(mine)

    def start(self, m):
        for copy in self.copies[m]:
            copy.start()

    def wait(self, m):
        for copy in self.copies[m]:
            copy.wait()


def fill_prefix(pre, wide, narrow, count, where=None):
    wide[...] = jnp.zeros_like(wide)
    wide[:, :count, :] = pre[...] if where is None else pre[:, :, where]
    narrow[...] = wide[...].astype(LOW)


def fill_places(order, ids, kpos, qpos):
    c, y, odd = ids[10], ids[11], ids[12]
    lane = lax.broadcasted_iota(jnp.int32, (1, 512), 1)
    column = jnp.zeros((1, 512), jnp.int32)
    for n in range(16):
        core = c if n < 8 else 1 - c
        line = y if n % 8 < 4 else 1 - y
        turned = odd if n % 4 < 2 else 1 - odd
        bucket = 2 * (2 * (2 * core + turned) + line) + n % 2
        first = order[bucket] * 32
        kpos[n * 32 : (n + 1) * 32, :] = lax.broadcasted_iota(jnp.int32, (32, 1), 0) + first
        column = jnp.where(lane // 32 == n, first + lane % 32, column)
    qpos[...] = column


def self_bias(kpos, qpos, t):
    seen = kpos[...] <= qpos[:, t * 128 : (t + 1) * 128]
    bias = jnp.where(seen, 0.0, MASKED)
    return jnp.concatenate([bias, bias], 1)


def self_fwd_kernel(
    count, ids, order, t0, t1, t2, t3, w0, w1, w2, w3, pre, q_ref, k_ref, v_ref,
    o0, o1, o2, o3, lse_ref, vt, kpos, qpos, wide, pre_l
):
    fill_places(order, ids, kpos, qpos)
    fill_prefix(pre, wide, pre_l, count, cols(ids[13] * 256, 256))
    for t, tok in enumerate((t0, t1, t2, t3)):
        rows = slice(t * 128, (t + 1) * 128)
        acc = [0.0, 0.0, 0.0]
        for n, (wq, wk, wv, wv2) in enumerate(head_weights((w0, w1, w2, w3))):
            some = tok[:, cols(ids[n] * 256, 256)]
            acc[0] += nn(some, wq)
            acc[1] += nn(some, wk)
            acc[2] += nn(some[:, :128], wv) + nn(some[:, 128:], wv2)
        q_ref[rows, :] = (acc[0] * SCALE).astype(LOW)
        k_ref[rows, :] = acc[1].astype(LOW)
        v_ref[rows, :] = acc[2].astype(LOW)
    vt[...] = v_ref[...].T
    for t in (3, 1, 2, 0):
        bias = self_bias(kpos, qpos, t)
        for p in range(2):
            lanes = slice(p * 128, (p + 1) * 128)
            qs = stacked(q_ref[t * 128 : (t + 1) * 128, lanes])
            got, lse = soft_pair(
                qs, pre_l[0, :, lanes], [k_ref[:, lanes]], pre_l[1, :, lanes], [vt[lanes, :]], [bias], count
            )
            (o0, o1, o2, o3)[t][:, lanes] = unstacked(got, 128).astype(LOW)
            lse_ref[p, t] = lse


def self_fwd(ids, order, toks, ws, pre, count):
    return call(
        functools.partial(self_fwd_kernel, count),
        "self_fwd",
        [SMEM, SMEM] + [VMEM] * 9,
        [
            out((512, 256)),
            out((512, 256)),
            out((512, 256)),
            out((128, 256)),
            out((128, 256)),
            out((128, 256)),
            out((128, 256)),
            out((2, 4, 1, 256), F32),
        ],
        [
            pltpu.VMEM((256, 512), LOW),
            pltpu.VMEM((512, 1), jnp.int32),
            pltpu.VMEM((1, 512), jnp.int32),
            pltpu.VMEM((2, 32, 256), F32),
            pltpu.VMEM((2, 32, 256), LOW),
        ],
    )(ids, order, *toks, *ws, pre)


def self_bwd_kernel(
    count, ids, order, q, k, v, d0, d1, d2, d3, g0, lse_ref, w0, w1, w2, w3, pre,
    near_ref, far_ref, sums_ref, kt, dq, dk, dv, gpre_ref, kpos, qpos, wide, pre_l
):
    fill_places(order, ids, kpos, qpos)
    fill_prefix(pre, wide, pre_l, count, cols(ids[13] * 256, 256))
    kt[...] = k[...].T
    grads = (d0, d1, d2, d3)
    for t in range(4):
        bias = self_bias(kpos, qpos, t)
        for p in range(2):
            lanes = slice(p * 128, (p + 1) * 128)
            qs = stacked(q[t * 128 : (t + 1) * 128, lanes])
            dos = stacked(grads[t][:128, lanes])
            g, gk, gv = soft_pair_back(
                qs,
                dos,
                lse_ref[p, t],
                pre_l[0, :, lanes],
                pre_l[1, :, lanes],
                [k[:, lanes]],
                [v[:, lanes]],
                [kt[lanes, :]],
                [bias],
                count,
            )
            dq[t * 128 : (t + 1) * 128, lanes] = unstacked(g, 128).astype(LOW)
            if t == 0:
                gpre_ref[:32, lanes] = gk[0]
                gpre_ref[32:, lanes] = gv[0]
                dk[:, lanes] = gk[1]
                dv[:, lanes] = gv[1]
            else:
                gpre_ref[:32, lanes] += gk[0]
                gpre_ref[32:, lanes] += gv[0]
                dk[:, lanes] += gk[1]
                dv[:, lanes] += gv[1]
    cross = g0[...] + d1[128:].astype(F32) + d2[128:].astype(F32) + d3[128:].astype(F32)
    for n, rows in enumerate((gpre_ref[:32], gpre_ref[32:], cross[:32], cross[32:])):
        sums_ref[:, 256 * n : 256 * (n + 1)] = rows.astype(LOW)
    dkl, dvl = dk[...].astype(LOW), dv[...].astype(LOW)
    for n, (wq, wk, wv, wv2) in enumerate(head_weights((w0, w1, w2, w3))):
        part = jnp.concatenate([nt(dvl, wv), nt(dvl, wv2)], 1)
        part = (part + nt(dq[...], wq) * SCALE + nt(dkl, wk)).astype(LOW)
        near_ref[:, cols(ids[n] * 256, 256)] = part[:256]
        far_ref[:, cols(ids[n] * 256, 256)] = part[256:]


def self_bwd(ids, order, q, k, v, grads, g0, lse, ws, pre, count):
    return call(
        functools.partial(self_bwd_kernel, count),
        "self_bwd",
        [SMEM, SMEM] + [VMEM] * 14,
        [out((256, 1024)), out((256, 1024)), out((32, 1024))],
        [
            pltpu.VMEM((256, 512), LOW),
            pltpu.VMEM((512, 256), LOW),
            pltpu.VMEM((512, 256), F32),
            pltpu.VMEM((512, 256), F32),
            pltpu.VMEM((64, 256), F32),
            pltpu.VMEM((512, 1), jnp.int32),
            pltpu.VMEM((1, 512), jnp.int32),
            pltpu.VMEM((2, 32, 256), F32),
            pltpu.VMEM((2, 32, 256), LOW),
        ],
    )(ids, order, q, k, v, *grads, g0, lse, *ws, pre)


def memory_fetch(parts, bufs, sems):
    copies = [
        [
            pltpu.make_async_copy(p.at[pl.ds(256 * j, 256)], b.at[j], sems.at[4 * j + n])
            for n, (p, b) in enumerate(zip(parts, bufs))
        ]
        for j in range(2)
    ]
    for copy in copies[0] + copies[1]:
        copy.start()
    return copies


def mem_kernel(ids, m0, m1, *refs):
    parts, res, bufs, sems = refs[:4], refs[4], refs[5:9], refs[9]
    copies = memory_fetch(parts, bufs, sems)
    for j in range(2):
        for copy in copies[j]:
            copy.wait()
        for n, mem in enumerate((m0.at[pl.ds(64, 128)], m1.at[pl.ds(64, 128)])):
            res[j, n * 128 : (n + 1) * 128, :] = mm(mem, bufs, direct(j), ids).astype(LOW)


def mem_fwd(ids, m0, m1, parts):
    return call(
        mem_kernel,
        "mem_fwd",
        [SMEM] + [VMEM] * 2 + [HBM] * 4,
        [out((2, 256, 1024))],
        [pltpu.VMEM((2, 256, 1024), LOW) for p in parts] + [pltpu.SemaphoreType.DMA((8,))],
    )(ids, m0, m1, *parts)[0]


def mem_back_kernel(ids, near, far_c, far_k, far_v, *refs):
    parts, (r0, r1), bufs, (wide, sems) = refs[:4], refs[4:6], refs[6:10], refs[10:]
    copies = memory_fetch(parts, bufs, sems)
    total = [
        (near[j].astype(F32) + far_c[j].astype(F32) + far_y[...].astype(F32)).astype(LOW)
        for j, far_y in enumerate((far_k, far_v))
    ]
    for copy in copies[0] + copies[1]:
        copy.wait()
    for n, place in enumerate(DIRECT):
        wide[:, place_of(ids, place)] = nt(total[0], bufs[n][0]) + nt(total[1], bufs[n][1])
    r0[...] = wide[:128].astype(LOW)
    r1[...] = wide[128:].astype(LOW)


def mem_back(ids, near, far_c, far_k, far_v, parts):
    return call(
        mem_back_kernel,
        "mem_back",
        [SMEM] + [VMEM] * 4 + [HBM] * 4,
        [out((128, 1024)), out((128, 1024))],
        [pltpu.VMEM((2, 256, 1024), LOW) for p in parts]
        + [pltpu.VMEM((256, 1024), F32), pltpu.SemaphoreType.DMA((8,))],
    )(ids, near, far_c, far_k, far_v, *parts)


def fill_bias(bias, ids, live):
    c, y, odd = ids[10], ids[11], ids[12]
    for n in range(8):
        core = c if n < 4 else 1 - c
        line = y if n % 4 < 2 else 1 - y
        turned = odd if n % 2 == 0 else 1 - odd
        first = (2 * (2 * core + turned) + line) * 128
        slot = lax.broadcasted_iota(jnp.int32, (128, 256), 0) + first
        bias[n * 128 : (n + 1) * 128, :] = jnp.where(slot < live[0, 0], 0.0, MASKED)


def mid_fwd_kernel(count, ids, live, o0, o1, o2, o3, tok, gain, shift, pre, *refs):
    kvs, parts, refs = refs[:4], refs[4:10], refs[10:]
    cq_ref, lse_ref, unit1, inv1, h2_ref, unit2, inv2, h2l = refs[:8]
    kv, bufs, (bias, flat, wide, pre_l, sems, kv_sems) = refs[8:12], refs[12:18], refs[18:]
    fetch = Fetch(parts, bufs, sems, [shared(j, 0) for j in range(3)])
    loads = [
        pltpu.make_async_copy(kvs[n].at[j], kv[n].at[j], kv_sems.at[n, j]) for j in range(2) for n in range(4)
    ]
    fetch.start(0)
    fetch.start(1)
    for copy in loads:
        copy.start()
    fetch.start(2)
    for n, o in enumerate((o0, o1, o2, o3)):
        flat[:, cols(ids[13 + n] * 256, 256)] = o[...]
    fill_bias(bias, ids, live)
    fill_prefix(pre, wide, pre_l, count)
    fetch.wait(0)
    h1, unit, inv = ln(
        tok[...].astype(F32) + mm(flat, bufs, shared(0, 0), ids), gain[0:1], shift[0:1]
    )
    unit1[...] = unit
    inv1[...] = inv
    flat[...] = h1.astype(LOW)
    fetch.wait(1)
    cq_ref[...] = (mm(flat, bufs, shared(1, 0), ids) * SCALE).astype(LOW)
    for copy in loads:
        copy.wait()
    for p in range(8):
        lanes = slice(p * 128, (p + 1) * 128)
        got, lse = soft_pair(
            stacked(cq_ref[:, lanes]),
            pre_l[0, :, lanes],
            [kv[n][0, :, lanes] for n in range(4)],
            pre_l[1, :, lanes],
            [kv[n][1, :, lanes].T for n in range(4)],
            [bias[n * 256 : (n + 1) * 256] for n in range(4)],
            count,
        )
        flat[:, lanes] = unstacked(got, 128).astype(LOW)
        lse_ref[p] = lse
    fetch.wait(2)
    h2, unit, inv = ln(h1 + mm(flat, bufs, shared(2, 0), ids), gain[1:2], shift[1:2])
    h2_ref[...] = h2
    unit2[...] = unit
    inv2[...] = inv
    h2l[...] = h2.astype(LOW)


def mid_fwd(ids, live, os, tok, gain, shift, pre, kvs, parts, count):
    wide, thin = out((128, 1024), F32), out((128, 1), F32)
    return call(
        functools.partial(mid_fwd_kernel, count),
        "mid_fwd",
        [SMEM, SMEM] + [VMEM] * 8 + [HBM] * 10,
        [out((128, 1024)), out((8, 1, 256), F32), wide, thin, wide, wide, thin, out((128, 1024))],
        [pltpu.VMEM((2, 256, 1024), LOW)] * 4
        + [pltpu.VMEM((3, *p.shape[1:]), LOW) for p in parts]
        + [
            pltpu.VMEM((1024, 256), F32),
            pltpu.VMEM((128, 1024), LOW),
            pltpu.VMEM((2, 32, 1024), F32),
            pltpu.VMEM((2, 32, 1024), LOW),
            pltpu.SemaphoreType.DMA((18,)),
            pltpu.SemaphoreType.DMA((4, 2)),
        ],
    )(ids, live, *os, tok, gain, shift, pre, *kvs, *parts)


def mlp_kernel(matrices, ids, h2, h2l, unit2, inv2, c0, c1, gain, shift, down_b, up_b, down_any, up_any, *refs):
    count = 1 + max(n for matrix in matrices for n, _, _ in matrix)
    parts, refs = refs[:count], refs[count:]
    m0, m1, dr2, keep, give, gaub, gadb = refs[:7]
    bufs, (down, up, act, slope, acc, sems, ad_sems) = refs[7 : 7 + count], refs[7 + count :]
    fetch = Fetch(parts, bufs, sems, matrices)
    ad = [
        pltpu.make_async_copy(down_any, down, ad_sems.at[0]),
        pltpu.make_async_copy(up_any, up, ad_sems.at[1]),
    ]
    for s in range(4):
        fetch.start(s)
    for copy in ad:
        copy.start()
    for s in range(4, 8):
        fetch.start(s)
    for s in range(4):
        fetch.wait(s)
        value, gradient = gelu_both(mm(h2l, bufs, matrices[s], ids))
        lanes = slice(s * 1024, (s + 1) * 1024)
        act[:, lanes] = value.astype(LOW)
        slope[:, lanes] = gradient
    for copy in ad:
        copy.wait()
    down_w, up_w = down[...].astype(LOW), up[...].astype(LOW)
    a, a_slope = gelu_both(nn(h2l[...], down_w) + down_b[...])
    a = a.astype(LOW)
    total = h2[...] + 4.0 * (nn(a, up_w) + up_b[...])

    def rows(s, place):
        first, size = PLACES[place]
        first = first(ids)
        return cols((first // 2) * 1024 + s * 256 + (first % 2) * 128, size)

    for s in range(4):
        fetch.wait(4 + s)
        for n, index, place in matrices[4 + s]:
            total += nn(act[:, rows(s, place)], bufs[n][index])
    res, unit3, inv3 = ln(total, gain[2:3], shift[2:3])
    m0[...] = res[:64].astype(LOW)
    m1[...] = res[64:].astype(LOW)
    cot = jnp.concatenate([c0[...], c1[...]], 0).astype(F32)
    dr3 = ln_back(cot, unit3, inv3, gain[2:3])
    dffn = dr3.astype(LOW)
    dad = (4.0 * dr3).astype(LOW)
    gau = tn(a, dad)
    gaub[...] = jnp.sum(dad.astype(F32), axis=0, keepdims=True)
    ddn = (a_slope * nt(dad, up_w)).astype(LOW)
    gadb[:, :512] = jnp.sum(ddn.astype(F32), axis=0, keepdims=True)
    gadb[:, 512:] = jnp.zeros((1, 512), F32)
    gadt = tn(ddn, h2l[...])
    first_core = ids[10] == 0
    keep[...] = jnp.where(first_core, gau, gadt)
    give[...] = jnp.where(first_core, gadt, gau).astype(LOW)
    for s in range(4):
        for n, index, place in matrices[4 + s]:
            where = rows(s, place)
            act[:, where] = (slope[:, where] * nt(dffn, bufs[n][index])).astype(LOW)
    acc[...] = dr3 + nt(ddn, down_w)
    for s in range(4):
        for n, index, place in matrices[s]:
            acc[:, place_of(ids, place)] += nt(act[:, s * 1024 : (s + 1) * 1024], bufs[n][index])
    dr2[...] = ln_back(acc[...], unit2[...], inv2[...], gain[1:2])


def mlp(ids, h2, h2l, unit2, inv2, cots, gain, shift, down_b, up_b, down, up, parts, matrices):
    return call(
        functools.partial(mlp_kernel, matrices),
        "mlp",
        [SMEM] + [VMEM] * 10 + [HBM] * (2 + len(parts)),
        [
            out((64, 1024)),
            out((64, 1024)),
            out((128, 1024), F32),
            out((512, 1024), F32),
            out((512, 1024)),
            out((1, 1024), F32),
            out((1, 1024), F32),
        ],
        [pltpu.VMEM((8, *p.shape[1:]) if n < 2 else p.shape, LOW) for n, p in enumerate(parts)]
        + [
            pltpu.VMEM((1024, 512), F32),
            pltpu.VMEM((512, 1024), F32),
            pltpu.VMEM((128, 4096), LOW),
            pltpu.VMEM((128, 4096), F32),
            pltpu.VMEM((128, 1024), F32),
            pltpu.SemaphoreType.DMA((sum(len(m) for m in matrices),)),
            pltpu.SemaphoreType.DMA((2,)),
        ],
    )(ids, h2, h2l, unit2, inv2, *cots, gain, shift, down_b, up_b, down, up, *parts)


def cross_bwd_kernel(count, ids, live, dr2, cq, lse, gaub, gadb, pre, *refs):
    kvs, parts, refs = refs[:4], refs[4:10], refs[10:]
    grads, (dcq, *sums) = refs[:4], refs[4:9]
    kv, bufs, (bias, flat, wide, wide_pre, pre_l, gpre, sems, kv_sems) = refs[9:13], refs[13:19], refs[19:]
    copies = [
        pltpu.make_async_copy(parts[n].at[2], bufs[n], sems.at[n]) for n in range(6)
    ]
    loads = [
        pltpu.make_async_copy(kvs[n].at[j], kv[n].at[j], kv_sems.at[n, j]) for j in range(2) for n in range(4)
    ]
    for copy in copies + loads:
        copy.start()
    fill_bias(bias, ids, live)
    fill_prefix(pre, wide_pre, pre_l, count)
    for copy in copies:
        copy.wait()
    value = dr2[...].astype(LOW)
    for n, place in enumerate(SHARED):
        wide[:, place_of(ids, place)] = nt(value, bufs[n][...])
    flat[...] = wide[...].astype(LOW)
    for copy in loads:
        copy.wait()
    for p in range(8):
        lanes = slice(p * 128, (p + 1) * 128)
        g, gk, gv = soft_pair_back(
            stacked(cq[:, lanes]),
            stacked(flat[:, lanes]),
            lse[p],
            pre_l[0, :, lanes],
            pre_l[1, :, lanes],
            [kv[n][0, :, lanes] for n in range(4)],
            [kv[n][1, :, lanes] for n in range(4)],
            [kv[n][0, :, lanes].T for n in range(4)],
            [bias[n * 256 : (n + 1) * 256] for n in range(4)],
            count,
        )
        for j, got in enumerate((gk, gv)):
            gpre[j, :, lanes] = got[0]
            for n in range(4):
                grads[n][j, :, lanes] = got[1 + n].astype(LOW)
        dcq[:, lanes] = unstacked(g, 128).astype(LOW)
    gpre[0, count : count + 1, :] = gaub[...]
    gpre[1, count : count + 1, :] = gadb[...]
    for j in range(2):
        rows = slice(32 * j, 32 * (j + 1))
        for n, dst in enumerate(sums):
            dst[rows, :] = gpre[j, :, cols(ids[13 + n] * 256, 256)].astype(dst.dtype)


def cross_bwd(ids, live, dr2, cq, lse, gaub, gadb, pre, kvs, parts, count):
    grad = out((2, 256, 1024))
    return call(
        functools.partial(cross_bwd_kernel, count),
        "cross_bwd",
        [SMEM, SMEM] + [VMEM] * 6 + [HBM] * 10,
        [grad, grad, grad, grad, out((128, 1024)), out((64, 256), F32)] + [out((64, 256))] * 3,
        [pltpu.VMEM((2, 256, 1024), LOW)] * 4
        + [pltpu.VMEM(p.shape[1:], LOW) for p in parts]
        + [
            pltpu.VMEM((1024, 256), F32),
            pltpu.VMEM((128, 1024), LOW),
            pltpu.VMEM((128, 1024), F32),
            pltpu.VMEM((2, 32, 1024), F32),
            pltpu.VMEM((2, 32, 1024), LOW),
            pltpu.VMEM((2, 32, 1024), F32),
            pltpu.SemaphoreType.DMA((6,)),
            pltpu.SemaphoreType.DMA((4, 2)),
        ],
    )(ids, live, dr2, cq, lse, gaub, gadb, pre, *kvs, *parts)


def query_bwd_kernel(ids, dr2, dcq, unit1, inv1, gain, g1, g2, g3, *refs):
    parts, (dr1, *grads), rest = refs[:6], refs[6:11], refs[11:]
    bufs, (wide, sems) = rest[:6], rest[6:]
    fetch = Fetch(parts, bufs, sems, [shared(1, 0), shared(0, 0)])
    fetch.start(0)
    fetch.start(1)
    fetch.wait(0)
    mm_back(dcq[...], bufs, shared(1, 0), ids, wide)
    grad = ln_back(dr2[...] + SCALE * wide[...], unit1[...], inv1[...], gain[0:1])
    dr1[...] = grad
    fetch.wait(1)
    mm_back(grad.astype(LOW), bufs, shared(0, 0), ids, wide)
    for dst, g in zip(grads[1:], (g1, g2, g3)):
        dst[128:, :] = g[...]
    for n, dst in enumerate(grads):
        dst[:128, :] = wide[:, cols(ids[13 + n] * 256, 256)].astype(LOW)


def query_bwd(ids, dr2, dcq, unit1, inv1, gain, sums, parts):
    return call(
        query_bwd_kernel,
        "query_bwd",
        [SMEM] + [VMEM] * 8 + [HBM] * 6,
        [out((128, 1024), F32), out((128, 256))] + [out((192, 256))] * 3,
        [pltpu.VMEM((2, *p.shape[1:]), LOW) for p in parts]
        + [pltpu.VMEM((128, 1024), F32), pltpu.SemaphoreType.DMA((12,))],
    )(ids, dr2, dcq, unit1, inv1, gain, *sums, *parts)


def quarters(ids, bits, size, start=0):
    first, second = ids[bits[0]], ids[bits[1]]
    pairs = ((first, second), (1 - first, second), (first, 1 - second), (1 - first, 1 - second))
    return [pl.ds(pl.multiple_of(start + (2 * a + b) * size, size), size) for a, b in pairs]


def halve_kernel(bits, count, ids, keep, *refs):
    gots, outs = refs[:count], refs[count:]
    for dst, rows in zip(outs, quarters(ids, bits, outs[0].shape[0])):
        total = keep[rows, :]
        for got in gots:
            total += got[rows, :].astype(F32)
        dst[...] = total.astype(dst.dtype)


def halve(ids, bits, keep, gots):
    size = keep.shape[0] // 4
    return call(
        functools.partial(halve_kernel, bits, len(gots)),
        "halve",
        [SMEM] + [VMEM] * (1 + len(gots)),
        [out((size, 1024), F32)] + [out((size, 1024))] * 3,
    )(ids, keep, *gots)


def mix_kernel(keep, part, g1, g2, g3, dst):
    dst[:32, :] = (
        keep[...] + g1[...].astype(F32) + g2[...].astype(F32) + g3[...].astype(F32)
    ).astype(LOW)
    dst[32:, :] = part[...]


def join_kernel(bits, ids, *refs):
    parts, dst = refs[:4], refs[4]
    for part, rows in zip(parts, quarters(ids, bits, 32)):
        dst[rows, :] = part[:32, :]
    own, other_y, other_z, both = (part[32:, :].astype(F32) for part in parts)
    dst[128:160, :] = (own + other_z).astype(LOW)
    dst[160:, :] = (other_y + both).astype(LOW)


def join_last_kernel(bits, ids, p0, p1, p2, p3, dst, wide):
    parts = (p0, p1, p2, p3)
    for part, rows in zip(parts, quarters(ids, bits, 128)):
        dst[rows, :] = part[:128, :]
    for part, rows in zip(parts, quarters(ids, bits, 64)):
        wide[rows, :] = part[128:, :].astype(F32)
    dst[512:, :] = (wide[:64] + wide[64:128] + wide[128:192] + wide[192:]).astype(LOW)


def totals_kernel(count, ids, mine, got, gau, gad, gps, gpc, gaub, gadb, wide):
    first_core = ids[10] == 0
    gau[...] = jnp.where(first_core, mine[:512], got[:512]).astype(F32)
    gad[...] = jnp.where(first_core, got[:512], mine[:512]).astype(F32).T
    for n in range(4):
        rows = (mine, got)[n // 2][512 + 32 * (n % 2) : 544 + 32 * (n % 2), :].astype(F32)
        for a in range(4):
            wide[32 * a : 32 * a + 32, cols(ids[13 + n] * 256, 256)] = rows[:, 256 * a : 256 * a + 256]
    for j in range(2):
        gps[j] = wide[32 * j : 32 * j + count, :]
        gpc[j] = wide[64 + 32 * j : 64 + 32 * j + count, :]
    gaub[...] = wide[64 + count : 65 + count, :]
    gadb[...] = wide[96 + count : 97 + count, :512]


AXES = ("x", "core", "pair", "z", "y")


def pairs_of(target):
    pairs = []
    for source in range(32):
        row, seq = divmod(source, 8)
        x, c, z, y = target(*divmod(row, 2), *divmod(seq, 2))
        pairs.append((source, (2 * x + c) * 8 + 2 * z + y))
    return pairs


SWAP_X = pairs_of(lambda x, c, z, y: (1 - x, c, z, y))
SWAP_C = pairs_of(lambda x, c, z, y: (x, 1 - c, z, y))
SWAP_Y = pairs_of(lambda x, c, z, y: (x, c, z, 1 - y))
SWAP_CY = pairs_of(lambda x, c, z, y: (x, 1 - c, z, 1 - y))
SWAP_Z = pairs_of(lambda x, c, z, y: (x, c, z ^ 1, y))
SWAP_PAIRS = pairs_of(lambda x, c, z, y: (x, c, z ^ 2, y))
SQUARE = (
    ((17, 18), (SWAP_X, SWAP_Z, pairs_of(lambda x, c, z, y: (1 - x, c, z ^ 1, y)))),
    ((20, 19), (SWAP_Y, SWAP_PAIRS, pairs_of(lambda x, c, z, y: (x, c, z ^ 2, 1 - y)))),
)
TURN = [pairs_of(lambda x, c, z, y, r=r: (x, z // 2, 2 * c + (z + r) % 2, y)) for r in range(2)]


def send(value, pairs):
    return lax.ppermute(value, AXES, pairs)


def local_pairs(
    tokens,
    memory,
    source_len,
    bucket_order,
    prefix_self,
    prefix_cross,
    self_query,
    self_kv,
    self_out,
    cross_query,
    cross_kv,
    cross_out,
    fc_in,
    fc_out,
    ln_gain,
    ln_bias,
    ad_down,
    ad_down_bias,
    ad_up,
    ad_up_bias,
    cotangent,
):
    f32 = F32
    x, c, odd, y = (lax.axis_index(name) for name in ("x", "core", "z", "y"))
    z = 2 * lax.axis_index("pair") + odd
    row = 2 * x + c
    count = prefix_self.shape[1]
    group = 2 * y + c
    far_row, both_row = 2 * (row ^ 2), 2 * (row ^ 3)
    ids = jnp.stack(
        [row, row ^ 1, row ^ 2, row ^ 3]
        + [2 * row, 2 * (row ^ 1), far_row + odd, far_row + 1 - odd, both_row + odd, both_row + 1 - odd]
        + [c, y, odd]
        + [group, group ^ 2, group ^ 1, group ^ 3]
        + [x, odd, z // 2, y]
        + [far_row + y, far_row + 1 - y, both_row + y, both_row + 1 - y]
    ).astype(jnp.int32)

    def after(value, *others):
        if isinstance(value, tuple):
            return lax.optimization_barrier((*value, *others))[: len(value)]
        return lax.optimization_barrier((value, *others))[0]

    def turn_out(first, second):
        first, second = send(first, TURN[0]), send(second, TURN[1])
        return jnp.stack([jnp.where(odd == 1, second, first), jnp.where(odd == 1, first, second)])

    blocks = inbound(ids, tokens, memory)
    first, second = (send(block, turn) for block, turn in zip(blocks, TURN))
    one = pack_first(after(ids, blocks[0]), self_query, self_kv, cross_kv)
    one_far, one_c = send(one, SWAP_X), send(one, SWAP_C)
    live = send(jnp.where(odd == 1, source_len[1], source_len[0]).reshape(1, 1), TURN[0])
    tok = call(
        tokens_kernel, "tokens", [VMEM, VMEM], [out((128, 1024))], [pltpu.SemaphoreType.DMA((2,))]
    )(after(first, one_c, live), second)[0]
    tok_y, tok_c = send(tok, SWAP_Y), send(tok, SWAP_C)
    toks = (tok, tok_y, tok_c, send(tok_y, SWAP_C))
    mid_own, ffn_own, mid_half, in_half, out_half, out_whole = pack(
        after(ids, tok),
        [(n, None, 0, 0, 0, n, 2, n, 12) for n in range(3)]
        + [(3, None, 0, 1024 * n, 1, n, 3, n, 12) for n in range(4)]
        + [(4, None, 256 * n, 0, 1, 4 + n, 4, n, 11) for n in range(2)]
        + [(4, None, 256 * n, 0, 1, 4 + n, 5, n - 2, None) for n in range(2, 4)],
        [
            (3, 256, 1024),
            (8, 256, 1024),
            (3, 128, 1024),
            (4, 128, 1024),
            (2, 128, 1024),
            (2, 256, 1024),
        ],
        self_out,
        cross_query,
        cross_out,
        fc_in,
        fc_out,
    )
    mid_near = send(mid_half, SWAP_X)
    mid_c = send(mid_own, SWAP_C)
    in_near = send(after(in_half, one_far), SWAP_X)

    one_parts = (one, one_c, one_far, send(after(one_far, toks[3], mid_half), SWAP_C))
    q, k, v, o0, o1, o2, o3, self_lse = self_fwd(
        ids, bucket_order, after(toks, mid_c), one_parts, prefix_self, count
    )
    os = (o0, send(o1, SWAP_Y), send(o2, SWAP_C), send(o3, SWAP_CY))
    mkv = mem_fwd(ids, after(first, q), second, one_parts)
    mkv_y = send(after(mkv, *os), SWAP_Y)
    mkv_c = send(mkv, SWAP_C)
    out_near = send(after(out_half, *os), SWAP_X)
    ffn_c = send(after(ffn_own, mkv), SWAP_C)
    mid_near_o = after(mid_near, *os)
    mid_other = send(mid_near_o, SWAP_Z)
    mid_parts = (mid_own, mid_c, mid_near, mid_other, send(after(mid_near, mkv_y), SWAP_C), send(mid_other, SWAP_C))
    in_other = send(after(in_near, mid_other), SWAP_Z)
    kvs = (mkv, mkv_y, mkv_c, send(mkv_y, SWAP_C))

    cq, cross_lse, unit1, inv1, h2, unit2, inv2, h2l = mid_fwd(
        ids, live, os, tok, ln_gain, ln_bias, prefix_cross, kvs, mid_parts, count
    )
    cot = [jnp.where(odd == 1, cotangent[1 - n], cotangent[n]) for n in range(2)]
    cots = [send(after(v, h2l), t) for v, t in zip(cot, TURN)]
    out_far = send(after(out_whole, kvs[3]), SWAP_X)
    in_near_l, out_near_l = after((in_near, out_near), h2l)
    out_other = send(out_near_l, SWAP_Y)
    ffn_parts = [ffn_own, ffn_c, in_near, in_other]
    ffn_parts += [send(t, SWAP_C) for t in (in_near_l, in_other)]
    ffn_parts += [out_near, out_other]
    ffn_parts += [send(t, SWAP_C) for t in (out_near_l, out_other)]
    ffn_parts += [out_far, send(out_far, SWAP_C)]
    matrices = [[(0, m, "own"), (1, m, "core")] for m in range(8)]
    for m in range(4):
        matrices[m] += [(2 + k, m, place) for k, place in enumerate(SHARED[2:])]
    for m in range(2):
        matrices[4 + m] += [(6 + k, m, place + "_y") for k, place in enumerate(SHARED[2:])]
        matrices[6 + m] += [(10, m, "far"), (11, m, "core_far")]
    m0, m1, dr2, keep, give, gaub, gadb = mlp(
        ids,
        h2,
        h2l,
        unit2,
        inv2,
        cots,
        ln_gain,
        ln_bias,
        ad_down_bias[None],
        ad_up_bias[None],
        ad_down,
        ad_up,
        ffn_parts,
        matrices,
    )
    mixed = turn_out(m0, m1)

    parts = [send(give, SWAP_C)]
    n0, n1, f0, f1, dcq, g0, *gs = cross_bwd(
        ids, live, dr2, cq, cross_lse, gaub, gadb, prefix_cross, kvs, mid_parts, count
    )
    far_c, near_c = send(f1, SWAP_C), send(f0, SWAP_C)
    bits, pairs = SQUARE[0]
    keep, *gives = halve(ids, bits, after(keep, dcq), parts)
    parts = [send(g, p) for g, p in zip(gives, pairs)]
    dr1, d0, d1, d2, d3 = query_bwd(ids, dr2, after(dcq, *gives), unit1, inv1, ln_gain, gs, mid_parts)
    grads = (d0, send(d1, SWAP_Y), send(d2, SWAP_C), send(d3, SWAP_CY))
    mem_k, mem_v = [
        (n1[n].astype(f32) + after(far_c, d0)[n].astype(f32)).astype(LOW) for n in range(2)
    ]
    far_k = send(after(mem_k, *grads), SWAP_Y)
    bits, pairs = SQUARE[1]
    keep, *gives = halve(ids, bits, keep, parts)
    parts = [send(g, p) for g, p in zip(gives, pairs)]
    near, far_part, part = self_bwd(
        ids,
        bucket_order,
        after(q, mem_k, mem_v, mixed, near_c),
        k,
        v,
        grads,
        g0,
        self_lse,
        one_parts,
        prefix_self,
        count,
    )
    got_c = send(after(far_part, far_k), SWAP_C)
    far_v = send(mem_v, SWAP_Y)
    mine = call(mix_kernel, "mix", [VMEM] * 5, [out((64, 1024))])(keep, part, *parts)[0]
    parts = [send(mine, p) for p in pairs]

    give_y = (near[128:].astype(f32) + got_c[128:].astype(f32)).astype(LOW)
    d_own = dr1 + near[:128].astype(f32) + got_c[:128].astype(f32)
    d_own = (d_own + send(give_y, SWAP_Y).astype(f32)).astype(LOW)
    d_tokens = turn_out(d_own[:64], d_own[64:])

    d_memory = turn_out(*mem_back(ids, n0, near_c, far_k, far_v, one_parts))

    whole = call(
        functools.partial(join_kernel, bits), "join", [SMEM] + [VMEM] * 4, [out((192, 1024))]
    )(ids, mine, *parts)[0]
    bits, pairs = SQUARE[0]
    parts = [send(whole, p) for p in pairs]
    whole = call(
        functools.partial(join_last_kernel, bits),
        "join",
        [SMEM] + [VMEM] * 4,
        [out((576, 1024))],
        [pltpu.VMEM((256, 1024), F32)],
    )(ids, whole, *parts)[0]
    grad_up, grad_down, grad_ps, grad_pc, grad_ub, grad_db = call(
        functools.partial(totals_kernel, count),
        "totals",
        [SMEM, VMEM, VMEM],
        [
            out((512, 1024), F32),
            out((1024, 512), F32),
            out(prefix_self.shape, F32),
            out(prefix_cross.shape, F32),
            out((1, 1024), F32),
            out((1, 512), F32),
        ],
        [pltpu.VMEM((128, 1024), F32)],
    )(ids, whole, send(whole, SWAP_C))
    return (
        mixed,
        d_tokens,
        d_memory,
        grad_ps,
        grad_pc,
        grad_down,
        grad_db[0],
        grad_up,
        grad_ub[0],
    )


def solution(mesh):
    in_specs = (
        P("row", "seq", None),
        P("row", "seq", None),
        P("row"),
        P(),
        P(),
        P(),
        P("row", None),
        P(None, "row", None),
        P("row", None),
        P("row", None),
        P(None, "row", None),
        P("row", None),
        P("row", None),
        P("row", None),
        P(),
        P(),
        P(),
        P(),
        P(),
        P(),
        P("row", "seq", None),
    )
    out_specs = (
        P("row", "seq", None),
        P("row", "seq", None),
        P("row", "seq", None),
        P(),
        P(),
        P(),
        P(),
        P(),
        P(),
    )
    if (mesh.shape["row"], mesh.shape["seq"]) != (4, 8):
        return jax.shard_map(
            local_rows, mesh=mesh, in_specs=in_specs, out_specs=out_specs, check_vma=False
        )
    fine = jax.sharding.Mesh(mesh.devices.reshape(2, 2, 2, 2, 2), AXES)
    split = {"row": ("x", "core"), "seq": ("pair", "z", "y")}

    def renamed(specs):
        return tuple(P(*(split.get(name) for name in spec)) for spec in specs)

    return jax.shard_map(
        local_pairs, mesh=fine, in_specs=renamed(in_specs), out_specs=renamed(out_specs), check_vma=False
    )
```

```python
import functools

import jax
import jax.numpy as jnp
from jax import lax
from jax.experimental import pallas as pl
from jax.experimental.pallas import tpu as pltpu
from jax.sharding import PartitionSpec as P

H = 16
HD = 64


EPSILON = 1e-05
MASKED = -1e30


def normalize(value, gain, shift):
    centre = value - jnp.mean(value, axis=-1, keepdims=True)
    inv_dev = lax.rsqrt(jnp.mean(centre * centre, axis=-1, keepdims=True) + EPSILON)
    unit_val = centre * inv_dev
    return (unit_val * gain + shift, unit_val, inv_dev)


def normalize_back(grad, unit_val, inv_dev, gain):
    scaled = grad * gain
    return inv_dev * (
        scaled
        - jnp.mean(scaled, axis=-1, keepdims=True)
        - unit_val * jnp.mean(scaled * unit_val, axis=-1, keepdims=True)
    )


def gelu_exact(value):
    return jax.nn.gelu(value, approximate=False)


def gelu_back(value, grad):
    return jax.vjp(gelu_exact, value)[1](grad)[0]


def head_split(matrix):
    return matrix.reshape(matrix.shape[0], -1, HD)


def masked_scores(queries, keys, mask):
    scores = jnp.einsum(
        "qhd,khd->hqk", head_split(queries), head_split(keys), preferred_element_type=jnp.float32
    )
    return jnp.where(mask[None], scores, MASKED)


def attend(queries, keys, values, mask):
    scores = masked_scores(queries, keys, mask)
    top_score = jnp.max(scores, axis=-1, keepdims=True)
    log_total = top_score + jnp.log(jnp.sum(jnp.exp(scores - top_score), axis=-1, keepdims=True))
    probs = jnp.exp(scores - log_total).astype(jnp.bfloat16)
    result = jnp.einsum(
        "hqk,khd->qhd", probs, head_split(values), preferred_element_type=jnp.float32
    )
    return (result.reshape(queries.shape[0], -1), log_total)


def attend_back(queries, keys, values, mask, log_total, grad_out):
    probs = jnp.exp(masked_scores(queries, keys, mask) - log_total)
    grad_heads = head_split(grad_out)
    grad_probs = jnp.einsum(
        "qhd,khd->hqk", grad_heads, head_split(values), preferred_element_type=jnp.float32
    )
    row_delta = jnp.sum(probs * grad_probs, axis=-1, keepdims=True)
    grad_scores = (probs * (grad_probs - row_delta)).astype(jnp.bfloat16)
    grad_query = jnp.einsum(
        "hqk,khd->qhd", grad_scores, head_split(keys), preferred_element_type=jnp.float32
    )
    grad_keys = jnp.einsum(
        "hqk,qhd->khd", grad_scores, head_split(queries), preferred_element_type=jnp.float32
    )
    grad_values = jnp.einsum(
        "hqk,qhd->khd", probs.astype(jnp.bfloat16), grad_heads, preferred_element_type=jnp.float32
    )
    return (
        grad_query.reshape(queries.shape[0], -1),
        grad_keys.reshape(keys.shape[0], -1),
        grad_values.reshape(values.shape[0], -1),
    )


def project(left, right):
    return jnp.dot(left, right, preferred_element_type=jnp.float32)


def local_rows(
    tokens,
    memory,
    source_len,
    bucket_order,
    prefix_self,
    prefix_cross,
    self_query,
    self_kv,
    self_out,
    cross_query,
    cross_kv,
    cross_out,
    fc_in,
    fc_out,
    ln_gain,
    ln_bias,
    ad_down,
    ad_down_bias,
    ad_up,
    ad_up_bias,
    cotangent,
):
    low_type = jnp.bfloat16
    row_count, tok_count, width = tokens.shape
    slot_count = memory.shape[1]
    prefix_count = prefix_self.shape[1]
    half_len = tok_count // 2
    scale = HD ** (-0.5)
    weight_set = (
        lax.all_gather(self_query.astype(low_type), "row", axis=0, tiled=True),
        lax.all_gather(self_kv.astype(low_type), "row", axis=1, tiled=True),
        lax.all_gather(self_out.astype(low_type), "row", axis=0, tiled=True),
        lax.all_gather(cross_query.astype(low_type), "row", axis=0, tiled=True),
        lax.all_gather(cross_kv.astype(low_type), "row", axis=1, tiled=True),
        lax.all_gather(cross_out.astype(low_type), "row", axis=0, tiled=True),
        lax.all_gather(fc_in.astype(low_type), "row", axis=0, tiled=True),
        lax.all_gather(fc_out.astype(low_type), "row", axis=0, tiled=True),
    )
    q_weight, kv_weight, o_weight, cq_weight, ckv_weight, co_weight, in_weight, out_weight = (
        weight_set
    )
    place = lax.axis_index("seq")
    offsets = jnp.arange(half_len, dtype=jnp.int32)
    all_pos = (bucket_order[:, None] * half_len + offsets[None, :]).reshape(-1)
    own_pos = lax.dynamic_slice_in_dim(all_pos, place * tok_count, tok_count)
    self_mask = jnp.concatenate(
        [jnp.ones((tok_count, prefix_count), jnp.bool_), all_pos[None, :] <= own_pos[:, None]],
        axis=1,
    )
    flat_tokens = tokens.reshape(-1, width)
    queries = (project(flat_tokens, q_weight) * scale).astype(low_type)
    own_keys = (
        project(flat_tokens, kv_weight[0]).astype(low_type).reshape(row_count, tok_count, width)
    )
    own_values = (
        project(flat_tokens, kv_weight[1]).astype(low_type).reshape(row_count, tok_count, width)
    )
    flat_memory = memory.reshape(-1, width)
    mem_keys = (
        project(flat_memory, ckv_weight[0]).astype(low_type).reshape(row_count, slot_count, width)
    )
    mem_values = (
        project(flat_memory, ckv_weight[1]).astype(low_type).reshape(row_count, slot_count, width)
    )
    all_keys, all_values, all_mkeys, all_mvalues = (
        lax.all_gather(own_keys, "seq", axis=1, tiled=True),
        lax.all_gather(own_values, "seq", axis=1, tiled=True),
        lax.all_gather(mem_keys, "seq", axis=1, tiled=True),
        lax.all_gather(mem_values, "seq", axis=1, tiled=True),
    )
    src_total = all_mkeys.shape[1]
    pre_self = prefix_self.astype(low_type)
    pre_cross = prefix_cross.astype(low_type)
    self_key_sets = [
        jnp.concatenate([pre_self[0], all_keys[row_index]], 0) for row_index in range(row_count)
    ]
    self_value_sets = [
        jnp.concatenate([pre_self[1], all_values[row_index]], 0) for row_index in range(row_count)
    ]
    cross_key_sets = [
        jnp.concatenate([pre_cross[0], all_mkeys[row_index]], 0) for row_index in range(row_count)
    ]
    cross_value_sets = [
        jnp.concatenate([pre_cross[1], all_mvalues[row_index]], 0) for row_index in range(row_count)
    ]
    slot_number = jnp.arange(src_total, dtype=jnp.int32)
    cross_masks = [
        jnp.concatenate(
            [jnp.ones((prefix_count,), jnp.bool_), slot_number < source_len[row_index]]
        )[None, :]
        for row_index in range(row_count)
    ]

    def rows_of(matrix, row_index):
        return matrix[row_index * tok_count : (row_index + 1) * tok_count]

    self_parts = [
        attend(
            rows_of(queries, row_index),
            self_key_sets[row_index],
            self_value_sets[row_index],
            self_mask,
        )
        for row_index in range(row_count)
    ]
    attended = jnp.concatenate([part[0] for part in self_parts], 0).astype(low_type)
    resid_one = flat_tokens.astype(jnp.float32) + project(attended, o_weight)
    hidden_one, unit_one, inv_one = normalize(resid_one, ln_gain[0], ln_bias[0])
    cross_queries = (project(hidden_one.astype(low_type), cq_weight) * scale).astype(low_type)
    cross_parts = [
        attend(
            rows_of(cross_queries, row_index),
            cross_key_sets[row_index],
            cross_value_sets[row_index],
            cross_masks[row_index],
        )
        for row_index in range(row_count)
    ]
    cross_att = jnp.concatenate([part[0] for part in cross_parts], 0).astype(low_type)
    resid_two = hidden_one + project(cross_att, co_weight)
    hidden_two, unit_two, inv_two = normalize(resid_two, ln_gain[1], ln_bias[1])
    hidden_low = hidden_two.astype(low_type)
    up_proj = project(hidden_low, in_weight)
    activated = gelu_exact(up_proj).astype(low_type)
    ffn_out = project(activated, out_weight)
    down_weight = ad_down.astype(low_type)
    up_weight = ad_up.astype(low_type)
    down_proj = project(hidden_low, down_weight) + ad_down_bias
    down_act = gelu_exact(down_proj).astype(low_type)
    adapted = project(down_act, up_weight) + ad_up_bias
    resid_three = hidden_two + ffn_out + 4.0 * adapted
    output, unit_three, inv_three = normalize(resid_three, ln_gain[2], ln_bias[2])
    mixed = output.astype(low_type).reshape(row_count, tok_count, width)
    weight_set = (
        lax.all_gather(self_query.astype(low_type), "row", axis=0, tiled=True),
        lax.all_gather(self_kv.astype(low_type), "row", axis=1, tiled=True),
        lax.all_gather(self_out.astype(low_type), "row", axis=0, tiled=True),
        lax.all_gather(cross_query.astype(low_type), "row", axis=0, tiled=True),
        lax.all_gather(cross_kv.astype(low_type), "row", axis=1, tiled=True),
        lax.all_gather(cross_out.astype(low_type), "row", axis=0, tiled=True),
        lax.all_gather(fc_in.astype(low_type), "row", axis=0, tiled=True),
        lax.all_gather(fc_out.astype(low_type), "row", axis=0, tiled=True),
    )
    q_weight, kv_weight, o_weight, cq_weight, ckv_weight, co_weight, in_weight, out_weight = (
        weight_set
    )
    grad_out = cotangent.astype(jnp.float32).reshape(-1, width)
    grad_three = normalize_back(grad_out, unit_three, inv_three, ln_gain[2])
    grad_ffn = grad_three.astype(low_type)
    grad_adapt = (4.0 * grad_three).astype(low_type)
    grad_up_w = jnp.einsum("na,nd->ad", down_act, grad_adapt, preferred_element_type=jnp.float32)
    grad_up_b = jnp.sum(grad_adapt.astype(jnp.float32), axis=0)
    grad_down = gelu_back(down_proj, project(grad_adapt, up_weight.T)).astype(low_type)
    grad_down_w = jnp.einsum("nd,na->da", hidden_low, grad_down, preferred_element_type=jnp.float32)
    grad_down_b = jnp.sum(grad_down.astype(jnp.float32), axis=0)
    grad_inner = gelu_back(up_proj, project(grad_ffn, out_weight.T)).astype(low_type)
    grad_hidden_two = (
        grad_three + project(grad_inner, in_weight.T) + project(grad_down, down_weight.T)
    )
    grad_two = normalize_back(grad_hidden_two, unit_two, inv_two, ln_gain[1])
    grad_cross_att = project(grad_two.astype(low_type), co_weight.T).astype(low_type)
    cross_grads = [
        attend_back(
            rows_of(cross_queries, row_index),
            cross_key_sets[row_index],
            cross_value_sets[row_index],
            cross_masks[row_index],
            cross_parts[row_index][1],
            rows_of(grad_cross_att, row_index),
        )
        for row_index in range(row_count)
    ]
    grad_cq = jnp.concatenate([part[0] for part in cross_grads], 0).astype(low_type)
    grad_hidden_one = grad_two + project(grad_cq, cq_weight.T) * scale
    grad_one = normalize_back(grad_hidden_one, unit_one, inv_one, ln_gain[0])
    grad_attended = project(grad_one.astype(low_type), o_weight.T).astype(low_type)
    self_grads = [
        attend_back(
            rows_of(queries, row_index),
            self_key_sets[row_index],
            self_value_sets[row_index],
            self_mask,
            self_parts[row_index][1],
            rows_of(grad_attended, row_index),
        )
        for row_index in range(row_count)
    ]
    pre_self_grad = jnp.stack(
        [
            sum((part[1][:prefix_count] for part in self_grads)),
            sum((part[2][:prefix_count] for part in self_grads)),
        ]
    )
    pre_cross_grad = jnp.stack(
        [
            sum((part[1][:prefix_count] for part in cross_grads)),
            sum((part[2][:prefix_count] for part in cross_grads)),
        ]
    )
    summed = [
        (
            lax.psum_scatter(
                self_grads[row_index][1][prefix_count:].astype(jnp.bfloat16),
                "seq",
                scatter_dimension=0,
                tiled=True,
            ).astype(jnp.float32),
            lax.psum_scatter(
                self_grads[row_index][2][prefix_count:].astype(jnp.bfloat16),
                "seq",
                scatter_dimension=0,
                tiled=True,
            ).astype(jnp.float32),
            lax.psum_scatter(
                cross_grads[row_index][1][prefix_count:].astype(jnp.bfloat16),
                "seq",
                scatter_dimension=0,
                tiled=True,
            ).astype(jnp.float32),
            lax.psum_scatter(
                cross_grads[row_index][2][prefix_count:].astype(jnp.bfloat16),
                "seq",
                scatter_dimension=0,
                tiled=True,
            ).astype(jnp.float32),
        )
        for row_index in range(row_count)
    ]
    key_grad = jnp.stack([part[0] for part in summed])
    value_grad = jnp.stack([part[1] for part in summed])
    mkey_grad = jnp.stack([part[2] for part in summed])
    mvalue_grad = jnp.stack([part[3] for part in summed])
    grad_query = jnp.concatenate([part[0] for part in self_grads], 0).astype(low_type)
    d_tokens = (
        grad_one
        + project(grad_query, q_weight.T) * scale
        + project(key_grad.astype(low_type).reshape(-1, width), kv_weight[0].T)
        + project(value_grad.astype(low_type).reshape(-1, width), kv_weight[1].T)
    )
    d_memory = project(mkey_grad.astype(low_type).reshape(-1, width), ckv_weight[0].T) + project(
        mvalue_grad.astype(low_type).reshape(-1, width), ckv_weight[1].T
    )
    totals = lax.psum(
        (pre_self_grad, pre_cross_grad, grad_down_w, grad_down_b, grad_up_w, grad_up_b),
        ("row", "seq"),
    )
    return (
        mixed,
        d_tokens.astype(low_type).reshape(row_count, tok_count, width),
        d_memory.astype(low_type).reshape(row_count, slot_count, width),
        totals[0],
        totals[1],
        totals[2],
        totals[3],
        totals[4],
        totals[5],
    )


LOW = jnp.bfloat16
F32 = jnp.float32
SCALE = 0.125
VMEM = pl.BlockSpec(memory_space=pltpu.VMEM)
SMEM = pl.BlockSpec(memory_space=pltpu.SMEM)
HBM = pl.BlockSpec(memory_space=pltpu.HBM)


def shape_of(shape, dtype=LOW):
    return jax.ShapeDtypeStruct(shape, dtype)


def nn(left, right):
    return jnp.dot(left, right, preferred_element_type=F32)


def nt(left, right):
    return lax.dot_general(left, right, (((1,), (1,)), ((), ())), preferred_element_type=F32)


def tn(left, right):
    return lax.dot_general(left, right, (((0,), (0,)), ((), ())), preferred_element_type=F32)


def cols(start, size):
    return pl.ds(pl.multiple_of(start, 128), size)


def ln(value, gain, shift):
    centre = value - jnp.mean(value, axis=-1, keepdims=True)
    inv = lax.rsqrt(jnp.mean(centre * centre, axis=-1, keepdims=True) + EPSILON)
    unit = centre * inv
    return unit * gain + shift, unit, inv


def ln_back(grad, unit, inv, gain):
    scaled = grad * gain
    return inv * (
        scaled
        - jnp.mean(scaled, axis=-1, keepdims=True)
        - unit * jnp.mean(scaled * unit, axis=-1, keepdims=True)
    )


def gelu_both(value):
    cdf = 0.5 * (1.0 + lax.erf(value * 0.7071067811865476))
    return value * cdf, cdf + value * (jnp.exp(-0.5 * value * value) * 0.3989422804014327)


def stacked(block):
    first = lax.broadcasted_iota(jnp.int32, block.shape, 1) < 64
    zero = jnp.zeros_like(block)
    return jnp.concatenate([jnp.where(first, block, zero), jnp.where(first, zero, block)], 0)


def unstacked(both, n):
    return jnp.concatenate([both[:64, :n], both[64:, n:]], 0).T


def pre_mask(shape, count):
    return lax.broadcasted_iota(jnp.int32, shape, 0) < count


def soft_pair(qs, k_pre, k_blocks, v_pre, vt_blocks, biases, count):
    s_pre = nt(k_pre, qs)
    s_pre = jnp.where(pre_mask(s_pre.shape, count), s_pre, MASKED)
    s_blocks = [nt(k, qs) + b for k, b in zip(k_blocks, biases)]
    top = jnp.max(s_pre, axis=0, keepdims=True)
    for s in s_blocks:
        top = jnp.maximum(top, jnp.max(s, axis=0, keepdims=True))
    e_pre = jnp.exp(s_pre - top)
    total = jnp.sum(e_pre, axis=0, keepdims=True)
    out = tn(v_pre, e_pre.astype(LOW))
    for s, vt in zip(s_blocks, vt_blocks):
        e = jnp.exp(s - top)
        total += jnp.sum(e, axis=0, keepdims=True)
        out += nn(vt, e.astype(LOW))
    return out * (1.0 / total), top + jnp.log(total)


def soft_pair_back(qs, dos, lse, k_pre, v_pre, ks, vs, kts, biases, count):
    s_pre = nt(k_pre, qs)
    p_pre = jnp.where(pre_mask(s_pre.shape, count), jnp.exp(s_pre - lse), 0.0)
    d_pre = nt(v_pre, dos)
    delta = jnp.sum(p_pre * d_pre, axis=0, keepdims=True)
    ps, ds = [], []
    for k, v, b in zip(ks, vs, biases):
        p = jnp.exp(nt(k, qs) + b - lse)
        d = nt(v, dos)
        delta += jnp.sum(p * d, axis=0, keepdims=True)
        ps.append(p)
        ds.append(d)
    g_pre = (p_pre * (d_pre - delta)).astype(LOW)
    dq = tn(k_pre, g_pre)
    dk, dv = [nn(g_pre, qs)], [nn(p_pre.astype(LOW), dos)]
    for p, d, kt in zip(ps, ds, kts):
        g = (p * (d - delta)).astype(LOW)
        dq += nn(kt, g)
        dk.append(nn(g, qs))
        dv.append(nn(p.astype(LOW), dos))
    return dq, dk, dv


COSTS = {
    "pack_heads": 1.5,
    "pack": 5.0,
    "self_fwd": 5.0,
    "mem_fwd": 2.3,
    "mid_fwd": 10.0,
    "mlp": 20.0,
    "cross_bwd": 11.0,
    "query_bwd": 3.0,
    "self_bwd": 6.5,
    "mem_back": 2.5,
    "totals": 3.0,
}
LIMITS = {
    "pack_heads": 60,
    "inbound": 20,
    "tokens": 4,
    "pack": 60,
    "self_fwd": 14,
    "self_bwd": 18,
    "mem_fwd": 14,
    "mem_back": 14,
    "mid_fwd": 24,
    "mlp": 48,
    "cross_bwd": 26,
    "query_bwd": 12,
    "halve": 6,
    "join": 8,
    "totals": 20,
    "mix": 4,
}


def call(kernel, name, ins, outs, scratch=()):
    flops = int(COSTS.get(name, 0.8) * 0.3e9)
    return pl.pallas_call(
        kernel,
        cost_estimate=pl.CostEstimate(flops=flops, bytes_accessed=1000, transcendentals=0),
        in_specs=ins,
        out_specs=[o[0] for o in outs],
        out_shape=[o[1] for o in outs],
        scratch_shapes=list(scratch),
        compiler_params=pltpu.CompilerParams(vmem_limit_bytes=LIMITS[name] * 2**20),
        name=name,
    )


def out(shape, dtype=LOW, space=VMEM):
    return space, jax.ShapeDtypeStruct(shape, dtype)


def inbound_kernel(ids, tokens, memory, first, second, sems):
    copies = []
    for n, dst in enumerate((first, second)):
        row = ids[12] if n == 0 else 1 - ids[12]
        for m, (src, start, size) in enumerate(((tokens, 0, 64), (memory, 64, 128))):
            copies.append(pltpu.make_async_copy(src.at[row], dst.at[pl.ds(start, size)], sems.at[n, m]))
    for copy in copies:
        copy.start()
    for copy in copies:
        copy.wait()


def inbound(ids, tokens, memory):
    return call(
        inbound_kernel,
        "inbound",
        [SMEM, HBM, HBM],
        [out((192, 1024)), out((192, 1024))],
        [pltpu.SemaphoreType.DMA((2, 2))],
    )(ids, tokens, memory)


def tokens_kernel(first, second, dst, sems):
    copies = [
        pltpu.make_async_copy(src.at[pl.ds(0, 64)], dst.at[pl.ds(64 * n, 64)], sems.at[n])
        for n, src in enumerate((first, second))
    ]
    for copy in copies:
        copy.start()
    for copy in copies:
        copy.wait()


def pack_first_kernel(ids, query, kv, ckv, dst, wide, sems):
    copies = [pltpu.make_async_copy(ckv.at[n], wide.at[pl.ds(256 * n, 256)], sems.at[n]) for n in range(2)]
    for n in range(2):
        group = cols(ids[13 + 2 * n] * 256, 256)
        for j, src in enumerate((query, kv.at[0])):
            copies.append(
                pltpu.make_async_copy(
                    src.at[:, group],
                    wide.at[pl.ds(512, 256), pl.ds(512 * n + 256 * j, 256)],
                    sems.at[2 + 4 * n + j],
                )
            )
        for j in range(2):
            copies.append(
                pltpu.make_async_copy(
                    kv.at[1, pl.ds(128 * j, 128), group],
                    wide.at[pl.ds(768, 128), pl.ds(512 * j + 256 * n, 256)],
                    sems.at[4 + 4 * n + j],
                )
            )
    for copy in copies:
        copy.start()
    for copy in copies:
        copy.wait()
    dst[...] = wide[...].astype(LOW)


def pack_first(ids, query, kv, ckv):
    return call(
        pack_first_kernel,
        "pack_heads",
        [SMEM, HBM, HBM, HBM],
        [out((896, 1024))],
        [pltpu.VMEM((896, 1024), F32), pltpu.SemaphoreType.DMA((10,))],
    )(ids, query, kv, ckv)[0]


def head_weights(parts):
    for n, part in enumerate(parts):
        g = n % 2
        yield (
            part[512:768, 512 * g : 512 * g + 256],
            part[512:768, 512 * g + 256 : 512 * g + 512],
            part[768:, 256 * g : 256 * g + 256],
            part[768:, 512 + 256 * g : 768 + 256 * g],
        )


def pack_kernel(sources, n_args, ids, *refs):
    args, refs = refs[:n_args], refs[n_args:]
    outs, (wide, narrow, in_sem, own_sem, part_sem) = refs[:-5], refs[-5:]
    count = len(sources)

    def fetch(m):
        arg, lead, row, col, kept_in = sources[m][:5]
        src = args[arg] if lead is None else args[arg].at[lead]
        start, size = row, 256
        if kept_in is None:
            start, size = pl.multiple_of(row + ids[sources[m][-1]] * 128, 128), 128
        return pltpu.make_async_copy(
            src.at[pl.ds(start, size), pl.ds(col, 1024)], wide.at[m, pl.ds(0, size)], in_sem.at[m]
        )

    def store(m):
        kept_in, kept_at, number, index, bit = sources[m][4:]
        kept = narrow.at[m]
        half = kept
        if kept_in is None:
            half = kept.at[pl.ds(0, 128)]
        elif bit is not None:
            half = kept.at[pl.ds(pl.multiple_of(ids[bit] * 128, 128), 128)]
        part = pltpu.make_async_copy(half, outs[number].at[index], part_sem.at[m])
        if kept_in is None:
            return (part,)
        return pltpu.make_async_copy(kept, outs[kept_in].at[kept_at], own_sem.at[m]), part

    for m in range(count):
        fetch(m).start()
    for m in range(count):
        fetch(m).wait()
        narrow[m] = wide[m].astype(LOW)
        for copy in store(m):
            copy.start()
    for m in range(count):
        for copy in store(m):
            copy.wait()


def pack(ids, sources, shapes, *args):
    return call(
        functools.partial(pack_kernel, sources, len(args)),
        "pack",
        [SMEM] + [HBM] * len(args),
        [out(shape, LOW, HBM) for shape in shapes],
        [
            pltpu.VMEM((len(sources), 256, 1024), F32),
            pltpu.VMEM((len(sources), 256, 1024), LOW),
            pltpu.SemaphoreType.DMA((len(sources),)),
            pltpu.SemaphoreType.DMA((len(sources),)),
            pltpu.SemaphoreType.DMA((len(sources),)),
        ],
    )(ids, *args)


PLACES = {
    "own": (lambda ids: ids[4], 256),
    "core": (lambda ids: ids[5], 256),
    "near": (lambda ids: ids[6], 128),
    "other": (lambda ids: ids[7], 128),
    "core_near": (lambda ids: ids[8], 128),
    "core_other": (lambda ids: ids[9], 128),
    "near_y": (lambda ids: ids[21], 128),
    "other_y": (lambda ids: ids[22], 128),
    "core_near_y": (lambda ids: ids[23], 128),
    "core_other_y": (lambda ids: ids[24], 128),
    "far": (lambda ids: 2 * ids[2], 256),
    "core_far": (lambda ids: 2 * ids[3], 256),
}
DIRECT = ("own", "core", "far", "core_far")
SHARED = ("own", "core", "near", "other", "core_near", "core_other")


def shared(index, first):
    return [(n, index + first if n < 2 else index, place) for n, place in enumerate(SHARED)]


def direct(index):
    return [(n, index, place) for n, place in enumerate(DIRECT)]


def place_of(ids, place):
    first, size = PLACES[place]
    return cols(first(ids) * 128, size)


def mm(x_ref, refs, matrix, ids):
    acc = None
    for n, index, place in matrix:
        term = nn(x_ref[:, place_of(ids, place)], refs[n][index])
        acc = term if acc is None else acc + term
    return acc


def mm_back(value, refs, matrix, ids, out_ref):
    for n, index, place in matrix:
        out_ref[:, place_of(ids, place)] = nt(value, refs[n][index])


class Fetch:
    def __init__(self, sources, targets, sems, matrices, first=0):
        self.copies, number = [], 0
        for matrix in matrices:
            mine = []
            for n, index, _ in matrix:
                to = index - first if n < 2 else index
                mine.append(pltpu.make_async_copy(sources[n].at[index], targets[n].at[to], sems.at[number]))
                number += 1
            self.copies.append(mine)

    def start(self, m):
        for copy in self.copies[m]:
            copy.start()

    def wait(self, m):
        for copy in self.copies[m]:
            copy.wait()


def fill_prefix(pre, wide, narrow, count, where=None):
    wide[...] = jnp.zeros_like(wide)
    wide[:, :count, :] = pre[...] if where is None else pre[:, :, where]
    narrow[...] = wide[...].astype(LOW)


def fill_places(order, ids, kpos, qpos):
    c, y, odd = ids[10], ids[11], ids[12]
    lane = lax.broadcasted_iota(jnp.int32, (1, 512), 1)
    column = jnp.zeros((1, 512), jnp.int32)
    for n in range(16):
        core = c if n < 8 else 1 - c
        line = y if n % 8 < 4 else 1 - y
        turned = odd if n % 4 < 2 else 1 - odd
        bucket = 2 * (2 * (2 * core + turned) + line) + n % 2
        first = order[bucket] * 32
        kpos[n * 32 : (n + 1) * 32, :] = lax.broadcasted_iota(jnp.int32, (32, 1), 0) + first
        column = jnp.where(lane // 32 == n, first + lane % 32, column)
    qpos[...] = column


def self_bias(kpos, qpos, t):
    seen = kpos[...] <= qpos[:, t * 128 : (t + 1) * 128]
    bias = jnp.where(seen, 0.0, MASKED)
    return jnp.concatenate([bias, bias], 1)


def self_fwd_kernel(
    count, ids, order, t0, t1, t2, t3, w0, w1, w2, w3, pre, q_ref, k_ref, v_ref,
    o0, o1, o2, o3, lse_ref, vt, kpos, qpos, wide, pre_l
):
    fill_places(order, ids, kpos, qpos)
    fill_prefix(pre, wide, pre_l, count, cols(ids[13] * 256, 256))
    for t, tok in enumerate((t0, t1, t2, t3)):
        rows = slice(t * 128, (t + 1) * 128)
        acc = [0.0, 0.0, 0.0]
        for n, (wq, wk, wv, wv2) in enumerate(head_weights((w0, w1, w2, w3))):
            some = tok[:, cols(ids[n] * 256, 256)]
            acc[0] += nn(some, wq)
            acc[1] += nn(some, wk)
            acc[2] += nn(some[:, :128], wv) + nn(some[:, 128:], wv2)
        q_ref[rows, :] = (acc[0] * SCALE).astype(LOW)
        k_ref[rows, :] = acc[1].astype(LOW)
        v_ref[rows, :] = acc[2].astype(LOW)
    vt[...] = v_ref[...].T
    for t in (3, 1, 2, 0):
        bias = self_bias(kpos, qpos, t)
        for p in range(2):
            lanes = slice(p * 128, (p + 1) * 128)
            qs = stacked(q_ref[t * 128 : (t + 1) * 128, lanes])
            got, lse = soft_pair(
                qs, pre_l[0, :, lanes], [k_ref[:, lanes]], pre_l[1, :, lanes], [vt[lanes, :]], [bias], count
            )
            (o0, o1, o2, o3)[t][:, lanes] = unstacked(got, 128).astype(LOW)
            lse_ref[p, t] = lse


def self_fwd(ids, order, toks, ws, pre, count):
    return call(
        functools.partial(self_fwd_kernel, count),
        "self_fwd",
        [SMEM, SMEM] + [VMEM] * 9,
        [
            out((512, 256)),
            out((512, 256)),
            out((512, 256)),
            out((128, 256)),
            out((128, 256)),
            out((128, 256)),
            out((128, 256)),
            out((2, 4, 1, 256), F32),
        ],
        [
            pltpu.VMEM((256, 512), LOW),
            pltpu.VMEM((512, 1), jnp.int32),
            pltpu.VMEM((1, 512), jnp.int32),
            pltpu.VMEM((2, 32, 256), F32),
            pltpu.VMEM((2, 32, 256), LOW),
        ],
    )(ids, order, *toks, *ws, pre)


def self_bwd_kernel(
    count, ids, order, q, k, v, d0, d1, d2, d3, g0, lse_ref, w0, w1, w2, w3, pre,
    near_ref, far_ref, sums_ref, kt, dq, dk, dv, gpre_ref, kpos, qpos, wide, pre_l
):
    fill_places(order, ids, kpos, qpos)
    fill_prefix(pre, wide, pre_l, count, cols(ids[13] * 256, 256))
    kt[...] = k[...].T
    grads = (d0, d1, d2, d3)
    for t in range(4):
        bias = self_bias(kpos, qpos, t)
        for p in range(2):
            lanes = slice(p * 128, (p + 1) * 128)
            qs = stacked(q[t * 128 : (t + 1) * 128, lanes])
            dos = stacked(grads[t][:128, lanes])
            g, gk, gv = soft_pair_back(
                qs,
                dos,
                lse_ref[p, t],
                pre_l[0, :, lanes],
                pre_l[1, :, lanes],
                [k[:, lanes]],
                [v[:, lanes]],
                [kt[lanes, :]],
                [bias],
                count,
            )
            dq[t * 128 : (t + 1) * 128, lanes] = unstacked(g, 128).astype(LOW)
            if t == 0:
                gpre_ref[:32, lanes] = gk[0]
                gpre_ref[32:, lanes] = gv[0]
                dk[:, lanes] = gk[1]
                dv[:, lanes] = gv[1]
            else:
                gpre_ref[:32, lanes] += gk[0]
                gpre_ref[32:, lanes] += gv[0]
                dk[:, lanes] += gk[1]
                dv[:, lanes] += gv[1]
    cross = g0[...] + d1[128:].astype(F32) + d2[128:].astype(F32) + d3[128:].astype(F32)
    for n, rows in enumerate((gpre_ref[:32], gpre_ref[32:], cross[:32], cross[32:])):
        sums_ref[:, 256 * n : 256 * (n + 1)] = rows.astype(LOW)
    dkl, dvl = dk[...].astype(LOW), dv[...].astype(LOW)
    for n, (wq, wk, wv, wv2) in enumerate(head_weights((w0, w1, w2, w3))):
        part = jnp.concatenate([nt(dvl, wv), nt(dvl, wv2)], 1)
        part = (part + nt(dq[...], wq) * SCALE + nt(dkl, wk)).astype(LOW)
        near_ref[:, cols(ids[n] * 256, 256)] = part[:256]
        far_ref[:, cols(ids[n] * 256, 256)] = part[256:]


def self_bwd(ids, order, q, k, v, grads, g0, lse, ws, pre, count):
    return call(
        functools.partial(self_bwd_kernel, count),
        "self_bwd",
        [SMEM, SMEM] + [VMEM] * 14,
        [out((256, 1024)), out((256, 1024)), out((32, 1024))],
        [
            pltpu.VMEM((256, 512), LOW),
            pltpu.VMEM((512, 256), LOW),
            pltpu.VMEM((512, 256), F32),
            pltpu.VMEM((512, 256), F32),
            pltpu.VMEM((64, 256), F32),
            pltpu.VMEM((512, 1), jnp.int32),
            pltpu.VMEM((1, 512), jnp.int32),
            pltpu.VMEM((2, 32, 256), F32),
            pltpu.VMEM((2, 32, 256), LOW),
        ],
    )(ids, order, q, k, v, *grads, g0, lse, *ws, pre)


def memory_fetch(parts, bufs, sems):
    copies = [
        [
            pltpu.make_async_copy(p.at[pl.ds(256 * j, 256)], b.at[j], sems.at[4 * j + n])
            for n, (p, b) in enumerate(zip(parts, bufs))
        ]
        for j in range(2)
    ]
    for copy in copies[0] + copies[1]:
        copy.start()
    return copies


def mem_kernel(ids, m0, m1, *refs):
    parts, res, bufs, sems = refs[:4], refs[4], refs[5:9], refs[9]
    copies = memory_fetch(parts, bufs, sems)
    for j in range(2):
        for copy in copies[j]:
            copy.wait()
        for n, mem in enumerate((m0.at[pl.ds(64, 128)], m1.at[pl.ds(64, 128)])):
            res[j, n * 128 : (n + 1) * 128, :] = mm(mem, bufs, direct(j), ids).astype(LOW)


def mem_fwd(ids, m0, m1, parts):
    return call(
        mem_kernel,
        "mem_fwd",
        [SMEM] + [VMEM] * 2 + [HBM] * 4,
        [out((2, 256, 1024))],
        [pltpu.VMEM((2, 256, 1024), LOW) for p in parts] + [pltpu.SemaphoreType.DMA((8,))],
    )(ids, m0, m1, *parts)[0]


def mem_back_kernel(ids, near, far_c, far_k, far_v, *refs):
    parts, (r0, r1), bufs, (wide, sems) = refs[:4], refs[4:6], refs[6:10], refs[10:]
    copies = memory_fetch(parts, bufs, sems)
    total = [
        (near[j].astype(F32) + far_c[j].astype(F32) + far_y[...].astype(F32)).astype(LOW)
        for j, far_y in enumerate((far_k, far_v))
    ]
    for copy in copies[0] + copies[1]:
        copy.wait()
    for n, place in enumerate(DIRECT):
        wide[:, place_of(ids, place)] = nt(total[0], bufs[n][0]) + nt(total[1], bufs[n][1])
    r0[...] = wide[:128].astype(LOW)
    r1[...] = wide[128:].astype(LOW)


def mem_back(ids, near, far_c, far_k, far_v, parts):
    return call(
        mem_back_kernel,
        "mem_back",
        [SMEM] + [VMEM] * 4 + [HBM] * 4,
        [out((128, 1024)), out((128, 1024))],
        [pltpu.VMEM((2, 256, 1024), LOW) for p in parts]
        + [pltpu.VMEM((256, 1024), F32), pltpu.SemaphoreType.DMA((8,))],
    )(ids, near, far_c, far_k, far_v, *parts)


def fill_bias(bias, ids, live):
    c, y, odd = ids[10], ids[11], ids[12]
    for n in range(8):
        core = c if n < 4 else 1 - c
        line = y if n % 4 < 2 else 1 - y
        turned = odd if n % 2 == 0 else 1 - odd
        first = (2 * (2 * core + turned) + line) * 128
        slot = lax.broadcasted_iota(jnp.int32, (128, 256), 0) + first
        bias[n * 128 : (n + 1) * 128, :] = jnp.where(slot < live[0, 0], 0.0, MASKED)


def mid_fwd_kernel(count, ids, live, o0, o1, o2, o3, tok, gain, shift, pre, *refs):
    kvs, parts, refs = refs[:4], refs[4:10], refs[10:]
    cq_ref, lse_ref, unit1, inv1, h2_ref, unit2, inv2, h2l = refs[:8]
    kv, bufs, (bias, flat, wide, pre_l, sems, kv_sems) = refs[8:12], refs[12:18], refs[18:]
    fetch = Fetch(parts, bufs, sems, [shared(j, 0) for j in range(3)])
    loads = [
        pltpu.make_async_copy(kvs[n].at[j], kv[n].at[j], kv_sems.at[n, j]) for j in range(2) for n in range(4)
    ]
    fetch.start(0)
    fetch.start(1)
    for copy in loads:
        copy.start()
    fetch.start(2)
    for n, o in enumerate((o0, o1, o2, o3)):
        flat[:, cols(ids[13 + n] * 256, 256)] = o[...]
    fill_bias(bias, ids, live)
    fill_prefix(pre, wide, pre_l, count)
    fetch.wait(0)
    h1, unit, inv = ln(
        tok[...].astype(F32) + mm(flat, bufs, shared(0, 0), ids), gain[0:1], shift[0:1]
    )
    unit1[...] = unit
    inv1[...] = inv
    flat[...] = h1.astype(LOW)
    fetch.wait(1)
    cq_ref[...] = (mm(flat, bufs, shared(1, 0), ids) * SCALE).astype(LOW)
    for copy in loads:
        copy.wait()
    for p in range(8):
        lanes = slice(p * 128, (p + 1) * 128)
        got, lse = soft_pair(
            stacked(cq_ref[:, lanes]),
            pre_l[0, :, lanes],
            [kv[n][0, :, lanes] for n in range(4)],
            pre_l[1, :, lanes],
            [kv[n][1, :, lanes].T for n in range(4)],
            [bias[n * 256 : (n + 1) * 256] for n in range(4)],
            count,
        )
        flat[:, lanes] = unstacked(got, 128).astype(LOW)
        lse_ref[p] = lse
    fetch.wait(2)
    h2, unit, inv = ln(h1 + mm(flat, bufs, shared(2, 0), ids), gain[1:2], shift[1:2])
    h2_ref[...] = h2
    unit2[...] = unit
    inv2[...] = inv
    h2l[...] = h2.astype(LOW)


def mid_fwd(ids, live, os, tok, gain, shift, pre, kvs, parts, count):
    wide, thin = out((128, 1024), F32), out((128, 1), F32)
    return call(
        functools.partial(mid_fwd_kernel, count),
        "mid_fwd",
        [SMEM, SMEM] + [VMEM] * 8 + [HBM] * 10,
        [out((128, 1024)), out((8, 1, 256), F32), wide, thin, wide, wide, thin, out((128, 1024))],
        [pltpu.VMEM((2, 256, 1024), LOW)] * 4
        + [pltpu.VMEM((3, *p.shape[1:]), LOW) for p in parts]
        + [
            pltpu.VMEM((1024, 256), F32),
            pltpu.VMEM((128, 1024), LOW),
            pltpu.VMEM((2, 32, 1024), F32),
            pltpu.VMEM((2, 32, 1024), LOW),
            pltpu.SemaphoreType.DMA((18,)),
            pltpu.SemaphoreType.DMA((4, 2)),
        ],
    )(ids, live, *os, tok, gain, shift, pre, *kvs, *parts)


def mlp_kernel(matrices, ids, h2, h2l, unit2, inv2, c0, c1, gain, shift, down_b, up_b, down_any, up_any, *refs):
    count = 1 + max(n for matrix in matrices for n, _, _ in matrix)
    parts, refs = refs[:count], refs[count:]
    m0, m1, dr2, keep, give, gaub, gadb = refs[:7]
    bufs, (down, up, act, slope, acc, sems, ad_sems) = refs[7 : 7 + count], refs[7 + count :]
    fetch = Fetch(parts, bufs, sems, matrices)
    ad = [
        pltpu.make_async_copy(down_any, down, ad_sems.at[0]),
        pltpu.make_async_copy(up_any, up, ad_sems.at[1]),
    ]
    for s in range(4):
        fetch.start(s)
    for copy in ad:
        copy.start()
    for s in range(4, 8):
        fetch.start(s)
    for s in range(4):
        fetch.wait(s)
        value, gradient = gelu_both(mm(h2l, bufs, matrices[s], ids))
        lanes = slice(s * 1024, (s + 1) * 1024)
        act[:, lanes] = value.astype(LOW)
        slope[:, lanes] = gradient
    for copy in ad:
        copy.wait()
    down_w, up_w = down[...].astype(LOW), up[...].astype(LOW)
    a, a_slope = gelu_both(nn(h2l[...], down_w) + down_b[...])
    a = a.astype(LOW)
    total = h2[...] + 4.0 * (nn(a, up_w) + up_b[...])

    def rows(s, place):
        first, size = PLACES[place]
        first = first(ids)
        return cols((first // 2) * 1024 + s * 256 + (first % 2) * 128, size)

    for s in range(4):
        fetch.wait(4 + s)
        for n, index, place in matrices[4 + s]:
            total += nn(act[:, rows(s, place)], bufs[n][index])
    res, unit3, inv3 = ln(total, gain[2:3], shift[2:3])
    m0[...] = res[:64].astype(LOW)
    m1[...] = res[64:].astype(LOW)
    cot = jnp.concatenate([c0[...], c1[...]], 0).astype(F32)
    dr3 = ln_back(cot, unit3, inv3, gain[2:3])
    dffn = dr3.astype(LOW)
    dad = (4.0 * dr3).astype(LOW)
    gau = tn(a, dad)
    gaub[...] = jnp.sum(dad.astype(F32), axis=0, keepdims=True)
    ddn = (a_slope * nt(dad, up_w)).astype(LOW)
    gadb[:, :512] = jnp.sum(ddn.astype(F32), axis=0, keepdims=True)
    gadb[:, 512:] = jnp.zeros((1, 512), F32)
    gadt = tn(ddn, h2l[...])
    first_core = ids[10] == 0
    keep[...] = jnp.where(first_core, gau, gadt)
    give[...] = jnp.where(first_core, gadt, gau).astype(LOW)
    for s in range(4):
        for n, index, place in matrices[4 + s]:
            where = rows(s, place)
            act[:, where] = (slope[:, where] * nt(dffn, bufs[n][index])).astype(LOW)
    acc[...] = dr3 + nt(ddn, down_w)
    for s in range(4):
        for n, index, place in matrices[s]:
            acc[:, place_of(ids, place)] += nt(act[:, s * 1024 : (s + 1) * 1024], bufs[n][index])
    dr2[...] = ln_back(acc[...], unit2[...], inv2[...], gain[1:2])


def mlp(ids, h2, h2l, unit2, inv2, cots, gain, shift, down_b, up_b, down, up, parts, matrices):
    return call(
        functools.partial(mlp_kernel, matrices),
        "mlp",
        [SMEM] + [VMEM] * 10 + [HBM] * (2 + len(parts)),
        [
            out((64, 1024)),
            out((64, 1024)),
            out((128, 1024), F32),
            out((512, 1024), F32),
            out((512, 1024)),
            out((1, 1024), F32),
            out((1, 1024), F32),
        ],
        [pltpu.VMEM((8, *p.shape[1:]) if n < 2 else p.shape, LOW) for n, p in enumerate(parts)]
        + [
            pltpu.VMEM((1024, 512), F32),
            pltpu.VMEM((512, 1024), F32),
            pltpu.VMEM((128, 4096), LOW),
            pltpu.VMEM((128, 4096), F32),
            pltpu.VMEM((128, 1024), F32),
            pltpu.SemaphoreType.DMA((sum(len(m) for m in matrices),)),
            pltpu.SemaphoreType.DMA((2,)),
        ],
    )(ids, h2, h2l, unit2, inv2, *cots, gain, shift, down_b, up_b, down, up, *parts)


def cross_bwd_kernel(count, ids, live, dr2, cq, lse, gaub, gadb, pre, *refs):
    kvs, parts, refs = refs[:4], refs[4:10], refs[10:]
    grads, (dcq, *sums) = refs[:4], refs[4:9]
    kv, bufs, (bias, flat, wide, wide_pre, pre_l, gpre, sems, kv_sems) = refs[9:13], refs[13:19], refs[19:]
    copies = [
        pltpu.make_async_copy(parts[n].at[2], bufs[n], sems.at[n]) for n in range(6)
    ]
    loads = [
        pltpu.make_async_copy(kvs[n].at[j], kv[n].at[j], kv_sems.at[n, j]) for j in range(2) for n in range(4)
    ]
    for copy in copies + loads:
        copy.start()
    fill_bias(bias, ids, live)
    fill_prefix(pre, wide_pre, pre_l, count)
    for copy in copies:
        copy.wait()
    value = dr2[...].astype(LOW)
    for n, place in enumerate(SHARED):
        wide[:, place_of(ids, place)] = nt(value, bufs[n][...])
    flat[...] = wide[...].astype(LOW)
    for copy in loads:
        copy.wait()
    for p in range(8):
        lanes = slice(p * 128, (p + 1) * 128)
        g, gk, gv = soft_pair_back(
            stacked(cq[:, lanes]),
            stacked(flat[:, lanes]),
            lse[p],
            pre_l[0, :, lanes],
            pre_l[1, :, lanes],
            [kv[n][0, :, lanes] for n in range(4)],
            [kv[n][1, :, lanes] for n in range(4)],
            [kv[n][0, :, lanes].T for n in range(4)],
            [bias[n * 256 : (n + 1) * 256] for n in range(4)],
            count,
        )
        for j, got in enumerate((gk, gv)):
            gpre[j, :, lanes] = got[0]
            for n in range(4):
                grads[n][j, :, lanes] = got[1 + n].astype(LOW)
        dcq[:, lanes] = unstacked(g, 128).astype(LOW)
    gpre[0, count : count + 1, :] = gaub[...]
    gpre[1, count : count + 1, :] = gadb[...]
    for j in range(2):
        rows = slice(32 * j, 32 * (j + 1))
        for n, dst in enumerate(sums):
            dst[rows, :] = gpre[j, :, cols(ids[13 + n] * 256, 256)].astype(dst.dtype)


def cross_bwd(ids, live, dr2, cq, lse, gaub, gadb, pre, kvs, parts, count):
    grad = out((2, 256, 1024))
    return call(
        functools.partial(cross_bwd_kernel, count),
        "cross_bwd",
        [SMEM, SMEM] + [VMEM] * 6 + [HBM] * 10,
        [grad, grad, grad, grad, out((128, 1024)), out((64, 256), F32)] + [out((64, 256))] * 3,
        [pltpu.VMEM((2, 256, 1024), LOW)] * 4
        + [pltpu.VMEM(p.shape[1:], LOW) for p in parts]
        + [
            pltpu.VMEM((1024, 256), F32),
            pltpu.VMEM((128, 1024), LOW),
            pltpu.VMEM((128, 1024), F32),
            pltpu.VMEM((2, 32, 1024), F32),
            pltpu.VMEM((2, 32, 1024), LOW),
            pltpu.VMEM((2, 32, 1024), F32),
            pltpu.SemaphoreType.DMA((6,)),
            pltpu.SemaphoreType.DMA((4, 2)),
        ],
    )(ids, live, dr2, cq, lse, gaub, gadb, pre, *kvs, *parts)


def query_bwd_kernel(ids, dr2, dcq, unit1, inv1, gain, g1, g2, g3, *refs):
    parts, (dr1, *grads), rest = refs[:6], refs[6:11], refs[11:]
    bufs, (wide, sems) = rest[:6], rest[6:]
    fetch = Fetch(parts, bufs, sems, [shared(1, 0), shared(0, 0)])
    fetch.start(0)
    fetch.start(1)
    fetch.wait(0)
    mm_back(dcq[...], bufs, shared(1, 0), ids, wide)
    grad = ln_back(dr2[...] + SCALE * wide[...], unit1[...], inv1[...], gain[0:1])
    dr1[...] = grad
    fetch.wait(1)
    mm_back(grad.astype(LOW), bufs, shared(0, 0), ids, wide)
    for dst, g in zip(grads[1:], (g1, g2, g3)):
        dst[128:, :] = g[...]
    for n, dst in enumerate(grads):
        dst[:128, :] = wide[:, cols(ids[13 + n] * 256, 256)].astype(LOW)


def query_bwd(ids, dr2, dcq, unit1, inv1, gain, sums, parts):
    return call(
        query_bwd_kernel,
        "query_bwd",
        [SMEM] + [VMEM] * 8 + [HBM] * 6,
        [out((128, 1024), F32), out((128, 256))] + [out((192, 256))] * 3,
        [pltpu.VMEM((2, *p.shape[1:]), LOW) for p in parts]
        + [pltpu.VMEM((128, 1024), F32), pltpu.SemaphoreType.DMA((12,))],
    )(ids, dr2, dcq, unit1, inv1, gain, *sums, *parts)


def quarters(ids, bits, size, start=0):
    first, second = ids[bits[0]], ids[bits[1]]
    pairs = ((first, second), (1 - first, second), (first, 1 - second), (1 - first, 1 - second))
    return [pl.ds(pl.multiple_of(start + (2 * a + b) * size, size), size) for a, b in pairs]


def halve_kernel(bits, count, ids, keep, *refs):
    gots, outs = refs[:count], refs[count:]
    for dst, rows in zip(outs, quarters(ids, bits, outs[0].shape[0])):
        total = keep[rows, :]
        for got in gots:
            total += got[rows, :].astype(F32)
        dst[...] = total.astype(dst.dtype)


def halve(ids, bits, keep, gots):
    size = keep.shape[0] // 4
    return call(
        functools.partial(halve_kernel, bits, len(gots)),
        "halve",
        [SMEM] + [VMEM] * (1 + len(gots)),
        [out((size, 1024), F32)] + [out((size, 1024))] * 3,
    )(ids, keep, *gots)


def mix_kernel(keep, part, g1, g2, g3, dst):
    dst[:32, :] = (
        keep[...] + g1[...].astype(F32) + g2[...].astype(F32) + g3[...].astype(F32)
    ).astype(LOW)
    dst[32:, :] = part[...]


def join_kernel(bits, ids, *refs):
    parts, dst = refs[:4], refs[4]
    for part, rows in zip(parts, quarters(ids, bits, 32)):
        dst[rows, :] = part[:32, :]
    own, other_y, other_z, both = (part[32:, :].astype(F32) for part in parts)
    dst[128:160, :] = (own + other_z).astype(LOW)
    dst[160:, :] = (other_y + both).astype(LOW)


def join_last_kernel(bits, ids, p0, p1, p2, p3, dst, wide):
    parts = (p0, p1, p2, p3)
    for part, rows in zip(parts, quarters(ids, bits, 128)):
        dst[rows, :] = part[:128, :]
    for part, rows in zip(parts, quarters(ids, bits, 64)):
        wide[rows, :] = part[128:, :].astype(F32)
    dst[512:, :] = (wide[:64] + wide[64:128] + wide[128:192] + wide[192:]).astype(LOW)


def totals_kernel(count, ids, mine, got, gau, gad, gps, gpc, gaub, gadb, wide):
    first_core = ids[10] == 0
    gau[...] = jnp.where(first_core, mine[:512], got[:512]).astype(F32)
    gad[...] = jnp.where(first_core, got[:512], mine[:512]).astype(F32).T
    for n in range(4):
        rows = (mine, got)[n // 2][512 + 32 * (n % 2) : 544 + 32 * (n % 2), :].astype(F32)
        for a in range(4):
            wide[32 * a : 32 * a + 32, cols(ids[13 + n] * 256, 256)] = rows[:, 256 * a : 256 * a + 256]
    for j in range(2):
        gps[j] = wide[32 * j : 32 * j + count, :]
        gpc[j] = wide[64 + 32 * j : 64 + 32 * j + count, :]
    gaub[...] = wide[64 + count : 65 + count, :]
    gadb[...] = wide[96 + count : 97 + count, :512]


AXES = ("x", "core", "pair", "z", "y")


def pairs_of(target):
    pairs = []
    for source in range(32):
        row, seq = divmod(source, 8)
        x, c, z, y = target(*divmod(row, 2), *divmod(seq, 2))
        pairs.append((source, (2 * x + c) * 8 + 2 * z + y))
    return pairs


SWAP_X = pairs_of(lambda x, c, z, y: (1 - x, c, z, y))
SWAP_C = pairs_of(lambda x, c, z, y: (x, 1 - c, z, y))
SWAP_Y = pairs_of(lambda x, c, z, y: (x, c, z, 1 - y))
SWAP_CY = pairs_of(lambda x, c, z, y: (x, 1 - c, z, 1 - y))
SWAP_Z = pairs_of(lambda x, c, z, y: (x, c, z ^ 1, y))
SWAP_PAIRS = pairs_of(lambda x, c, z, y: (x, c, z ^ 2, y))
SQUARE = (
    ((17, 18), (SWAP_X, SWAP_Z, pairs_of(lambda x, c, z, y: (1 - x, c, z ^ 1, y)))),
    ((20, 19), (SWAP_Y, SWAP_PAIRS, pairs_of(lambda x, c, z, y: (x, c, z ^ 2, 1 - y)))),
)
TURN = [pairs_of(lambda x, c, z, y, r=r: (x, z // 2, 2 * c + (z + r) % 2, y)) for r in range(2)]


def send(value, pairs):
    return lax.ppermute(value, AXES, pairs)


def local_pairs(
    tokens,
    memory,
    source_len,
    bucket_order,
    prefix_self,
    prefix_cross,
    self_query,
    self_kv,
    self_out,
    cross_query,
    cross_kv,
    cross_out,
    fc_in,
    fc_out,
    ln_gain,
    ln_bias,
    ad_down,
    ad_down_bias,
    ad_up,
    ad_up_bias,
    cotangent,
):
    f32 = F32
    x, c, odd, y = (lax.axis_index(name) for name in ("x", "core", "z", "y"))
    z = 2 * lax.axis_index("pair") + odd
    row = 2 * x + c
    count = prefix_self.shape[1]
    group = 2 * y + c
    far_row, both_row = 2 * (row ^ 2), 2 * (row ^ 3)
    ids = jnp.stack(
        [row, row ^ 1, row ^ 2, row ^ 3]
        + [2 * row, 2 * (row ^ 1), far_row + odd, far_row + 1 - odd, both_row + odd, both_row + 1 - odd]
        + [c, y, odd]
        + [group, group ^ 2, group ^ 1, group ^ 3]
        + [x, odd, z // 2, y]
        + [far_row + y, far_row + 1 - y, both_row + y, both_row + 1 - y]
    ).astype(jnp.int32)

    def after(value, *others):
        if isinstance(value, tuple):
            return lax.optimization_barrier((*value, *others))[: len(value)]
        return lax.optimization_barrier((value, *others))[0]

    def turn_out(first, second):
        first, second = send(first, TURN[0]), send(second, TURN[1])
        return jnp.stack([jnp.where(odd == 1, second, first), jnp.where(odd == 1, first, second)])

    blocks = inbound(ids, tokens, memory)
    first, second = (send(block, turn) for block, turn in zip(blocks, TURN))
    one = pack_first(after(ids, blocks[0]), self_query, self_kv, cross_kv)
    one_far, one_c = send(one, SWAP_X), send(one, SWAP_C)
    live = send(jnp.where(odd == 1, source_len[1], source_len[0]).reshape(1, 1), TURN[0])
    tok = call(
        tokens_kernel, "tokens", [VMEM, VMEM], [out((128, 1024))], [pltpu.SemaphoreType.DMA((2,))]
    )(after(first, one_c, live), second)[0]
    tok_y, tok_c = send(tok, SWAP_Y), send(tok, SWAP_C)
    toks = (tok, tok_y, tok_c, send(tok_y, SWAP_C))
    mid_own, ffn_own, mid_half, in_half, out_half, out_whole = pack(
        after(ids, tok),
        [(n, None, 0, 0, 0, n, 2, n, 12) for n in range(3)]
        + [(3, None, 0, 1024 * n, 1, n, 3, n, 12) for n in range(4)]
        + [(4, None, 256 * n, 0, 1, 4 + n, 4, n, 11) for n in range(2)]
        + [(4, None, 256 * n, 0, 1, 4 + n, 5, n - 2, None) for n in range(2, 4)],
        [
            (3, 256, 1024),
            (8, 256, 1024),
            (3, 128, 1024),
            (4, 128, 1024),
            (2, 128, 1024),
            (2, 256, 1024),
        ],
        self_out,
        cross_query,
        cross_out,
        fc_in,
        fc_out,
    )
    mid_near = send(mid_half, SWAP_X)
    mid_c = send(mid_own, SWAP_C)
    in_near = send(after(in_half, one_far), SWAP_X)

    one_parts = (one, one_c, one_far, send(after(one_far, toks[3], mid_half), SWAP_C))
    q, k, v, o0, o1, o2, o3, self_lse = self_fwd(
        ids, bucket_order, after(toks, mid_c), one_parts, prefix_self, count
    )
    os = (o0, send(o1, SWAP_Y), send(o2, SWAP_C), send(o3, SWAP_CY))
    mkv = mem_fwd(ids, after(first, q), second, one_parts)
    mkv_y = send(after(mkv, *os), SWAP_Y)
    mkv_c = send(mkv, SWAP_C)
    out_near = send(after(out_half, *os), SWAP_X)
    ffn_c = send(after(ffn_own, mkv), SWAP_C)
    mid_near_o = after(mid_near, *os)
    mid_other = send(mid_near_o, SWAP_Z)
    mid_parts = (mid_own, mid_c, mid_near, mid_other, send(after(mid_near, mkv_y), SWAP_C), send(mid_other, SWAP_C))
    in_other = send(after(in_near, mid_other), SWAP_Z)
    kvs = (mkv, mkv_y, mkv_c, send(mkv_y, SWAP_C))

    cq, cross_lse, unit1, inv1, h2, unit2, inv2, h2l = mid_fwd(
        ids, live, os, tok, ln_gain, ln_bias, prefix_cross, kvs, mid_parts, count
    )
    cot = [jnp.where(odd == 1, cotangent[1 - n], cotangent[n]) for n in range(2)]
    cots = [send(after(v, h2l), t) for v, t in zip(cot, TURN)]
    out_far = send(after(out_whole, kvs[3]), SWAP_X)
    in_near_l, out_near_l = after((in_near, out_near), h2l)
    out_other = send(out_near_l, SWAP_Y)
    ffn_parts = [ffn_own, ffn_c, in_near, in_other]
    ffn_parts += [send(t, SWAP_C) for t in (in_near_l, in_other)]
    ffn_parts += [out_near, out_other]
    ffn_parts += [send(t, SWAP_C) for t in (out_near_l, out_other)]
    ffn_parts += [out_far, send(out_far, SWAP_C)]
    matrices = [[(0, m, "own"), (1, m, "core")] for m in range(8)]
    for m in range(4):
        matrices[m] += [(2 + k, m, place) for k, place in enumerate(SHARED[2:])]
    for m in range(2):
        matrices[4 + m] += [(6 + k, m, place + "_y") for k, place in enumerate(SHARED[2:])]
        matrices[6 + m] += [(10, m, "far"), (11, m, "core_far")]
    m0, m1, dr2, keep, give, gaub, gadb = mlp(
        ids,
        h2,
        h2l,
        unit2,
        inv2,
        cots,
        ln_gain,
        ln_bias,
        ad_down_bias[None],
        ad_up_bias[None],
        ad_down,
        ad_up,
        ffn_parts,
        matrices,
    )
    mixed = turn_out(m0, m1)

    parts = [send(give, SWAP_C)]
    n0, n1, f0, f1, dcq, g0, *gs = cross_bwd(
        ids, live, dr2, cq, cross_lse, gaub, gadb, prefix_cross, kvs, mid_parts, count
    )
    far_c, near_c = send(f1, SWAP_C), send(f0, SWAP_C)
    bits, pairs = SQUARE[0]
    keep, *gives = halve(ids, bits, after(keep, dcq), parts)
    parts = [send(g, p) for g, p in zip(gives, pairs)]
    dr1, d0, d1, d2, d3 = query_bwd(ids, dr2, after(dcq, *gives), unit1, inv1, ln_gain, gs, mid_parts)
    grads = (d0, send(d1, SWAP_Y), send(d2, SWAP_C), send(d3, SWAP_CY))
    mem_k, mem_v = [
        (n1[n].astype(f32) + after(far_c, d0)[n].astype(f32)).astype(LOW) for n in range(2)
    ]
    far_k = send(after(mem_k, *grads), SWAP_Y)
    bits, pairs = SQUARE[1]
    keep, *gives = halve(ids, bits, keep, parts)
    parts = [send(g, p) for g, p in zip(gives, pairs)]
    near, far_part, part = self_bwd(
        ids,
        bucket_order,
        after(q, mem_k, mem_v, mixed, near_c),
        k,
        v,
        grads,
        g0,
        self_lse,
        one_parts,
        prefix_self,
        count,
    )
    got_c = send(after(far_part, far_k), SWAP_C)
    far_v = send(mem_v, SWAP_Y)
    mine = call(mix_kernel, "mix", [VMEM] * 5, [out((64, 1024))])(keep, part, *parts)[0]
    parts = [send(mine, p) for p in pairs]

    give_y = (near[128:].astype(f32) + got_c[128:].astype(f32)).astype(LOW)
    d_own = dr1 + near[:128].astype(f32) + got_c[:128].astype(f32)
    d_own = (d_own + send(give_y, SWAP_Y).astype(f32)).astype(LOW)
    d_tokens = turn_out(d_own[:64], d_own[64:])

    d_memory = turn_out(*mem_back(ids, n0, near_c, far_k, far_v, one_parts))

    whole = call(
        functools.partial(join_kernel, bits), "join", [SMEM] + [VMEM] * 4, [out((192, 1024))]
    )(ids, mine, *parts)[0]
    bits, pairs = SQUARE[0]
    parts = [send(whole, p) for p in pairs]
    whole = call(
        functools.partial(join_last_kernel, bits),
        "join",
        [SMEM] + [VMEM] * 4,
        [out((576, 1024))],
        [pltpu.VMEM((256, 1024), F32)],
    )(ids, whole, *parts)[0]
    grad_up, grad_down, grad_ps, grad_pc, grad_ub, grad_db = call(
        functools.partial(totals_kernel, count),
        "totals",
        [SMEM, VMEM, VMEM],
        [
            out((512, 1024), F32),
            out((1024, 512), F32),
            out(prefix_self.shape, F32),
            out(prefix_cross.shape, F32),
            out((1, 1024), F32),
            out((1, 512), F32),
        ],
        [pltpu.VMEM((128, 1024), F32)],
    )(ids, whole, send(whole, SWAP_C))
    return (
        mixed,
        d_tokens,
        d_memory,
        grad_ps,
        grad_pc,
        grad_down,
        grad_db[0],
        grad_up,
        grad_ub[0],
    )


def solution(mesh):
    in_specs = (
        P("row", "seq", None),
        P("row", "seq", None),
        P("row"),
        P(),
        P(),
        P(),
        P("row", None),
        P(None, "row", None),
        P("row", None),
        P("row", None),
        P(None, "row", None),
        P("row", None),
        P("row", None),
        P("row", None),
        P(),
        P(),
        P(),
        P(),
        P(),
        P(),
        P("row", "seq", None),
    )
    out_specs = (
        P("row", "seq", None),
        P("row", "seq", None),
        P("row", "seq", None),
        P(),
        P(),
        P(),
        P(),
        P(),
        P(),
    )
    if (mesh.shape["row"], mesh.shape["seq"]) != (4, 8):
        return jax.shard_map(
            local_rows, mesh=mesh, in_specs=in_specs, out_specs=out_specs, check_vma=False
        )
    fine = jax.sharding.Mesh(mesh.devices.reshape(2, 2, 2, 2, 2), AXES)
    split = {"row": ("x", "core"), "seq": ("pair", "z", "y")}

    def renamed(specs):
        return tuple(P(*(split.get(name) for name in spec)) for spec in specs)

    return jax.shard_map(
        local_pairs, mesh=fine, in_specs=renamed(in_specs), out_specs=renamed(out_specs), check_vma=False
    )
```

```python
import functools

import jax
import jax.numpy as jnp
from jax import lax
from jax.experimental import pallas as pl
from jax.experimental.pallas import tpu as pltpu
from jax.sharding import PartitionSpec as P

H = 16
HD = 64


EPSILON = 1e-05
MASKED = -1e30


def normalize(value, gain, shift):
    centre = value - jnp.mean(value, axis=-1, keepdims=True)
    inv_dev = lax.rsqrt(jnp.mean(centre * centre, axis=-1, keepdims=True) + EPSILON)
    unit_val = centre * inv_dev
    return (unit_val * gain + shift, unit_val, inv_dev)


def normalize_back(grad, unit_val, inv_dev, gain):
    scaled = grad * gain
    return inv_dev * (
        scaled
        - jnp.mean(scaled, axis=-1, keepdims=True)
        - unit_val * jnp.mean(scaled * unit_val, axis=-1, keepdims=True)
    )


def gelu_exact(value):
    return jax.nn.gelu(value, approximate=False)


def gelu_back(value, grad):
    return jax.vjp(gelu_exact, value)[1](grad)[0]


def head_split(matrix):
    return matrix.reshape(matrix.shape[0], -1, HD)


def masked_scores(queries, keys, mask):
    scores = jnp.einsum(
        "qhd,khd->hqk", head_split(queries), head_split(keys), preferred_element_type=jnp.float32
    )
    return jnp.where(mask[None], scores, MASKED)


def attend(queries, keys, values, mask):
    scores = masked_scores(queries, keys, mask)
    top_score = jnp.max(scores, axis=-1, keepdims=True)
    log_total = top_score + jnp.log(jnp.sum(jnp.exp(scores - top_score), axis=-1, keepdims=True))
    probs = jnp.exp(scores - log_total).astype(jnp.bfloat16)
    result = jnp.einsum(
        "hqk,khd->qhd", probs, head_split(values), preferred_element_type=jnp.float32
    )
    return (result.reshape(queries.shape[0], -1), log_total)


def attend_back(queries, keys, values, mask, log_total, grad_out):
    probs = jnp.exp(masked_scores(queries, keys, mask) - log_total)
    grad_heads = head_split(grad_out)
    grad_probs = jnp.einsum(
        "qhd,khd->hqk", grad_heads, head_split(values), preferred_element_type=jnp.float32
    )
    row_delta = jnp.sum(probs * grad_probs, axis=-1, keepdims=True)
    grad_scores = (probs * (grad_probs - row_delta)).astype(jnp.bfloat16)
    grad_query = jnp.einsum(
        "hqk,khd->qhd", grad_scores, head_split(keys), preferred_element_type=jnp.float32
    )
    grad_keys = jnp.einsum(
        "hqk,qhd->khd", grad_scores, head_split(queries), preferred_element_type=jnp.float32
    )
    grad_values = jnp.einsum(
        "hqk,qhd->khd", probs.astype(jnp.bfloat16), grad_heads, preferred_element_type=jnp.float32
    )
    return (
        grad_query.reshape(queries.shape[0], -1),
        grad_keys.reshape(keys.shape[0], -1),
        grad_values.reshape(values.shape[0], -1),
    )


def project(left, right):
    return jnp.dot(left, right, preferred_element_type=jnp.float32)


def local_rows(
    tokens,
    memory,
    source_len,
    bucket_order,
    prefix_self,
    prefix_cross,
    self_query,
    self_kv,
    self_out,
    cross_query,
    cross_kv,
    cross_out,
    fc_in,
    fc_out,
    ln_gain,
    ln_bias,
    ad_down,
    ad_down_bias,
    ad_up,
    ad_up_bias,
    cotangent,
):
    low_type = jnp.bfloat16
    row_count, tok_count, width = tokens.shape
    slot_count = memory.shape[1]
    prefix_count = prefix_self.shape[1]
    half_len = tok_count // 2
    scale = HD ** (-0.5)
    weight_set = (
        lax.all_gather(self_query.astype(low_type), "row", axis=0, tiled=True),
        lax.all_gather(self_kv.astype(low_type), "row", axis=1, tiled=True),
        lax.all_gather(self_out.astype(low_type), "row", axis=0, tiled=True),
        lax.all_gather(cross_query.astype(low_type), "row", axis=0, tiled=True),
        lax.all_gather(cross_kv.astype(low_type), "row", axis=1, tiled=True),
        lax.all_gather(cross_out.astype(low_type), "row", axis=0, tiled=True),
        lax.all_gather(fc_in.astype(low_type), "row", axis=0, tiled=True),
        lax.all_gather(fc_out.astype(low_type), "row", axis=0, tiled=True),
    )
    q_weight, kv_weight, o_weight, cq_weight, ckv_weight, co_weight, in_weight, out_weight = (
        weight_set
    )
    place = lax.axis_index("seq")
    offsets = jnp.arange(half_len, dtype=jnp.int32)
    all_pos = (bucket_order[:, None] * half_len + offsets[None, :]).reshape(-1)
    own_pos = lax.dynamic_slice_in_dim(all_pos, place * tok_count, tok_count)
    self_mask = jnp.concatenate(
        [jnp.ones((tok_count, prefix_count), jnp.bool_), all_pos[None, :] <= own_pos[:, None]],
        axis=1,
    )
    flat_tokens = tokens.reshape(-1, width)
    queries = (project(flat_tokens, q_weight) * scale).astype(low_type)
    own_keys = (
        project(flat_tokens, kv_weight[0]).astype(low_type).reshape(row_count, tok_count, width)
    )
    own_values = (
        project(flat_tokens, kv_weight[1]).astype(low_type).reshape(row_count, tok_count, width)
    )
    flat_memory = memory.reshape(-1, width)
    mem_keys = (
        project(flat_memory, ckv_weight[0]).astype(low_type).reshape(row_count, slot_count, width)
    )
    mem_values = (
        project(flat_memory, ckv_weight[1]).astype(low_type).reshape(row_count, slot_count, width)
    )
    all_keys, all_values, all_mkeys, all_mvalues = (
        lax.all_gather(own_keys, "seq", axis=1, tiled=True),
        lax.all_gather(own_values, "seq", axis=1, tiled=True),
        lax.all_gather(mem_keys, "seq", axis=1, tiled=True),
        lax.all_gather(mem_values, "seq", axis=1, tiled=True),
    )
    src_total = all_mkeys.shape[1]
    pre_self = prefix_self.astype(low_type)
    pre_cross = prefix_cross.astype(low_type)
    self_key_sets = [
        jnp.concatenate([pre_self[0], all_keys[row_index]], 0) for row_index in range(row_count)
    ]
    self_value_sets = [
        jnp.concatenate([pre_self[1], all_values[row_index]], 0) for row_index in range(row_count)
    ]
    cross_key_sets = [
        jnp.concatenate([pre_cross[0], all_mkeys[row_index]], 0) for row_index in range(row_count)
    ]
    cross_value_sets = [
        jnp.concatenate([pre_cross[1], all_mvalues[row_index]], 0) for row_index in range(row_count)
    ]
    slot_number = jnp.arange(src_total, dtype=jnp.int32)
    cross_masks = [
        jnp.concatenate(
            [jnp.ones((prefix_count,), jnp.bool_), slot_number < source_len[row_index]]
        )[None, :]
        for row_index in range(row_count)
    ]

    def rows_of(matrix, row_index):
        return matrix[row_index * tok_count : (row_index + 1) * tok_count]

    self_parts = [
        attend(
            rows_of(queries, row_index),
            self_key_sets[row_index],
            self_value_sets[row_index],
            self_mask,
        )
        for row_index in range(row_count)
    ]
    attended = jnp.concatenate([part[0] for part in self_parts], 0).astype(low_type)
    resid_one = flat_tokens.astype(jnp.float32) + project(attended, o_weight)
    hidden_one, unit_one, inv_one = normalize(resid_one, ln_gain[0], ln_bias[0])
    cross_queries = (project(hidden_one.astype(low_type), cq_weight) * scale).astype(low_type)
    cross_parts = [
        attend(
            rows_of(cross_queries, row_index),
            cross_key_sets[row_index],
            cross_value_sets[row_index],
            cross_masks[row_index],
        )
        for row_index in range(row_count)
    ]
    cross_att = jnp.concatenate([part[0] for part in cross_parts], 0).astype(low_type)
    resid_two = hidden_one + project(cross_att, co_weight)
    hidden_two, unit_two, inv_two = normalize(resid_two, ln_gain[1], ln_bias[1])
    hidden_low = hidden_two.astype(low_type)
    up_proj = project(hidden_low, in_weight)
    activated = gelu_exact(up_proj).astype(low_type)
    ffn_out = project(activated, out_weight)
    down_weight = ad_down.astype(low_type)
    up_weight = ad_up.astype(low_type)
    down_proj = project(hidden_low, down_weight) + ad_down_bias
    down_act = gelu_exact(down_proj).astype(low_type)
    adapted = project(down_act, up_weight) + ad_up_bias
    resid_three = hidden_two + ffn_out + 4.0 * adapted
    output, unit_three, inv_three = normalize(resid_three, ln_gain[2], ln_bias[2])
    mixed = output.astype(low_type).reshape(row_count, tok_count, width)
    weight_set = (
        lax.all_gather(self_query.astype(low_type), "row", axis=0, tiled=True),
        lax.all_gather(self_kv.astype(low_type), "row", axis=1, tiled=True),
        lax.all_gather(self_out.astype(low_type), "row", axis=0, tiled=True),
        lax.all_gather(cross_query.astype(low_type), "row", axis=0, tiled=True),
        lax.all_gather(cross_kv.astype(low_type), "row", axis=1, tiled=True),
        lax.all_gather(cross_out.astype(low_type), "row", axis=0, tiled=True),
        lax.all_gather(fc_in.astype(low_type), "row", axis=0, tiled=True),
        lax.all_gather(fc_out.astype(low_type), "row", axis=0, tiled=True),
    )
    q_weight, kv_weight, o_weight, cq_weight, ckv_weight, co_weight, in_weight, out_weight = (
        weight_set
    )
    grad_out = cotangent.astype(jnp.float32).reshape(-1, width)
    grad_three = normalize_back(grad_out, unit_three, inv_three, ln_gain[2])
    grad_ffn = grad_three.astype(low_type)
    grad_adapt = (4.0 * grad_three).astype(low_type)
    grad_up_w = jnp.einsum("na,nd->ad", down_act, grad_adapt, preferred_element_type=jnp.float32)
    grad_up_b = jnp.sum(grad_adapt.astype(jnp.float32), axis=0)
    grad_down = gelu_back(down_proj, project(grad_adapt, up_weight.T)).astype(low_type)
    grad_down_w = jnp.einsum("nd,na->da", hidden_low, grad_down, preferred_element_type=jnp.float32)
    grad_down_b = jnp.sum(grad_down.astype(jnp.float32), axis=0)
    grad_inner = gelu_back(up_proj, project(grad_ffn, out_weight.T)).astype(low_type)
    grad_hidden_two = (
        grad_three + project(grad_inner, in_weight.T) + project(grad_down, down_weight.T)
    )
    grad_two = normalize_back(grad_hidden_two, unit_two, inv_two, ln_gain[1])
    grad_cross_att = project(grad_two.astype(low_type), co_weight.T).astype(low_type)
    cross_grads = [
        attend_back(
            rows_of(cross_queries, row_index),
            cross_key_sets[row_index],
            cross_value_sets[row_index],
            cross_masks[row_index],
            cross_parts[row_index][1],
            rows_of(grad_cross_att, row_index),
        )
        for row_index in range(row_count)
    ]
    grad_cq = jnp.concatenate([part[0] for part in cross_grads], 0).astype(low_type)
    grad_hidden_one = grad_two + project(grad_cq, cq_weight.T) * scale
    grad_one = normalize_back(grad_hidden_one, unit_one, inv_one, ln_gain[0])
    grad_attended = project(grad_one.astype(low_type), o_weight.T).astype(low_type)
    self_grads = [
        attend_back(
            rows_of(queries, row_index),
            self_key_sets[row_index],
            self_value_sets[row_index],
            self_mask,
            self_parts[row_index][1],
            rows_of(grad_attended, row_index),
        )
        for row_index in range(row_count)
    ]
    pre_self_grad = jnp.stack(
        [
            sum((part[1][:prefix_count] for part in self_grads)),
            sum((part[2][:prefix_count] for part in self_grads)),
        ]
    )
    pre_cross_grad = jnp.stack(
        [
            sum((part[1][:prefix_count] for part in cross_grads)),
            sum((part[2][:prefix_count] for part in cross_grads)),
        ]
    )
    summed = [
        (
            lax.psum_scatter(
                self_grads[row_index][1][prefix_count:].astype(jnp.bfloat16),
                "seq",
                scatter_dimension=0,
                tiled=True,
            ).astype(jnp.float32),
            lax.psum_scatter(
                self_grads[row_index][2][prefix_count:].astype(jnp.bfloat16),
                "seq",
                scatter_dimension=0,
                tiled=True,
            ).astype(jnp.float32),
            lax.psum_scatter(
                cross_grads[row_index][1][prefix_count:].astype(jnp.bfloat16),
                "seq",
                scatter_dimension=0,
                tiled=True,
            ).astype(jnp.float32),
            lax.psum_scatter(
                cross_grads[row_index][2][prefix_count:].astype(jnp.bfloat16),
                "seq",
                scatter_dimension=0,
                tiled=True,
            ).astype(jnp.float32),
        )
        for row_index in range(row_count)
    ]
    key_grad = jnp.stack([part[0] for part in summed])
    value_grad = jnp.stack([part[1] for part in summed])
    mkey_grad = jnp.stack([part[2] for part in summed])
    mvalue_grad = jnp.stack([part[3] for part in summed])
    grad_query = jnp.concatenate([part[0] for part in self_grads], 0).astype(low_type)
    d_tokens = (
        grad_one
        + project(grad_query, q_weight.T) * scale
        + project(key_grad.astype(low_type).reshape(-1, width), kv_weight[0].T)
        + project(value_grad.astype(low_type).reshape(-1, width), kv_weight[1].T)
    )
    d_memory = project(mkey_grad.astype(low_type).reshape(-1, width), ckv_weight[0].T) + project(
        mvalue_grad.astype(low_type).reshape(-1, width), ckv_weight[1].T
    )
    totals = lax.psum(
        (pre_self_grad, pre_cross_grad, grad_down_w, grad_down_b, grad_up_w, grad_up_b),
        ("row", "seq"),
    )
    return (
        mixed,
        d_tokens.astype(low_type).reshape(row_count, tok_count, width),
        d_memory.astype(low_type).reshape(row_count, slot_count, width),
        totals[0],
        totals[1],
        totals[2],
        totals[3],
        totals[4],
        totals[5],
    )


LOW = jnp.bfloat16
F32 = jnp.float32
SCALE = 0.125
VMEM = pl.BlockSpec(memory_space=pltpu.VMEM)
SMEM = pl.BlockSpec(memory_space=pltpu.SMEM)
HBM = pl.BlockSpec(memory_space=pltpu.HBM)


def shape_of(shape, dtype=LOW):
    return jax.ShapeDtypeStruct(shape, dtype)


def nn(left, right):
    return jnp.dot(left, right, preferred_element_type=F32)


def nt(left, right):
    return lax.dot_general(left, right, (((1,), (1,)), ((), ())), preferred_element_type=F32)


def tn(left, right):
    return lax.dot_general(left, right, (((0,), (0,)), ((), ())), preferred_element_type=F32)


def cols(start, size):
    return pl.ds(pl.multiple_of(start, 128), size)


def ln(value, gain, shift):
    centre = value - jnp.mean(value, axis=-1, keepdims=True)
    inv = lax.rsqrt(jnp.mean(centre * centre, axis=-1, keepdims=True) + EPSILON)
    unit = centre * inv
    return unit * gain + shift, unit, inv


def ln_back(grad, unit, inv, gain):
    scaled = grad * gain
    return inv * (
        scaled
        - jnp.mean(scaled, axis=-1, keepdims=True)
        - unit * jnp.mean(scaled * unit, axis=-1, keepdims=True)
    )


def gelu_both(value):
    cdf = 0.5 * (1.0 + lax.erf(value * 0.7071067811865476))
    return value * cdf, cdf + value * (jnp.exp(-0.5 * value * value) * 0.3989422804014327)


def stacked(block):
    first = lax.broadcasted_iota(jnp.int32, block.shape, 1) < 64
    zero = jnp.zeros_like(block)
    return jnp.concatenate([jnp.where(first, block, zero), jnp.where(first, zero, block)], 0)


def unstacked(both, n):
    return jnp.concatenate([both[:64, :n], both[64:, n:]], 0).T


def pre_mask(shape, count):
    return lax.broadcasted_iota(jnp.int32, shape, 0) < count


def soft_pair(qs, k_pre, k_blocks, v_pre, vt_blocks, biases, count):
    s_pre = nt(k_pre, qs)
    s_pre = jnp.where(pre_mask(s_pre.shape, count), s_pre, MASKED)
    s_blocks = [nt(k, qs) + b for k, b in zip(k_blocks, biases)]
    top = jnp.max(s_pre, axis=0, keepdims=True)
    for s in s_blocks:
        top = jnp.maximum(top, jnp.max(s, axis=0, keepdims=True))
    e_pre = jnp.exp(s_pre - top)
    total = jnp.sum(e_pre, axis=0, keepdims=True)
    out = tn(v_pre, e_pre.astype(LOW))
    for s, vt in zip(s_blocks, vt_blocks):
        e = jnp.exp(s - top)
        total += jnp.sum(e, axis=0, keepdims=True)
        out += nn(vt, e.astype(LOW))
    return out * (1.0 / total), top + jnp.log(total)


def soft_pair_back(qs, dos, lse, k_pre, v_pre, ks, vs, kts, biases, count):
    s_pre = nt(k_pre, qs)
    p_pre = jnp.where(pre_mask(s_pre.shape, count), jnp.exp(s_pre - lse), 0.0)
    d_pre = nt(v_pre, dos)
    delta = jnp.sum(p_pre * d_pre, axis=0, keepdims=True)
    ps, ds = [], []
    for k, v, b in zip(ks, vs, biases):
        p = jnp.exp(nt(k, qs) + b - lse)
        d = nt(v, dos)
        delta += jnp.sum(p * d, axis=0, keepdims=True)
        ps.append(p)
        ds.append(d)
    g_pre = (p_pre * (d_pre - delta)).astype(LOW)
    dq = tn(k_pre, g_pre)
    dk, dv = [nn(g_pre, qs)], [nn(p_pre.astype(LOW), dos)]
    for p, d, kt in zip(ps, ds, kts):
        g = (p * (d - delta)).astype(LOW)
        dq += nn(kt, g)
        dk.append(nn(g, qs))
        dv.append(nn(p.astype(LOW), dos))
    return dq, dk, dv


COSTS = {
    "pack_heads": 1.5,
    "pack": 5.0,
    "self_fwd": 5.0,
    "mem_fwd": 2.3,
    "mid_fwd": 10.0,
    "mlp": 20.0,
    "cross_bwd": 11.0,
    "query_bwd": 3.0,
    "self_bwd": 6.5,
    "mem_back": 2.5,
    "totals": 3.0,
}
LIMITS = {
    "pack_heads": 60,
    "inbound": 20,
    "tokens": 4,
    "pack": 60,
    "self_fwd": 14,
    "self_bwd": 18,
    "mem_fwd": 14,
    "mem_back": 14,
    "mid_fwd": 24,
    "mlp": 48,
    "cross_bwd": 26,
    "query_bwd": 12,
    "halve": 6,
    "join": 8,
    "totals": 20,
    "mix": 4,
}


def call(kernel, name, ins, outs, scratch=()):
    flops = int(COSTS.get(name, 0.8) * 0.6e9)
    return pl.pallas_call(
        kernel,
        cost_estimate=pl.CostEstimate(flops=flops, bytes_accessed=1000, transcendentals=0),
        in_specs=ins,
        out_specs=[o[0] for o in outs],
        out_shape=[o[1] for o in outs],
        scratch_shapes=list(scratch),
        compiler_params=pltpu.CompilerParams(vmem_limit_bytes=LIMITS[name] * 2**20),
        name=name,
    )


def out(shape, dtype=LOW, space=VMEM):
    return space, jax.ShapeDtypeStruct(shape, dtype)


def inbound_kernel(ids, tokens, memory, first, second, sems):
    copies = []
    for n, dst in enumerate((first, second)):
        row = ids[12] if n == 0 else 1 - ids[12]
        for m, (src, start, size) in enumerate(((tokens, 0, 64), (memory, 64, 128))):
            copies.append(pltpu.make_async_copy(src.at[row], dst.at[pl.ds(start, size)], sems.at[n, m]))
    for copy in copies:
        copy.start()
    for copy in copies:
        copy.wait()


def inbound(ids, tokens, memory):
    return call(
        inbound_kernel,
        "inbound",
        [SMEM, HBM, HBM],
        [out((192, 1024)), out((192, 1024))],
        [pltpu.SemaphoreType.DMA((2, 2))],
    )(ids, tokens, memory)


def tokens_kernel(first, second, dst, sems):
    copies = [
        pltpu.make_async_copy(src.at[pl.ds(0, 64)], dst.at[pl.ds(64 * n, 64)], sems.at[n])
        for n, src in enumerate((first, second))
    ]
    for copy in copies:
        copy.start()
    for copy in copies:
        copy.wait()


def pack_first_kernel(ids, query, kv, ckv, dst, wide, sems):
    copies = [pltpu.make_async_copy(ckv.at[n], wide.at[pl.ds(256 * n, 256)], sems.at[n]) for n in range(2)]
    for n in range(2):
        group = cols(ids[13 + 2 * n] * 256, 256)
        for j, src in enumerate((query, kv.at[0])):
            copies.append(
                pltpu.make_async_copy(
                    src.at[:, group],
                    wide.at[pl.ds(512, 256), pl.ds(512 * n + 256 * j, 256)],
                    sems.at[2 + 4 * n + j],
                )
            )
        for j in range(2):
            copies.append(
                pltpu.make_async_copy(
                    kv.at[1, pl.ds(128 * j, 128), group],
                    wide.at[pl.ds(768, 128), pl.ds(512 * j + 256 * n, 256)],
                    sems.at[4 + 4 * n + j],
                )
            )
    for copy in copies:
        copy.start()
    for copy in copies:
        copy.wait()
    dst[...] = wide[...].astype(LOW)


def pack_first(ids, query, kv, ckv):
    return call(
        pack_first_kernel,
        "pack_heads",
        [SMEM, HBM, HBM, HBM],
        [out((896, 1024))],
        [pltpu.VMEM((896, 1024), F32), pltpu.SemaphoreType.DMA((10,))],
    )(ids, query, kv, ckv)[0]


def head_weights(parts):
    for n, part in enumerate(parts):
        g = n % 2
        yield (
            part[512:768, 512 * g : 512 * g + 256],
            part[512:768, 512 * g + 256 : 512 * g + 512],
            part[768:, 256 * g : 256 * g + 256],
            part[768:, 512 + 256 * g : 768 + 256 * g],
        )


def pack_kernel(sources, n_args, ids, *refs):
    args, refs = refs[:n_args], refs[n_args:]
    outs, (wide, narrow, in_sem, own_sem, part_sem) = refs[:-5], refs[-5:]
    count = len(sources)

    def fetch(m):
        arg, lead, row, col, kept_in = sources[m][:5]
        src = args[arg] if lead is None else args[arg].at[lead]
        start, size = row, 256
        if kept_in is None:
            start, size = pl.multiple_of(row + ids[sources[m][-1]] * 128, 128), 128
        return pltpu.make_async_copy(
            src.at[pl.ds(start, size), pl.ds(col, 1024)], wide.at[m, pl.ds(0, size)], in_sem.at[m]
        )

    def store(m):
        kept_in, kept_at, number, index, bit = sources[m][4:]
        kept = narrow.at[m]
        half = kept
        if kept_in is None:
            half = kept.at[pl.ds(0, 128)]
        elif bit is not None:
            half = kept.at[pl.ds(pl.multiple_of(ids[bit] * 128, 128), 128)]
        part = pltpu.make_async_copy(half, outs[number].at[index], part_sem.at[m])
        if kept_in is None:
            return (part,)
        return pltpu.make_async_copy(kept, outs[kept_in].at[kept_at], own_sem.at[m]), part

    for m in range(count):
        fetch(m).start()
    for m in range(count):
        fetch(m).wait()
        narrow[m] = wide[m].astype(LOW)
        for copy in store(m):
            copy.start()
    for m in range(count):
        for copy in store(m):
            copy.wait()


def pack(ids, sources, shapes, *args):
    return call(
        functools.partial(pack_kernel, sources, len(args)),
        "pack",
        [SMEM] + [HBM] * len(args),
        [out(shape, LOW, HBM) for shape in shapes],
        [
            pltpu.VMEM((len(sources), 256, 1024), F32),
            pltpu.VMEM((len(sources), 256, 1024), LOW),
            pltpu.SemaphoreType.DMA((len(sources),)),
            pltpu.SemaphoreType.DMA((len(sources),)),
            pltpu.SemaphoreType.DMA((len(sources),)),
        ],
    )(ids, *args)


PLACES = {
    "own": (lambda ids: ids[4], 256),
    "core": (lambda ids: ids[5], 256),
    "near": (lambda ids: ids[6], 128),
    "other": (lambda ids: ids[7], 128),
    "core_near": (lambda ids: ids[8], 128),
    "core_other": (lambda ids: ids[9], 128),
    "near_y": (lambda ids: ids[21], 128),
    "other_y": (lambda ids: ids[22], 128),
    "core_near_y": (lambda ids: ids[23], 128),
    "core_other_y": (lambda ids: ids[24], 128),
    "far": (lambda ids: 2 * ids[2], 256),
    "core_far": (lambda ids: 2 * ids[3], 256),
}
DIRECT = ("own", "core", "far", "core_far")
SHARED = ("own", "core", "near", "other", "core_near", "core_other")


def shared(index, first):
    return [(n, index + first if n < 2 else index, place) for n, place in enumerate(SHARED)]


def direct(index):
    return [(n, index, place) for n, place in enumerate(DIRECT)]


def place_of(ids, place):
    first, size = PLACES[place]
    return cols(first(ids) * 128, size)


def mm(x_ref, refs, matrix, ids):
    acc = None
    for n, index, place in matrix:
        term = nn(x_ref[:, place_of(ids, place)], refs[n][index])
        acc = term if acc is None else acc + term
    return acc


def mm_back(value, refs, matrix, ids, out_ref):
    for n, index, place in matrix:
        out_ref[:, place_of(ids, place)] = nt(value, refs[n][index])


class Fetch:
    def __init__(self, sources, targets, sems, matrices, first=0):
        self.copies, number = [], 0
        for matrix in matrices:
            mine = []
            for n, index, _ in matrix:
                to = index - first if n < 2 else index
                mine.append(pltpu.make_async_copy(sources[n].at[index], targets[n].at[to], sems.at[number]))
                number += 1
            self.copies.append(mine)

    def start(self, m):
        for copy in self.copies[m]:
            copy.start()

    def wait(self, m):
        for copy in self.copies[m]:
            copy.wait()


def fill_prefix(pre, wide, narrow, count, where=None):
    wide[...] = jnp.zeros_like(wide)
    wide[:, :count, :] = pre[...] if where is None else pre[:, :, where]
    narrow[...] = wide[...].astype(LOW)


def fill_places(order, ids, kpos, qpos):
    c, y, odd = ids[10], ids[11], ids[12]
    lane = lax.broadcasted_iota(jnp.int32, (1, 512), 1)
    column = jnp.zeros((1, 512), jnp.int32)
    for n in range(16):
        core = c if n < 8 else 1 - c
        line = y if n % 8 < 4 else 1 - y
        turned = odd if n % 4 < 2 else 1 - odd
        bucket = 2 * (2 * (2 * core + turned) + line) + n % 2
        first = order[bucket] * 32
        kpos[n * 32 : (n + 1) * 32, :] = lax.broadcasted_iota(jnp.int32, (32, 1), 0) + first
        column = jnp.where(lane // 32 == n, first + lane % 32, column)
    qpos[...] = column


def self_bias(kpos, qpos, t):
    seen = kpos[...] <= qpos[:, t * 128 : (t + 1) * 128]
    bias = jnp.where(seen, 0.0, MASKED)
    return jnp.concatenate([bias, bias], 1)


def self_fwd_kernel(
    count, ids, order, t0, t1, t2, t3, w0, w1, w2, w3, pre, q_ref, k_ref, v_ref,
    o0, o1, o2, o3, lse_ref, vt, kpos, qpos, wide, pre_l
):
    fill_places(order, ids, kpos, qpos)
    fill_prefix(pre, wide, pre_l, count, cols(ids[13] * 256, 256))
    for t, tok in enumerate((t0, t1, t2, t3)):
        rows = slice(t * 128, (t + 1) * 128)
        acc = [0.0, 0.0, 0.0]
        for n, (wq, wk, wv, wv2) in enumerate(head_weights((w0, w1, w2, w3))):
            some = tok[:, cols(ids[n] * 256, 256)]
            acc[0] += nn(some, wq)
            acc[1] += nn(some, wk)
            acc[2] += nn(some[:, :128], wv) + nn(some[:, 128:], wv2)
        q_ref[rows, :] = (acc[0] * SCALE).astype(LOW)
        k_ref[rows, :] = acc[1].astype(LOW)
        v_ref[rows, :] = acc[2].astype(LOW)
    vt[...] = v_ref[...].T
    for t in (3, 1, 2, 0):
        bias = self_bias(kpos, qpos, t)
        for p in range(2):
            lanes = slice(p * 128, (p + 1) * 128)
            qs = stacked(q_ref[t * 128 : (t + 1) * 128, lanes])
            got, lse = soft_pair(
                qs, pre_l[0, :, lanes], [k_ref[:, lanes]], pre_l[1, :, lanes], [vt[lanes, :]], [bias], count
            )
            (o0, o1, o2, o3)[t][:, lanes] = unstacked(got, 128).astype(LOW)
            lse_ref[p, t] = lse


def self_fwd(ids, order, toks, ws, pre, count):
    return call(
        functools.partial(self_fwd_kernel, count),
        "self_fwd",
        [SMEM, SMEM] + [VMEM] * 9,
        [
            out((512, 256)),
            out((512, 256)),
            out((512, 256)),
            out((128, 256)),
            out((128, 256)),
            out((128, 256)),
            out((128, 256)),
            out((2, 4, 1, 256), F32),
        ],
        [
            pltpu.VMEM((256, 512), LOW),
            pltpu.VMEM((512, 1), jnp.int32),
            pltpu.VMEM((1, 512), jnp.int32),
            pltpu.VMEM((2, 32, 256), F32),
            pltpu.VMEM((2, 32, 256), LOW),
        ],
    )(ids, order, *toks, *ws, pre)


def self_bwd_kernel(
    count, ids, order, q, k, v, d0, d1, d2, d3, g0, lse_ref, w0, w1, w2, w3, pre,
    near_ref, far_ref, sums_ref, kt, dq, dk, dv, gpre_ref, kpos, qpos, wide, pre_l
):
    fill_places(order, ids, kpos, qpos)
    fill_prefix(pre, wide, pre_l, count, cols(ids[13] * 256, 256))
    kt[...] = k[...].T
    grads = (d0, d1, d2, d3)
    for t in range(4):
        bias = self_bias(kpos, qpos, t)
        for p in range(2):
            lanes = slice(p * 128, (p + 1) * 128)
            qs = stacked(q[t * 128 : (t + 1) * 128, lanes])
            dos = stacked(grads[t][:128, lanes])
            g, gk, gv = soft_pair_back(
                qs,
                dos,
                lse_ref[p, t],
                pre_l[0, :, lanes],
                pre_l[1, :, lanes],
                [k[:, lanes]],
                [v[:, lanes]],
                [kt[lanes, :]],
                [bias],
                count,
            )
            dq[t * 128 : (t + 1) * 128, lanes] = unstacked(g, 128).astype(LOW)
            if t == 0:
                gpre_ref[:32, lanes] = gk[0]
                gpre_ref[32:, lanes] = gv[0]
                dk[:, lanes] = gk[1]
                dv[:, lanes] = gv[1]
            else:
                gpre_ref[:32, lanes] += gk[0]
                gpre_ref[32:, lanes] += gv[0]
                dk[:, lanes] += gk[1]
                dv[:, lanes] += gv[1]
    cross = g0[...] + d1[128:].astype(F32) + d2[128:].astype(F32) + d3[128:].astype(F32)
    for n, rows in enumerate((gpre_ref[:32], gpre_ref[32:], cross[:32], cross[32:])):
        sums_ref[:, 256 * n : 256 * (n + 1)] = rows.astype(LOW)
    dkl, dvl = dk[...].astype(LOW), dv[...].astype(LOW)
    for n, (wq, wk, wv, wv2) in enumerate(head_weights((w0, w1, w2, w3))):
        part = jnp.concatenate([nt(dvl, wv), nt(dvl, wv2)], 1)
        part = (part + nt(dq[...], wq) * SCALE + nt(dkl, wk)).astype(LOW)
        near_ref[:, cols(ids[n] * 256, 256)] = part[:256]
        far_ref[:, cols(ids[n] * 256, 256)] = part[256:]


def self_bwd(ids, order, q, k, v, grads, g0, lse, ws, pre, count):
    return call(
        functools.partial(self_bwd_kernel, count),
        "self_bwd",
        [SMEM, SMEM] + [VMEM] * 14,
        [out((256, 1024)), out((256, 1024)), out((32, 1024))],
        [
            pltpu.VMEM((256, 512), LOW),
            pltpu.VMEM((512, 256), LOW),
            pltpu.VMEM((512, 256), F32),
            pltpu.VMEM((512, 256), F32),
            pltpu.VMEM((64, 256), F32),
            pltpu.VMEM((512, 1), jnp.int32),
            pltpu.VMEM((1, 512), jnp.int32),
            pltpu.VMEM((2, 32, 256), F32),
            pltpu.VMEM((2, 32, 256), LOW),
        ],
    )(ids, order, q, k, v, *grads, g0, lse, *ws, pre)


def memory_fetch(parts, bufs, sems):
    copies = [
        [
            pltpu.make_async_copy(p.at[pl.ds(256 * j, 256)], b.at[j], sems.at[4 * j + n])
            for n, (p, b) in enumerate(zip(parts, bufs))
        ]
        for j in range(2)
    ]
    for copy in copies[0] + copies[1]:
        copy.start()
    return copies


def mem_kernel(ids, m0, m1, *refs):
    parts, res, bufs, sems = refs[:4], refs[4], refs[5:9], refs[9]
    copies = memory_fetch(parts, bufs, sems)
    for j in range(2):
        for copy in copies[j]:
            copy.wait()
        for n, mem in enumerate((m0.at[pl.ds(64, 128)], m1.at[pl.ds(64, 128)])):
            res[j, n * 128 : (n + 1) * 128, :] = mm(mem, bufs, direct(j), ids).astype(LOW)


def mem_fwd(ids, m0, m1, parts):
    return call(
        mem_kernel,
        "mem_fwd",
        [SMEM] + [VMEM] * 2 + [HBM] * 4,
        [out((2, 256, 1024))],
        [pltpu.VMEM((2, 256, 1024), LOW) for p in parts] + [pltpu.SemaphoreType.DMA((8,))],
    )(ids, m0, m1, *parts)[0]


def mem_back_kernel(ids, near, far_c, far_k, far_v, *refs):
    parts, (r0, r1), bufs, (wide, sems) = refs[:4], refs[4:6], refs[6:10], refs[10:]
    copies = memory_fetch(parts, bufs, sems)
    total = [
        (near[j].astype(F32) + far_c[j].astype(F32) + far_y[...].astype(F32)).astype(LOW)
        for j, far_y in enumerate((far_k, far_v))
    ]
    for copy in copies[0] + copies[1]:
        copy.wait()
    for n, place in enumerate(DIRECT):
        wide[:, place_of(ids, place)] = nt(total[0], bufs[n][0]) + nt(total[1], bufs[n][1])
    r0[...] = wide[:128].astype(LOW)
    r1[...] = wide[128:].astype(LOW)


def mem_back(ids, near, far_c, far_k, far_v, parts):
    return call(
        mem_back_kernel,
        "mem_back",
        [SMEM] + [VMEM] * 4 + [HBM] * 4,
        [out((128, 1024)), out((128, 1024))],
        [pltpu.VMEM((2, 256, 1024), LOW) for p in parts]
        + [pltpu.VMEM((256, 1024), F32), pltpu.SemaphoreType.DMA((8,))],
    )(ids, near, far_c, far_k, far_v, *parts)


def fill_bias(bias, ids, live):
    c, y, odd = ids[10], ids[11], ids[12]
    for n in range(8):
        core = c if n < 4 else 1 - c
        line = y if n % 4 < 2 else 1 - y
        turned = odd if n % 2 == 0 else 1 - odd
        first = (2 * (2 * core + turned) + line) * 128
        slot = lax.broadcasted_iota(jnp.int32, (128, 256), 0) + first
        bias[n * 128 : (n + 1) * 128, :] = jnp.where(slot < live[0, 0], 0.0, MASKED)


def mid_fwd_kernel(count, ids, live, o0, o1, o2, o3, tok, gain, shift, pre, *refs):
    kvs, parts, refs = refs[:4], refs[4:10], refs[10:]
    cq_ref, lse_ref, unit1, inv1, h2_ref, unit2, inv2, h2l = refs[:8]
    kv, bufs, (bias, flat, wide, pre_l, sems, kv_sems) = refs[8:12], refs[12:18], refs[18:]
    fetch = Fetch(parts, bufs, sems, [shared(j, 0) for j in range(3)])
    loads = [
        pltpu.make_async_copy(kvs[n].at[j], kv[n].at[j], kv_sems.at[n, j]) for j in range(2) for n in range(4)
    ]
    fetch.start(0)
    fetch.start(1)
    for copy in loads:
        copy.start()
    fetch.start(2)
    for n, o in enumerate((o0, o1, o2, o3)):
        flat[:, cols(ids[13 + n] * 256, 256)] = o[...]
    fill_bias(bias, ids, live)
    fill_prefix(pre, wide, pre_l, count)
    fetch.wait(0)
    h1, unit, inv = ln(
        tok[...].astype(F32) + mm(flat, bufs, shared(0, 0), ids), gain[0:1], shift[0:1]
    )
    unit1[...] = unit
    inv1[...] = inv
    flat[...] = h1.astype(LOW)
    fetch.wait(1)
    cq_ref[...] = (mm(flat, bufs, shared(1, 0), ids) * SCALE).astype(LOW)
    for copy in loads:
        copy.wait()
    for p in range(8):
        lanes = slice(p * 128, (p + 1) * 128)
        got, lse = soft_pair(
            stacked(cq_ref[:, lanes]),
            pre_l[0, :, lanes],
            [kv[n][0, :, lanes] for n in range(4)],
            pre_l[1, :, lanes],
            [kv[n][1, :, lanes].T for n in range(4)],
            [bias[n * 256 : (n + 1) * 256] for n in range(4)],
            count,
        )
        flat[:, lanes] = unstacked(got, 128).astype(LOW)
        lse_ref[p] = lse
    fetch.wait(2)
    h2, unit, inv = ln(h1 + mm(flat, bufs, shared(2, 0), ids), gain[1:2], shift[1:2])
    h2_ref[...] = h2
    unit2[...] = unit
    inv2[...] = inv
    h2l[...] = h2.astype(LOW)


def mid_fwd(ids, live, os, tok, gain, shift, pre, kvs, parts, count):
    wide, thin = out((128, 1024), F32), out((128, 1), F32)
    return call(
        functools.partial(mid_fwd_kernel, count),
        "mid_fwd",
        [SMEM, SMEM] + [VMEM] * 8 + [HBM] * 10,
        [out((128, 1024)), out((8, 1, 256), F32), wide, thin, wide, wide, thin, out((128, 1024))],
        [pltpu.VMEM((2, 256, 1024), LOW)] * 4
        + [pltpu.VMEM((3, *p.shape[1:]), LOW) for p in parts]
        + [
            pltpu.VMEM((1024, 256), F32),
            pltpu.VMEM((128, 1024), LOW),
            pltpu.VMEM((2, 32, 1024), F32),
            pltpu.VMEM((2, 32, 1024), LOW),
            pltpu.SemaphoreType.DMA((18,)),
            pltpu.SemaphoreType.DMA((4, 2)),
        ],
    )(ids, live, *os, tok, gain, shift, pre, *kvs, *parts)


def mlp_kernel(matrices, ids, h2, h2l, unit2, inv2, c0, c1, gain, shift, down_b, up_b, down_any, up_any, *refs):
    count = 1 + max(n for matrix in matrices for n, _, _ in matrix)
    parts, refs = refs[:count], refs[count:]
    m0, m1, dr2, keep, give, gaub, gadb = refs[:7]
    bufs, (down, up, act, slope, acc, sems, ad_sems) = refs[7 : 7 + count], refs[7 + count :]
    fetch = Fetch(parts, bufs, sems, matrices)
    ad = [
        pltpu.make_async_copy(down_any, down, ad_sems.at[0]),
        pltpu.make_async_copy(up_any, up, ad_sems.at[1]),
    ]
    for s in range(4):
        fetch.start(s)
    for copy in ad:
        copy.start()
    for s in range(4, 8):
        fetch.start(s)
    for s in range(4):
        fetch.wait(s)
        value, gradient = gelu_both(mm(h2l, bufs, matrices[s], ids))
        lanes = slice(s * 1024, (s + 1) * 1024)
        act[:, lanes] = value.astype(LOW)
        slope[:, lanes] = gradient
    for copy in ad:
        copy.wait()
    down_w, up_w = down[...].astype(LOW), up[...].astype(LOW)
    a, a_slope = gelu_both(nn(h2l[...], down_w) + down_b[...])
    a = a.astype(LOW)
    total = h2[...] + 4.0 * (nn(a, up_w) + up_b[...])

    def rows(s, place):
        first, size = PLACES[place]
        first = first(ids)
        return cols((first // 2) * 1024 + s * 256 + (first % 2) * 128, size)

    for s in range(4):
        fetch.wait(4 + s)
        for n, index, place in matrices[4 + s]:
            total += nn(act[:, rows(s, place)], bufs[n][index])
    res, unit3, inv3 = ln(total, gain[2:3], shift[2:3])
    m0[...] = res[:64].astype(LOW)
    m1[...] = res[64:].astype(LOW)
    cot = jnp.concatenate([c0[...], c1[...]], 0).astype(F32)
    dr3 = ln_back(cot, unit3, inv3, gain[2:3])
    dffn = dr3.astype(LOW)
    dad = (4.0 * dr3).astype(LOW)
    gau = tn(a, dad)
    gaub[...] = jnp.sum(dad.astype(F32), axis=0, keepdims=True)
    ddn = (a_slope * nt(dad, up_w)).astype(LOW)
    gadb[:, :512] = jnp.sum(ddn.astype(F32), axis=0, keepdims=True)
    gadb[:, 512:] = jnp.zeros((1, 512), F32)
    gadt = tn(ddn, h2l[...])
    first_core = ids[10] == 0
    keep[...] = jnp.where(first_core, gau, gadt)
    give[...] = jnp.where(first_core, gadt, gau).astype(LOW)
    for s in range(4):
        for n, index, place in matrices[4 + s]:
            where = rows(s, place)
            act[:, where] = (slope[:, where] * nt(dffn, bufs[n][index])).astype(LOW)
    acc[...] = dr3 + nt(ddn, down_w)
    for s in range(4):
        for n, index, place in matrices[s]:
            acc[:, place_of(ids, place)] += nt(act[:, s * 1024 : (s + 1) * 1024], bufs[n][index])
    dr2[...] = ln_back(acc[...], unit2[...], inv2[...], gain[1:2])


def mlp(ids, h2, h2l, unit2, inv2, cots, gain, shift, down_b, up_b, down, up, parts, matrices):
    return call(
        functools.partial(mlp_kernel, matrices),
        "mlp",
        [SMEM] + [VMEM] * 10 + [HBM] * (2 + len(parts)),
        [
            out((64, 1024)),
            out((64, 1024)),
            out((128, 1024), F32),
            out((512, 1024), F32),
            out((512, 1024)),
            out((1, 1024), F32),
            out((1, 1024), F32),
        ],
        [pltpu.VMEM((8, *p.shape[1:]) if n < 2 else p.shape, LOW) for n, p in enumerate(parts)]
        + [
            pltpu.VMEM((1024, 512), F32),
            pltpu.VMEM((512, 1024), F32),
            pltpu.VMEM((128, 4096), LOW),
            pltpu.VMEM((128, 4096), F32),
            pltpu.VMEM((128, 1024), F32),
            pltpu.SemaphoreType.DMA((sum(len(m) for m in matrices),)),
            pltpu.SemaphoreType.DMA((2,)),
        ],
    )(ids, h2, h2l, unit2, inv2, *cots, gain, shift, down_b, up_b, down, up, *parts)


def cross_bwd_kernel(count, ids, live, dr2, cq, lse, gaub, gadb, pre, *refs):
    kvs, parts, refs = refs[:4], refs[4:10], refs[10:]
    grads, (dcq, *sums) = refs[:4], refs[4:9]
    kv, bufs, (bias, flat, wide, wide_pre, pre_l, gpre, sems, kv_sems) = refs[9:13], refs[13:19], refs[19:]
    copies = [
        pltpu.make_async_copy(parts[n].at[2], bufs[n], sems.at[n]) for n in range(6)
    ]
    loads = [
        pltpu.make_async_copy(kvs[n].at[j], kv[n].at[j], kv_sems.at[n, j]) for j in range(2) for n in range(4)
    ]
    for copy in copies + loads:
        copy.start()
    fill_bias(bias, ids, live)
    fill_prefix(pre, wide_pre, pre_l, count)
    for copy in copies:
        copy.wait()
    value = dr2[...].astype(LOW)
    for n, place in enumerate(SHARED):
        wide[:, place_of(ids, place)] = nt(value, bufs[n][...])
    flat[...] = wide[...].astype(LOW)
    for copy in loads:
        copy.wait()
    for p in range(8):
        lanes = slice(p * 128, (p + 1) * 128)
        g, gk, gv = soft_pair_back(
            stacked(cq[:, lanes]),
            stacked(flat[:, lanes]),
            lse[p],
            pre_l[0, :, lanes],
            pre_l[1, :, lanes],
            [kv[n][0, :, lanes] for n in range(4)],
            [kv[n][1, :, lanes] for n in range(4)],
            [kv[n][0, :, lanes].T for n in range(4)],
            [bias[n * 256 : (n + 1) * 256] for n in range(4)],
            count,
        )
        for j, got in enumerate((gk, gv)):
            gpre[j, :, lanes] = got[0]
            for n in range(4):
                grads[n][j, :, lanes] = got[1 + n].astype(LOW)
        dcq[:, lanes] = unstacked(g, 128).astype(LOW)
    gpre[0, count : count + 1, :] = gaub[...]
    gpre[1, count : count + 1, :] = gadb[...]
    for j in range(2):
        rows = slice(32 * j, 32 * (j + 1))
        for n, dst in enumerate(sums):
            dst[rows, :] = gpre[j, :, cols(ids[13 + n] * 256, 256)].astype(dst.dtype)


def cross_bwd(ids, live, dr2, cq, lse, gaub, gadb, pre, kvs, parts, count):
    grad = out((2, 256, 1024))
    return call(
        functools.partial(cross_bwd_kernel, count),
        "cross_bwd",
        [SMEM, SMEM] + [VMEM] * 6 + [HBM] * 10,
        [grad, grad, grad, grad, out((128, 1024)), out((64, 256), F32)] + [out((64, 256))] * 3,
        [pltpu.VMEM((2, 256, 1024), LOW)] * 4
        + [pltpu.VMEM(p.shape[1:], LOW) for p in parts]
        + [
            pltpu.VMEM((1024, 256), F32),
            pltpu.VMEM((128, 1024), LOW),
            pltpu.VMEM((128, 1024), F32),
            pltpu.VMEM((2, 32, 1024), F32),
            pltpu.VMEM((2, 32, 1024), LOW),
            pltpu.VMEM((2, 32, 1024), F32),
            pltpu.SemaphoreType.DMA((6,)),
            pltpu.SemaphoreType.DMA((4, 2)),
        ],
    )(ids, live, dr2, cq, lse, gaub, gadb, pre, *kvs, *parts)


def query_bwd_kernel(ids, dr2, dcq, unit1, inv1, gain, g1, g2, g3, *refs):
    parts, (dr1, *grads), rest = refs[:6], refs[6:11], refs[11:]
    bufs, (wide, sems) = rest[:6], rest[6:]
    fetch = Fetch(parts, bufs, sems, [shared(1, 0), shared(0, 0)])
    fetch.start(0)
    fetch.start(1)
    fetch.wait(0)
    mm_back(dcq[...], bufs, shared(1, 0), ids, wide)
    grad = ln_back(dr2[...] + SCALE * wide[...], unit1[...], inv1[...], gain[0:1])
    dr1[...] = grad
    fetch.wait(1)
    mm_back(grad.astype(LOW), bufs, shared(0, 0), ids, wide)
    for dst, g in zip(grads[1:], (g1, g2, g3)):
        dst[128:, :] = g[...]
    for n, dst in enumerate(grads):
        dst[:128, :] = wide[:, cols(ids[13 + n] * 256, 256)].astype(LOW)


def query_bwd(ids, dr2, dcq, unit1, inv1, gain, sums, parts):
    return call(
        query_bwd_kernel,
        "query_bwd",
        [SMEM] + [VMEM] * 8 + [HBM] * 6,
        [out((128, 1024), F32), out((128, 256))] + [out((192, 256))] * 3,
        [pltpu.VMEM((2, *p.shape[1:]), LOW) for p in parts]
        + [pltpu.VMEM((128, 1024), F32), pltpu.SemaphoreType.DMA((12,))],
    )(ids, dr2, dcq, unit1, inv1, gain, *sums, *parts)


def quarters(ids, bits, size, start=0):
    first, second = ids[bits[0]], ids[bits[1]]
    pairs = ((first, second), (1 - first, second), (first, 1 - second), (1 - first, 1 - second))
    return [pl.ds(pl.multiple_of(start + (2 * a + b) * size, size), size) for a, b in pairs]


def halve_kernel(bits, count, ids, keep, *refs):
    gots, outs = refs[:count], refs[count:]
    for dst, rows in zip(outs, quarters(ids, bits, outs[0].shape[0])):
        total = keep[rows, :]
        for got in gots:
            total += got[rows, :].astype(F32)
        dst[...] = total.astype(dst.dtype)


def halve(ids, bits, keep, gots):
    size = keep.shape[0] // 4
    return call(
        functools.partial(halve_kernel, bits, len(gots)),
        "halve",
        [SMEM] + [VMEM] * (1 + len(gots)),
        [out((size, 1024), F32)] + [out((size, 1024))] * 3,
    )(ids, keep, *gots)


def mix_kernel(keep, part, g1, g2, g3, dst):
    dst[:32, :] = (
        keep[...] + g1[...].astype(F32) + g2[...].astype(F32) + g3[...].astype(F32)
    ).astype(LOW)
    dst[32:, :] = part[...]


def join_kernel(bits, ids, *refs):
    parts, dst = refs[:4], refs[4]
    for part, rows in zip(parts, quarters(ids, bits, 32)):
        dst[rows, :] = part[:32, :]
    own, other_y, other_z, both = (part[32:, :].astype(F32) for part in parts)
    dst[128:160, :] = (own + other_z).astype(LOW)
    dst[160:, :] = (other_y + both).astype(LOW)


def join_last_kernel(bits, ids, p0, p1, p2, p3, dst, wide):
    parts = (p0, p1, p2, p3)
    for part, rows in zip(parts, quarters(ids, bits, 128)):
        dst[rows, :] = part[:128, :]
    for part, rows in zip(parts, quarters(ids, bits, 64)):
        wide[rows, :] = part[128:, :].astype(F32)
    dst[512:, :] = (wide[:64] + wide[64:128] + wide[128:192] + wide[192:]).astype(LOW)


def totals_kernel(count, ids, mine, got, gau, gad, gps, gpc, gaub, gadb, wide):
    first_core = ids[10] == 0
    gau[...] = jnp.where(first_core, mine[:512], got[:512]).astype(F32)
    gad[...] = jnp.where(first_core, got[:512], mine[:512]).astype(F32).T
    for n in range(4):
        rows = (mine, got)[n // 2][512 + 32 * (n % 2) : 544 + 32 * (n % 2), :].astype(F32)
        for a in range(4):
            wide[32 * a : 32 * a + 32, cols(ids[13 + n] * 256, 256)] = rows[:, 256 * a : 256 * a + 256]
    for j in range(2):
        gps[j] = wide[32 * j : 32 * j + count, :]
        gpc[j] = wide[64 + 32 * j : 64 + 32 * j + count, :]
    gaub[...] = wide[64 + count : 65 + count, :]
    gadb[...] = wide[96 + count : 97 + count, :512]


AXES = ("x", "core", "pair", "z", "y")


def pairs_of(target):
    pairs = []
    for source in range(32):
        row, seq = divmod(source, 8)
        x, c, z, y = target(*divmod(row, 2), *divmod(seq, 2))
        pairs.append((source, (2 * x + c) * 8 + 2 * z + y))
    return pairs


SWAP_X = pairs_of(lambda x, c, z, y: (1 - x, c, z, y))
SWAP_C = pairs_of(lambda x, c, z, y: (x, 1 - c, z, y))
SWAP_Y = pairs_of(lambda x, c, z, y: (x, c, z, 1 - y))
SWAP_CY = pairs_of(lambda x, c, z, y: (x, 1 - c, z, 1 - y))
SWAP_Z = pairs_of(lambda x, c, z, y: (x, c, z ^ 1, y))
SWAP_PAIRS = pairs_of(lambda x, c, z, y: (x, c, z ^ 2, y))
SQUARE = (
    ((17, 18), (SWAP_X, SWAP_Z, pairs_of(lambda x, c, z, y: (1 - x, c, z ^ 1, y)))),
    ((20, 19), (SWAP_Y, SWAP_PAIRS, pairs_of(lambda x, c, z, y: (x, c, z ^ 2, 1 - y)))),
)
TURN = [pairs_of(lambda x, c, z, y, r=r: (x, z // 2, 2 * c + (z + r) % 2, y)) for r in range(2)]


def send(value, pairs):
    return lax.ppermute(value, AXES, pairs)


def local_pairs(
    tokens,
    memory,
    source_len,
    bucket_order,
    prefix_self,
    prefix_cross,
    self_query,
    self_kv,
    self_out,
    cross_query,
    cross_kv,
    cross_out,
    fc_in,
    fc_out,
    ln_gain,
    ln_bias,
    ad_down,
    ad_down_bias,
    ad_up,
    ad_up_bias,
    cotangent,
):
    f32 = F32
    x, c, odd, y = (lax.axis_index(name) for name in ("x", "core", "z", "y"))
    z = 2 * lax.axis_index("pair") + odd
    row = 2 * x + c
    count = prefix_self.shape[1]
    group = 2 * y + c
    far_row, both_row = 2 * (row ^ 2), 2 * (row ^ 3)
    ids = jnp.stack(
        [row, row ^ 1, row ^ 2, row ^ 3]
        + [2 * row, 2 * (row ^ 1), far_row + odd, far_row + 1 - odd, both_row + odd, both_row + 1 - odd]
        + [c, y, odd]
        + [group, group ^ 2, group ^ 1, group ^ 3]
        + [x, odd, z // 2, y]
        + [far_row + y, far_row + 1 - y, both_row + y, both_row + 1 - y]
    ).astype(jnp.int32)

    def after(value, *others):
        if isinstance(value, tuple):
            return lax.optimization_barrier((*value, *others))[: len(value)]
        return lax.optimization_barrier((value, *others))[0]

    def turn_out(first, second):
        first, second = send(first, TURN[0]), send(second, TURN[1])
        return jnp.stack([jnp.where(odd == 1, second, first), jnp.where(odd == 1, first, second)])

    blocks = inbound(ids, tokens, memory)
    first, second = (send(block, turn) for block, turn in zip(blocks, TURN))
    one = pack_first(after(ids, blocks[0]), self_query, self_kv, cross_kv)
    one_far, one_c = send(one, SWAP_X), send(one, SWAP_C)
    live = send(jnp.where(odd == 1, source_len[1], source_len[0]).reshape(1, 1), TURN[0])
    tok = call(
        tokens_kernel, "tokens", [VMEM, VMEM], [out((128, 1024))], [pltpu.SemaphoreType.DMA((2,))]
    )(after(first, one_c, live), second)[0]
    tok_y, tok_c = send(tok, SWAP_Y), send(tok, SWAP_C)
    toks = (tok, tok_y, tok_c, send(tok_y, SWAP_C))
    mid_own, ffn_own, mid_half, in_half, out_half, out_whole = pack(
        after(ids, tok),
        [(n, None, 0, 0, 0, n, 2, n, 12) for n in range(3)]
        + [(3, None, 0, 1024 * n, 1, n, 3, n, 12) for n in range(4)]
        + [(4, None, 256 * n, 0, 1, 4 + n, 4, n, 11) for n in range(2)]
        + [(4, None, 256 * n, 0, 1, 4 + n, 5, n - 2, None) for n in range(2, 4)],
        [
            (3, 256, 1024),
            (8, 256, 1024),
            (3, 128, 1024),
            (4, 128, 1024),
            (2, 128, 1024),
            (2, 256, 1024),
        ],
        self_out,
        cross_query,
        cross_out,
        fc_in,
        fc_out,
    )
    mid_near = send(mid_half, SWAP_X)
    mid_c = send(mid_own, SWAP_C)
    in_near = send(after(in_half, one_far), SWAP_X)

    one_parts = (one, one_c, one_far, send(after(one_far, toks[3], mid_half), SWAP_C))
    q, k, v, o0, o1, o2, o3, self_lse = self_fwd(
        ids, bucket_order, after(toks, mid_c), one_parts, prefix_self, count
    )
    os = (o0, send(o1, SWAP_Y), send(o2, SWAP_C), send(o3, SWAP_CY))
    mkv = mem_fwd(ids, after(first, q), second, one_parts)
    mkv_y = send(after(mkv, *os), SWAP_Y)
    mkv_c = send(mkv, SWAP_C)
    out_near = send(after(out_half, *os), SWAP_X)
    ffn_c = send(after(ffn_own, mkv), SWAP_C)
    mid_near_o = after(mid_near, *os)
    mid_other = send(mid_near_o, SWAP_Z)
    mid_parts = (mid_own, mid_c, mid_near, mid_other, send(after(mid_near, mkv_y), SWAP_C), send(mid_other, SWAP_C))
    in_other = send(after(in_near, mid_other), SWAP_Z)
    kvs = (mkv, mkv_y, mkv_c, send(mkv_y, SWAP_C))

    cq, cross_lse, unit1, inv1, h2, unit2, inv2, h2l = mid_fwd(
        ids, live, os, tok, ln_gain, ln_bias, prefix_cross, kvs, mid_parts, count
    )
    cot = [jnp.where(odd == 1, cotangent[1 - n], cotangent[n]) for n in range(2)]
    cots = [send(after(v, h2l), t) for v, t in zip(cot, TURN)]
    out_far = send(after(out_whole, kvs[3]), SWAP_X)
    in_near_l, out_near_l = after((in_near, out_near), h2l)
    out_other = send(out_near_l, SWAP_Y)
    ffn_parts = [ffn_own, ffn_c, in_near, in_other]
    ffn_parts += [send(t, SWAP_C) for t in (in_near_l, in_other)]
    ffn_parts += [out_near, out_other]
    ffn_parts += [send(t, SWAP_C) for t in (out_near_l, out_other)]
    ffn_parts += [out_far, send(out_far, SWAP_C)]
    matrices = [[(0, m, "own"), (1, m, "core")] for m in range(8)]
    for m in range(4):
        matrices[m] += [(2 + k, m, place) for k, place in enumerate(SHARED[2:])]
    for m in range(2):
        matrices[4 + m] += [(6 + k, m, place + "_y") for k, place in enumerate(SHARED[2:])]
        matrices[6 + m] += [(10, m, "far"), (11, m, "core_far")]
    m0, m1, dr2, keep, give, gaub, gadb = mlp(
        ids,
        h2,
        h2l,
        unit2,
        inv2,
        cots,
        ln_gain,
        ln_bias,
        ad_down_bias[None],
        ad_up_bias[None],
        ad_down,
        ad_up,
        ffn_parts,
        matrices,
    )
    mixed = turn_out(m0, m1)

    parts = [send(give, SWAP_C)]
    n0, n1, f0, f1, dcq, g0, *gs = cross_bwd(
        ids, live, dr2, cq, cross_lse, gaub, gadb, prefix_cross, kvs, mid_parts, count
    )
    far_c, near_c = send(f1, SWAP_C), send(f0, SWAP_C)
    bits, pairs = SQUARE[0]
    keep, *gives = halve(ids, bits, after(keep, dcq), parts)
    parts = [send(g, p) for g, p in zip(gives, pairs)]
    dr1, d0, d1, d2, d3 = query_bwd(ids, dr2, after(dcq, *gives), unit1, inv1, ln_gain, gs, mid_parts)
    grads = (d0, send(d1, SWAP_Y), send(d2, SWAP_C), send(d3, SWAP_CY))
    mem_k, mem_v = [
        (n1[n].astype(f32) + after(far_c, d0)[n].astype(f32)).astype(LOW) for n in range(2)
    ]
    far_k = send(after(mem_k, *grads), SWAP_Y)
    bits, pairs = SQUARE[1]
    keep, *gives = halve(ids, bits, keep, parts)
    parts = [send(g, p) for g, p in zip(gives, pairs)]
    near, far_part, part = self_bwd(
        ids,
        bucket_order,
        after(q, mem_k, mem_v, mixed, near_c),
        k,
        v,
        grads,
        g0,
        self_lse,
        one_parts,
        prefix_self,
        count,
    )
    got_c = send(after(far_part, far_k), SWAP_C)
    far_v = send(mem_v, SWAP_Y)
    mine = call(mix_kernel, "mix", [VMEM] * 5, [out((64, 1024))])(keep, part, *parts)[0]
    parts = [send(mine, p) for p in pairs]

    give_y = (near[128:].astype(f32) + got_c[128:].astype(f32)).astype(LOW)
    d_own = dr1 + near[:128].astype(f32) + got_c[:128].astype(f32)
    d_own = (d_own + send(give_y, SWAP_Y).astype(f32)).astype(LOW)
    d_tokens = turn_out(d_own[:64], d_own[64:])

    d_memory = turn_out(*mem_back(ids, n0, near_c, far_k, far_v, one_parts))

    whole = call(
        functools.partial(join_kernel, bits), "join", [SMEM] + [VMEM] * 4, [out((192, 1024))]
    )(ids, mine, *parts)[0]
    bits, pairs = SQUARE[0]
    parts = [send(whole, p) for p in pairs]
    whole = call(
        functools.partial(join_last_kernel, bits),
        "join",
        [SMEM] + [VMEM] * 4,
        [out((576, 1024))],
        [pltpu.VMEM((256, 1024), F32)],
    )(ids, whole, *parts)[0]
    grad_up, grad_down, grad_ps, grad_pc, grad_ub, grad_db = call(
        functools.partial(totals_kernel, count),
        "totals",
        [SMEM, VMEM, VMEM],
        [
            out((512, 1024), F32),
            out((1024, 512), F32),
            out(prefix_self.shape, F32),
            out(prefix_cross.shape, F32),
            out((1, 1024), F32),
            out((1, 512), F32),
        ],
        [pltpu.VMEM((128, 1024), F32)],
    )(ids, whole, send(whole, SWAP_C))
    return (
        mixed,
        d_tokens,
        d_memory,
        grad_ps,
        grad_pc,
        grad_down,
        grad_db[0],
        grad_up,
        grad_ub[0],
    )


def solution(mesh):
    in_specs = (
        P("row", "seq", None),
        P("row", "seq", None),
        P("row"),
        P(),
        P(),
        P(),
        P("row", None),
        P(None, "row", None),
        P("row", None),
        P("row", None),
        P(None, "row", None),
        P("row", None),
        P("row", None),
        P("row", None),
        P(),
        P(),
        P(),
        P(),
        P(),
        P(),
        P("row", "seq", None),
    )
    out_specs = (
        P("row", "seq", None),
        P("row", "seq", None),
        P("row", "seq", None),
        P(),
        P(),
        P(),
        P(),
        P(),
        P(),
    )
    if (mesh.shape["row"], mesh.shape["seq"]) != (4, 8):
        return jax.shard_map(
            local_rows, mesh=mesh, in_specs=in_specs, out_specs=out_specs, check_vma=False
        )
    fine = jax.sharding.Mesh(mesh.devices.reshape(2, 2, 2, 2, 2), AXES)
    split = {"row": ("x", "core"), "seq": ("pair", "z", "y")}

    def renamed(specs):
        return tuple(P(*(split.get(name) for name in spec)) for spec in specs)

    return jax.shard_map(
        local_pairs, mesh=fine, in_specs=renamed(in_specs), out_specs=renamed(out_specs), check_vma=False
    )
```
